128 devices in a mesh: pipe: 4 (over y_lo, core), dp: 32 (over y_hi, z, x).
Axes of the slice: x: 4, y: 4 (y_hi: 2, y_lo: 2; y = y_hi * 2 + y_lo), z: 4, core: 2. Of those that a mesh axis runs over, the one named last changes fastest.
Arguments:
- stash: bfloat16 [4, 2, 5120, 6144], P('pipe', None, 'dp'), may hold values from -6 to 6
- attn: bfloat16 [4, 2, 32, 6, 160, 160], P('pipe', None, 'dp'), may hold values from 0 to 0.03930664
- w_value: bfloat16 [4, 6144, 768], P('pipe'), may hold values from -0.078125 to 0.078125
- w_out: bfloat16 [4, 768, 6144], P('pipe'), may hold values from -0.21875 to 0.21875
- out_grad: bfloat16 [2, 5120, 6144], P(None, 'dp', 'pipe'), may hold values from -6 to 6
- order: int32 [2], replicated, may hold values from 0 to 1, each once
- check_rows: int32 [8, 6144], replicated, may hold values from -3 to 3
Outputs:
- grad_value: float32 [4, 6144, 768], P('pipe', 'dp')
- grad_out_t: float32 [4, 6144, 768], P('pipe', 'dp')
- checksums: float32 [4, 2, 8, 768], P('pipe')
- input_grad: bfloat16 [2, 5120, 6144], P(None, 'dp', 'pipe')
The draws below stay inside these ranges and needn't reach their ends.
Inputs may be any that keep to these rules, and one draw needn't show every extreme that they name: `order`: a permutation of the micro-batches.
All inputs are finite; a program needn't handle non-finite values.
Results may differ from the reference program's by a relative error of at most 0.022.
Values may be sent and summed in bfloat16 or wider, within the bound.
No kernel may reach another device: no remote copies, remote signals or barrier semaphores. Data moves between devices by JAX's collectives and lax.ppermute only.
A program may use at most 192 MiB of HBM per device.

```python
import jax
import jax.numpy as jnp
from jax import lax

D = 6144
HEADS = 6
HEAD_DIM = 128
SEQ = 160
MICRO = 2
CHECKS = 8
INNER = 768
TOK = 5120
SECTIONS = 4
N_DP = 32


def place_ends(result, stream_key, low, top_value):
    place = [jax.random.randint(jax.random.fold_in(stream_key, axis), (), 0, length) for axis, length in enumerate(result.shape)]
    longest = result.shape.index(max(result.shape))
    beside = place[:longest] + [(place[longest] + 1) % result.shape[longest]] + place[longest + 1:]
    return result.at[tuple(place)].set(low).at[tuple(beside)].set(top_value)


def block_levels(stream_key, extent, shards, low, largest):
    factor_of, own = 1.0, jax.random.fold_in(stream_key, 6)
    for position, parts in shards:
        draws = jnp.exp(jax.random.uniform(jax.random.fold_in(own, position), (parts,), jnp.float32, low / len(shards), largest / len(shards)))
        factor_of = factor_of * jnp.repeat(draws, extent[position] // parts).reshape([-1 if axis == position else 1 for axis in range(len(extent))])
    return factor_of


def gaussian(rng, dims, scale, bound, cuts=(), held_as=jnp.bfloat16):
    factor_of = block_levels(rng, dims, cuts, -0.22, 0.18) if cuts else 1.0
    array = jax.random.normal(rng, dims, jnp.float32) * scale * factor_of
    return jnp.minimum(jnp.maximum(array, -bound), bound).astype(held_as)


def setup_inputs(seed: int = 0) -> dict:
    key_list = jax.random.split(jax.random.key(seed), 8)
    return {
        "stash": gaussian(key_list[0], (SECTIONS, MICRO, TOK, D), 1.0, 6.0, ((0, 4), (2, 32))),
        "attn": jnp.clip(0.03930664 * jax.random.uniform(key_list[1], (SECTIONS, MICRO, N_DP, HEADS, SEQ, SEQ), jnp.float32) ** block_levels(key_list[1], (SECTIONS, MICRO, N_DP, HEADS, SEQ, SEQ), ((0, 4), (2, 32)), -0.2, 0.2), 0.0, 0.03930664).astype(jnp.bfloat16),
        "w_value": gaussian(key_list[2], (SECTIONS, D, INNER), D ** -0.5, 0.078125, ((0, 4),)),
        "w_out": gaussian(key_list[3], (SECTIONS, INNER, D), INNER ** -0.5, 0.21875, ((0, 4),)),
        "out_grad": gaussian(key_list[4], (MICRO, TOK, D), 1.0, 6.0, ((1, 32), (2, 4))),
        "order": jax.random.permutation(key_list[5], MICRO).astype(jnp.int32),
        "check_rows": place_ends(jax.random.randint(key_list[6], (CHECKS, D), -3, 4), jax.random.fold_in(key_list[6], 1), -3, 3).astype(jnp.int32),
    }


def section_step(xm, pm, dy, wv, wo):
    causal = (jnp.arange(SEQ)[:, None] >= jnp.arange(SEQ)[None, :]).astype(jnp.float32)
    weights = pm.astype(jnp.float32) * causal
    v = jnp.dot(xm, wv, preferred_element_type=jnp.float32).astype(jnp.bfloat16)
    vr = v.astype(jnp.float32).reshape(N_DP, SEQ, HEADS, HEAD_DIM)
    ctx = jnp.einsum("rhij,rjhd->rihd", weights, vr).reshape(TOK, INNER).astype(jnp.bfloat16)
    dctx = jnp.dot(dy, wo.T, preferred_element_type=jnp.float32).astype(jnp.bfloat16)
    dcr = dctx.astype(jnp.float32).reshape(N_DP, SEQ, HEADS, HEAD_DIM)
    dv = jnp.einsum("rhij,rihd->rjhd", weights, dcr).reshape(TOK, INNER).astype(jnp.bfloat16)
    dx = (dy.astype(jnp.float32) + jnp.dot(dv, wv.T, preferred_element_type=jnp.float32)).astype(jnp.bfloat16)
    return ctx, dv, dx


def by_replica(arr, width):
    return arr.reshape(MICRO, N_DP, SEQ, width).transpose(1, 0, 2, 3).reshape(N_DP, MICRO * SEQ, width)


def reference(stash, attn, w_value, w_out, out_grad, order, check_rows):
    grads = [out_grad[m] for m in range(MICRO)]
    ck = check_rows.astype(jnp.float32)
    grad_scale = jnp.float32((MICRO * SEQ * N_DP) ** -0.5)
    check_scale = jnp.float32(D ** -0.5)
    value_list = []
    out_list = []
    check_list = []
    for sect in reversed(range(SECTIONS)):
        ctx_b = jnp.zeros((MICRO, TOK, INNER), jnp.bfloat16)
        dv_b = jnp.zeros((MICRO, TOK, INNER), jnp.bfloat16)
        dy_b = jnp.zeros((MICRO, TOK, D), jnp.bfloat16)
        new_grads = []
        for m in range(MICRO):
            batch = order[m]
            ctx, dv, dx = section_step(stash[sect][batch], attn[sect][batch], grads[m], w_value[sect], w_out[sect])
            ctx_b = ctx_b.at[batch].set(ctx)
            dv_b = dv_b.at[batch].set(dv)
            dy_b = dy_b.at[batch].set(grads[m])
            new_grads.append(dx)
        grads = new_grads
        items = (by_replica(stash[sect], D), by_replica(dv_b, INNER), by_replica(dy_b, D), by_replica(ctx_b, INNER))

        def replica(carry, item):
            xr, dvr, dyr, cr = item
            tv = (jnp.dot(xr.T, dvr, preferred_element_type=jnp.float32) * grad_scale).astype(jnp.bfloat16)
            to = (jnp.dot(dyr.T, cr, preferred_element_type=jnp.float32) * grad_scale).astype(jnp.bfloat16)
            tv, to = lax.optimization_barrier((tv, to))
            return (carry[0] + tv.astype(jnp.float32), carry[1] + to.astype(jnp.float32)), None

        zero = jnp.zeros((D, INNER), jnp.float32)
        (gv, go), _ = lax.scan(replica, (zero, zero), items)
        value_list.insert(0, gv)
        out_list.insert(0, go)
        check_list.insert(0, check_scale * jnp.stack([jnp.dot(ck, gv, precision=lax.Precision.HIGHEST), jnp.dot(ck, go, precision=lax.Precision.HIGHEST)]))
    input_grad = jnp.stack(grads)
    return jnp.stack(value_list), jnp.stack(out_list), jnp.stack(check_list), input_grad
```

```python
import functools

import jax
import jax.numpy as jnp
from jax import lax
from jax.experimental import pallas as pl
from jax.experimental.pallas import tpu as pltpu
from jax.sharding import Mesh
from jax.sharding import PartitionSpec as P

F32 = jnp.float32
BF16 = jnp.bfloat16
NT = (((1,), (1,)), ((), ()))
TN = (((0,), (0,)), ((), ()))
REPLICAS = ("yh", "z", "x")


def shifted(array, axis, distance):
    size = lax.axis_size(axis)
    return lax.ppermute(array, axis, [(i, (i + distance) % size) for i in range(size)])


def total(*terms):
    result = terms[0].astype(F32)
    for term in terms[1:]:
        result = result + term.astype(F32)
    return result


def section_kernel(first, chunks, heads, head_dim, flags, *refs):
    if first:
        pieces, refs = refs[:chunks], refs[chunks:]
    else:
        incoming, refs = refs[0], refs[1:]
    probs, w_out, w_value = refs[:3]
    dx_out, dy_out, dv_out, dy_kept, acc, dvals = refs[-6:]
    step = pl.program_id(0)
    valid = flags[0] == 1
    seq = acc.shape[0]

    def forward(column, block):
        dy_kept[column] = block
        dy_out[0] = block
        part = lax.dot_general(block, w_out[...], NT, preferred_element_type=F32)
        if column == 0:
            acc[...] = part
        else:
            acc[...] += part

    for column in range(chunks):

        @pl.when(jnp.logical_and(valid, step == column))
        def _():
            forward(column, pieces[column][...] if first else incoming[...])

    @pl.when(jnp.logical_and(valid, step == chunks - 1))
    def _():
        dctx = acc[...].astype(BF16)
        query = lax.broadcasted_iota(jnp.int32, (seq, seq), 0)
        keys = lax.broadcasted_iota(jnp.int32, (seq, seq), 1)
        for head in range(heads):
            weights = jnp.where(query >= keys, probs[0, head].astype(F32), 0.0).astype(BF16)
            columns = slice(head * head_dim, (head + 1) * head_dim)
            part = lax.dot_general(weights, dctx[:, columns], TN, preferred_element_type=F32)
            dvals[:, columns] = part.astype(BF16)
        dv_out[0] = dvals[...]

    @pl.when(jnp.logical_and(valid, step >= chunks))
    def _():
        part = lax.dot_general(dvals[...], w_value[...], NT, preferred_element_type=F32)
        dx_out[...] = (dy_kept[step - chunks].astype(F32) + part).astype(BF16)


def section_step(flags, dy, probs, w_out, w_value, stores):
    first = isinstance(dy, tuple)
    micro, heads, seq, _ = probs.shape
    inner, width = w_out.shape
    chunks = 4
    share = width // chunks
    fixed2 = lambda j, f: (0, 0)
    ahead = lambda j, f: jnp.where(f[0] == 1, jnp.minimum(j, chunks - 1), 0)
    behind = lambda j, f: jnp.where(f[0] == 1, jnp.maximum(j - chunks, 0), 0)
    in_specs = []
    if first:
        in_specs += [pl.BlockSpec((seq, share), fixed2)] * chunks
    else:
        in_specs += [pl.BlockSpec((seq, share), lambda j, f: (0, ahead(j, f)))]
    in_specs += [
        pl.BlockSpec((1, heads, seq, seq), lambda j, f: (f[1], 0, 0, 0)),
        pl.BlockSpec((inner, share), lambda j, f: (0, ahead(j, f))),
        pl.BlockSpec((share, inner), lambda j, f: (behind(j, f), 0)),
    ]
    operands = (dy if first else (dy,)) + (probs, w_out, w_value)
    aliases = {}
    if stores is not None:
        aliases = {1 + len(operands): 1, 2 + len(operands): 2}
        in_specs += [pl.BlockSpec(memory_space=pl.ANY)] * 2
        operands += stores
    return pl.pallas_call(
        functools.partial(section_kernel, first, chunks, heads, inner // heads),
        grid_spec=pltpu.PrefetchScalarGridSpec(
            num_scalar_prefetch=1,
            grid=(2 * chunks,),
            in_specs=in_specs,
            out_specs=[
                pl.BlockSpec((seq, share), lambda j, f: (0, behind(j, f))),
                pl.BlockSpec((1, seq, share), lambda j, f: (f[2], 0, ahead(j, f))),
                pl.BlockSpec((1, seq, inner), lambda j, f: (f[2], 0, 0)),
            ],
            scratch_shapes=[
                pltpu.VMEM((chunks, seq, share), BF16),
                pltpu.VMEM((seq, inner), F32),
                pltpu.VMEM((seq, inner), BF16),
            ],
        ),
        out_shape=[
            jax.ShapeDtypeStruct((seq, width), BF16),
            jax.ShapeDtypeStruct((micro + 1, seq, width), BF16),
            jax.ShapeDtypeStruct((micro + 1, seq, inner), BF16),
        ],
        input_output_aliases=aliases,
        cost_estimate=pl.CostEstimate(
            flops=4 * seq * width * inner, bytes_accessed=4 * width * inner, transcendentals=0
        ),
        compiler_params=pltpu.CompilerParams(vmem_limit_bytes=40 * 1024 * 1024),
    )(flags, *operands)


def ring_phase(axis, local, halves):
    low, high = halves
    up2 = shifted(local(2, low).astype(BF16), axis, 1)
    down2 = shifted(local(2, high).astype(BF16), axis, -1)
    up1 = shifted(local(1, high).astype(BF16), axis, 1)
    down1 = shifted(local(3, low).astype(BF16), axis, -1)
    up = shifted(total(local(1, low), up2).astype(BF16), axis, 1)
    down = shifted(total(local(3, high), down2).astype(BF16), axis, -1)
    return total(local(0, low), down1, up), total(local(0, high), up1, down)


def second_phase(axis, parts):
    place = lax.axis_index(axis)
    parts = [part.astype(BF16) for part in parts]

    def local(ahead, half):
        return lax.dynamic_index_in_dim(parts[half], (place + ahead) % 4, 0, False)

    return ring_phase(axis, local, (0, 1))


def last_phase(parts):
    high = lax.axis_index("yh") == 1
    away = jnp.where(high, parts[0], parts[1]).astype(BF16)
    kept = jnp.where(high, parts[1], parts[0])
    return kept + shifted(away, "yh", 1).astype(F32)


def replica_sum(rows):
    for axis in ("x", "z"):
        rows = rows + shifted(rows, axis, 1) + shifted(rows, axis, -1) + shifted(rows, axis, 2)
    return rows + shifted(rows, "yh", 1)


def on_device(stash, attn, w_value, w_out, out_grad, order, check_rows):
    section = lax.axis_index("pipe")
    inputs = stash[0]
    probs = attn[0][:, 0]
    wv = w_value[0]
    wo = w_out[0]
    micro, seq, width = inputs.shape
    inner = wv.shape[1]
    heads = probs.shape[1]
    head_dim = inner // heads
    sections = lax.axis_size("pipe")
    replicas = lax.axis_size("yh") * lax.axis_size("z") * lax.axis_size("x")
    grad_scale = F32((micro * seq * replicas) ** -0.5)
    check_scale = F32(width**-0.5)
    share = width // sections

    tops = []
    for m in range(micro):
        own = out_grad[m]
        gathered = [lax.ppermute(own, "pipe", [(s, sections - 1)]) for s in range(sections - 1)]
        tops.append(tuple(gathered) + (own,))

    x_flat = inputs.reshape(micro * seq, width)
    x_turned = x_flat.T
    values = jnp.dot(x_flat, wv, preferred_element_type=F32).astype(BF16)
    causal = (jnp.arange(seq)[:, None] >= jnp.arange(seq)[None, :]).astype(BF16)
    context = jnp.einsum(
        "bhij,bjhd->bihd",
        probs * causal,
        values.reshape(micro, seq, heads, head_dim),
        preferred_element_type=F32,
    )
    ctx_flat = context.reshape(micro * seq, inner).astype(BF16)

    arriving = list(tops)
    stores = None
    results = [None] * micro
    for turn in range(sections):
        here = section == sections - 1 - turn
        for m in range(micro):
            flags = jnp.stack(
                [here.astype(jnp.int32), order[m], jnp.where(here, order[m], micro)]
            )
            dx, dy_store, dv_store = section_step(flags, arriving[m], probs, wo, wv, stores)
            stores = (dy_store, dv_store)
            if turn < sections - 1:
                arriving[m] = lax.ppermute(
                    dx, "pipe", [(sections - 1 - turn, sections - 2 - turn)]
                )
            else:
                parts = [dx[:, s * share : (s + 1) * share] for s in range(sections)]
                owned = parts[0]
                for s in range(1, sections):
                    owned = jnp.where(
                        section == s, lax.ppermute(parts[s], "pipe", [(0, s)]), owned
                    )
                results[m] = owned

    dy_flat = dy_store[:micro].reshape(micro * seq, width)
    dv_flat = dv_store[:micro].reshape(micro * seq, inner)

    rows = width // replicas
    z_place, x_place = lax.axis_index("z"), lax.axis_index("x")

    def out_term(ahead, half):
        start = half * (width // 2) + ((z_place + ahead) % 4) * (4 * rows)
        columns = lax.dynamic_slice_in_dim(dy_flat, start, 4 * rows, 1)
        return lax.dot_general(columns, ctx_flat, TN, preferred_element_type=F32) * grad_scale

    turned = x_turned.reshape(2, 4, 4, rows, micro * seq)

    def value_term(ahead, half):
        columns = lax.dynamic_index_in_dim(turned[half], (x_place + ahead) % 4, 1, False)
        columns = columns.reshape(4 * rows, micro * seq)
        return jnp.dot(columns, dv_flat, preferred_element_type=F32) * grad_scale

    out_parts = ring_phase("z", out_term, (0, 1))
    value_parts = ring_phase("x", value_term, (0, 1))
    out_parts = second_phase("x", [part.reshape(4, rows, inner) for part in out_parts])
    value_parts = second_phase("z", [part.reshape(4, rows, inner) for part in value_parts])
    grad_o = last_phase(out_parts)
    grad_v = last_phase(value_parts)

    check_bf = check_rows.astype(BF16)
    highest = lax.Precision.HIGHEST
    value_rows = lax.dot_general(check_bf, x_flat, NT, preferred_element_type=F32)
    out_rows = lax.dot_general(check_bf, dy_flat, NT, preferred_element_type=F32)
    checks = jnp.stack(
        [
            jnp.dot(value_rows, dv_flat.astype(F32), precision=highest),
            jnp.dot(out_rows, ctx_flat.astype(F32), precision=highest),
        ]
    )
    check_sum = replica_sum(checks * (grad_scale * check_scale))
    return (grad_v[None], grad_o[None], check_sum[None], jnp.stack(results))


def solution(mesh):
    fine = Mesh(mesh.devices.reshape(4, 2, 4, 4), ("pipe",) + REPLICAS)
    return jax.shard_map(
        on_device,
        mesh=fine,
        in_specs=(
            P("pipe", None, REPLICAS, None),
            P("pipe", None, REPLICAS, None, None, None),
            P("pipe", None, None),
            P("pipe", None, None),
            P(None, REPLICAS, "pipe"),
            P(),
            P(),
        ),
        out_specs=(
            P("pipe", REPLICAS, None),
            P("pipe", REPLICAS, None),
            P("pipe", None, None, None),
            P(None, REPLICAS, "pipe"),
        ),
        check_vma=False,
    )
```

```python
import functools

import jax
import jax.numpy as jnp
from jax import lax
from jax.experimental import pallas as pl
from jax.experimental.pallas import tpu as pltpu
from jax.sharding import Mesh
from jax.sharding import PartitionSpec as P

F32 = jnp.float32
BF16 = jnp.bfloat16
NT = (((1,), (1,)), ((), ()))
TN = (((0,), (0,)), ((), ()))
REPLICAS = ("yh", "z", "x")
CHUNKS = 8
RING = 4
VMEM_LIMIT = 34


def shifted(array, axis, distance):
    size = lax.axis_size(axis)
    return lax.ppermute(array, axis, [(i, (i + distance) % size) for i in range(size)])


def total(*terms):
    result = terms[0].astype(F32)
    for term in terms[1:]:
        result = result + term.astype(F32)
    return result


def section_kernel(first, heads, head_dim, meta, token, *refs):
    sources = refs[: RING if first else 1]
    refs = refs[len(sources) :]
    probs, rows, w_out, w_value = refs[:4]
    token_out, dx_out, y0, y1, y2, y3, dv_out, seen_out = refs[-19:-11]
    dy, dx, wo_in, wv_in, acc, dvals, weights_in, rows_in, seen, in_sems, out_sems = refs[-11:]
    seq, inner = acc.shape
    width = CHUNKS * inner
    token_out[0] = 0

    @pl.when(meta[0] == 1)
    def _():
        loads = []
        for c in range(CHUNKS):
            if first:
                source = sources[c // 2].at[:, pl.ds((c % 2) * inner, inner)]
            else:
                source = sources[0].at[c]
            loads.append(pltpu.make_async_copy(source, dy.at[c], in_sems.at[c]))
        loads.append(pltpu.make_async_copy(rows, rows_in, in_sems.at[CHUNKS]))
        loads.append(pltpu.make_async_copy(probs.at[meta[1]], weights_in, in_sems.at[CHUNKS + 1]))
        upper, lower = [], []
        for c in range(CHUNKS):
            part = pl.ds(c * inner, inner)
            upper.append(
                pltpu.make_async_copy(w_out.at[:, part], wo_in.at[c], in_sems.at[CHUNKS + 2 + c])
            )
            lower.append(
                pltpu.make_async_copy(w_value.at[part], wv_in.at[c], in_sems.at[2 * CHUNKS + 2 + c])
            )
        loads[CHUNKS].start()
        for c in range(CHUNKS):
            loads[c].start()
            upper[c].start()
        loads[CHUNKS + 1].start()
        loads[CHUNKS].wait()
        for c in range(CHUNKS):
            loads[c].wait()
            upper[c].wait()
            lower[c].start()
            columns = slice(c * inner, (c + 1) * inner)
            part = lax.dot_general(dy[c], wo_in[c], NT, preferred_element_type=F32)
            checks = lax.dot_general(rows_in[:, columns], dy[c], NT, preferred_element_type=F32)
            if c == 0:
                acc[...] = part
                seen[...] = checks
            else:
                acc[...] += part
                seen[...] += checks
        stores = [pltpu.make_async_copy(seen, seen_out, out_sems.at[0])]
        for ahead, kept in enumerate((y0, y1, y2, y3)):
            for half in range(2):
                chunk = half * RING + lax.rem(meta[2] + ahead, RING)
                stores.append(
                    pltpu.make_async_copy(dy.at[chunk], kept.at[half], out_sems.at[len(stores)])
                )
        for store in stores:
            store.start()
        loads[CHUNKS + 1].wait()
        dctx = acc[...].astype(BF16)
        query = lax.broadcasted_iota(jnp.int32, (seq, seq), 0)
        keys = lax.broadcasted_iota(jnp.int32, (seq, seq), 1)
        for head in range(heads):
            weights = jnp.where(query >= keys, weights_in[head].astype(F32), 0.0).astype(BF16)
            columns = slice(head * head_dim, (head + 1) * head_dim)
            part = lax.dot_general(weights, dctx[:, columns], TN, preferred_element_type=F32)
            dvals[:, columns] = part.astype(BF16)
        stores.append(pltpu.make_async_copy(dvals, dv_out, out_sems.at[len(stores)]))
        stores[-1].start()
        for c in range(CHUNKS):
            lower[c].wait()
            part = lax.dot_general(dvals[...], wv_in[c], NT, preferred_element_type=F32)
            dx[c] = (dy[c].astype(F32) + part).astype(BF16)
            stores.append(
                pltpu.make_async_copy(dx.at[c], dx_out.at[c], out_sems.at[len(stores)])
            )
            stores[-1].start()
        for store in stores:
            store.wait()


def section_step(meta, token, sources, probs, rows, w_out, w_value, kept, after=()):
    first = len(sources) > 1
    micro, heads, seq, _ = probs.shape
    inner, width = w_out.shape
    in_memory = pl.BlockSpec(memory_space=pltpu.HBM)
    in_smem = pl.BlockSpec(memory_space=pltpu.SMEM)
    operands = (meta, token) + tuple(sources) + (probs, rows, w_out, w_value)
    in_specs = [in_smem, in_smem] + [in_memory] * (len(sources) + 4)
    aliases = {}
    if kept is not None:
        aliases = {len(operands) + i: 2 + i for i in range(len(kept))}
        in_specs += [in_memory] * len(kept)
        operands += tuple(kept)
    in_specs += [in_memory] * len(after)
    operands += tuple(after)
    copies = 1 + 2 * RING + 1 + CHUNKS
    token, dx, *kept = pl.pallas_call(
        functools.partial(section_kernel, first, heads, inner // heads),
        in_specs=in_specs,
        out_specs=[in_smem] + [in_memory] * 7,
        out_shape=[
            jax.ShapeDtypeStruct((1,), jnp.int32),
            pltpu.HBM((CHUNKS, seq, inner), BF16),
        ]
        + [pltpu.HBM((2, seq, inner), BF16)] * RING
        + [
            pltpu.HBM((seq, inner), BF16),
            pltpu.HBM((rows.shape[0], seq), F32),
        ],
        scratch_shapes=[
            pltpu.VMEM((CHUNKS, seq, inner), BF16),
            pltpu.VMEM((CHUNKS, seq, inner), BF16),
            pltpu.VMEM((CHUNKS, inner, inner), BF16),
            pltpu.VMEM((CHUNKS, inner, inner), BF16),
            pltpu.VMEM((seq, inner), F32),
            pltpu.VMEM((seq, inner), BF16),
            pltpu.VMEM((heads, seq, seq), BF16),
            pltpu.VMEM(rows.shape, BF16),
            pltpu.VMEM((rows.shape[0], seq), F32),
            pltpu.SemaphoreType.DMA((3 * CHUNKS + 2,)),
            pltpu.SemaphoreType.DMA((copies,)),
        ],
        input_output_aliases=aliases,
        cost_estimate=pl.CostEstimate(
            flops=4 * seq * width * inner, bytes_accessed=4 * width * inner, transcendentals=0
        ),
        compiler_params=pltpu.CompilerParams(vmem_limit_bytes=VMEM_LIMIT * 1024 * 1024),
    )(*operands)
    return token, dx, kept


def early_kernel(heads, head_dim, meta, token, inputs, probs, rows, w_value, *refs):
    token_out, ctx_out, seen_out, x0, x1, x2, x3 = refs[:7]
    x, cut, wv_in, weights_in, rows_in, ctx, seen, in_sems, out_sems = refs[7:]
    micro, seq, inner = ctx.shape
    width = x.shape[2]
    share = cut.shape[3] // CHUNKS
    token_out[0] = token[0]
    loads = []
    for m in range(micro):
        loads.append(pltpu.make_async_copy(inputs.at[meta[1 + m]], x.at[m], in_sems.at[2 * m]))
        loads.append(
            pltpu.make_async_copy(probs.at[meta[1 + m]], weights_in.at[m], in_sems.at[2 * m + 1])
        )
    loads.append(pltpu.make_async_copy(rows, rows_in, in_sems.at[2 * micro]))
    for c in range(CHUNKS):
        source = w_value.at[pl.ds(c * inner, inner)]
        loads.append(pltpu.make_async_copy(source, wv_in.at[c], in_sems.at[2 * micro + 1 + c]))
    for load in loads:
        load.start()
    loads[2 * micro].wait()
    stores = []
    query = lax.broadcasted_iota(jnp.int32, (seq, seq), 0)
    keys = lax.broadcasted_iota(jnp.int32, (seq, seq), 1)
    for m in range(micro):
        loads[2 * m].wait()
        for part in range(CHUNKS):
            for place in range(RING):
                start = (part * RING + place) * share
                cut[m, place, :, part * share : (part + 1) * share] = x[m, :, start : start + share]
        for ahead, out in enumerate((x0, x1, x2, x3)):
            place = lax.rem(meta[0] + ahead, RING)
            stores.append(
                pltpu.make_async_copy(cut.at[m, place], out.at[m], out_sems.at[len(stores)])
            )
            stores[-1].start()
    for m in range(micro):
        loads[2 * m + 1].wait()
        acc = None
        for c in range(CHUNKS):
            columns = slice(c * inner, (c + 1) * inner)
            block = x[m, :, columns]
            if m == 0:
                loads[2 * micro + 1 + c].wait()
            part = jnp.dot(block, wv_in[c], preferred_element_type=F32)
            checks = lax.dot_general(rows_in[:, columns], block, NT, preferred_element_type=F32)
            acc, checked = (part, checks) if c == 0 else (acc + part, checked + checks)
        seen[m] = checked
        values = acc.astype(BF16)
        for head in range(heads):
            weights = jnp.where(query >= keys, weights_in[m, head].astype(F32), 0.0).astype(BF16)
            columns = slice(head * head_dim, (head + 1) * head_dim)
            part = jnp.dot(weights, values[:, columns], preferred_element_type=F32)
            ctx[m, :, columns] = part.astype(BF16)
    stores.append(pltpu.make_async_copy(ctx, ctx_out, out_sems.at[len(stores)]))
    stores.append(pltpu.make_async_copy(seen, seen_out, out_sems.at[len(stores)]))
    for store in stores[-2:]:
        store.start()
    for store in stores:
        store.wait()


def early_step(meta, token, inputs, probs, rows, w_value):
    micro, seq, width = inputs.shape
    inner = w_value.shape[1]
    heads = probs.shape[1]
    in_memory = pl.BlockSpec(memory_space=pltpu.HBM)
    in_smem = pl.BlockSpec(memory_space=pltpu.SMEM)
    token, ctx, seen, *blocks = pl.pallas_call(
        functools.partial(early_kernel, heads, inner // heads),
        in_specs=[in_smem, in_smem] + [in_memory] * 4,
        out_specs=[in_smem] + [in_memory] * 6,
        out_shape=[
            jax.ShapeDtypeStruct((1,), jnp.int32),
            jax.ShapeDtypeStruct((micro, seq, inner), BF16),
            jax.ShapeDtypeStruct((micro, rows.shape[0], seq), F32),
        ]
        + [pltpu.HBM((micro, seq, width // RING), BF16)] * RING,
        scratch_shapes=[
            pltpu.VMEM((micro, seq, width), BF16),
            pltpu.VMEM((micro, RING, seq, width // RING), BF16),
            pltpu.VMEM((CHUNKS, inner, inner), BF16),
            pltpu.VMEM((micro, heads, seq, seq), BF16),
            pltpu.VMEM(rows.shape, BF16),
            pltpu.VMEM((micro, seq, inner), BF16),
            pltpu.VMEM((micro, rows.shape[0], seq), F32),
            pltpu.SemaphoreType.DMA((2 * micro + 1 + CHUNKS,)),
            pltpu.SemaphoreType.DMA((RING * micro + 2,)),
        ],
        cost_estimate=pl.CostEstimate(
            flops=8 * micro * seq * width * inner,
            bytes_accessed=4 * width * inner,
            transcendentals=0,
        ),
        compiler_params=pltpu.CompilerParams(vmem_limit_bytes=VMEM_LIMIT * 1024 * 1024),
    )(meta, token, inputs, probs, rows, w_value)
    return token, ctx, seen, blocks


def ring_sum(axis, parts):
    place = lax.axis_index(axis)

    def local(ahead, half):
        return lax.dynamic_index_in_dim(parts[half], (place + ahead) % RING, 0, False)

    up2 = shifted(local(2, 0).astype(BF16), axis, 1)
    down2 = shifted(local(2, 1).astype(BF16), axis, -1)
    up = jnp.stack([local(1, 1), total(local(1, 0), up2)]).astype(BF16)
    down = jnp.stack([local(3, 0), total(local(3, 1), down2)]).astype(BF16)
    up = shifted(up, axis, 1)
    down = shifted(down, axis, -1)
    return total(local(0, 0), down[0], up[1]), total(local(0, 1), up[0], down[1])


def last_phase(parts):
    high = lax.axis_index("yh") == 1
    away = jnp.where(high, parts[0], parts[1]).astype(BF16)
    kept = jnp.where(high, parts[1], parts[0])
    return kept + shifted(away, "yh", 1).astype(F32)


def replica_sum(rows):
    for axis in ("x", "z"):
        rows = rows + shifted(rows, axis, 1)
        rows = rows + shifted(rows, axis, 2)
    return rows + shifted(rows, "yh", 1)


def exchanged(blocks, axis):
    return [blocks[0]] + [shifted(blocks[k], axis, d) for k, d in ((1, 1), (2, 2), (3, -1))]


def on_device(stash, attn, w_value, w_out, out_grad, order, check_rows):
    section = lax.axis_index("pipe")
    inputs = stash[0]
    probs = attn[0][:, 0]
    wv = w_value[0]
    wo = w_out[0]
    micro, seq, width = inputs.shape
    inner = wv.shape[1]
    heads = probs.shape[1]
    head_dim = inner // heads
    sections = lax.axis_size("pipe")
    replicas = lax.axis_size("yh") * lax.axis_size("z") * lax.axis_size("x")
    grad_scale = F32((micro * seq * replicas) ** -0.5)
    check_scale = F32(width**-0.5)
    highest = lax.Precision.HIGHEST
    n_checks = check_rows.shape[0]
    rows = width // replicas
    z_place, x_place = lax.axis_index("z"), lax.axis_index("x")

    in_hbm = lambda array: pltpu.with_memory_space_constraint(array, pltpu.HBM)
    wo, wv, inputs, probs = in_hbm(wo), in_hbm(wv), in_hbm(inputs), in_hbm(probs)
    check_bf = jnp.pad(check_rows, ((0, 16 - n_checks), (0, 0))).astype(BF16)

    arriving = []
    for m in range(micro):
        own = out_grad[m]
        gathered = [lax.ppermute(own, "pipe", [(s, sections - 1)]) for s in range(sections - 1)]
        arriving.append(tuple(gathered) + (own,))

    token = jnp.zeros((1,), jnp.int32)
    kept = [None] * micro
    results = [None] * micro
    after, y_from, dv_from, early = [], [], [], {}
    for turn in range(sections):
        here = (section == sections - 1 - turn).astype(jnp.int32)
        for m in range(micro):
            meta = jnp.stack([here, order[m], z_place])
            waits = early.get((turn, m), ()) + tuple(after)
            token, dx, kept[m] = section_step(
                meta, token, arriving[m], probs, check_bf, wo, wv, kept[m], waits
            )
            if turn == sections - 1:
                *y_blocks, dv, _ = kept[m]
                dv_from.append(exchanged([dv] * RING, "x"))
                y_from.append(exchanged(y_blocks, "z"))
                after = dv_from[m][1:] + [y_from[m][1], y_from[m][3]]
            if turn == 0 and m == 0:
                places = jnp.concatenate([x_place[None], order])
                token, context, seen_values, blocks = early_step(
                    places, token, inputs, probs, check_bf, wv
                )
                x_from = exchanged(blocks, "x")
                ctx_from = exchanged([context] * RING, "z")
                early = {
                    (2, 0): (x_from[1], x_from[3]),
                    (2, 1): (x_from[2], ctx_from[1], ctx_from[3]),
                    (3, 0): (ctx_from[2],),
                }
            if turn < sections - 1:
                pair = [(sections - 1 - turn, sections - 2 - turn)]
                arriving[m] = (lax.ppermute(dx, "pipe", pair),)
            else:
                parts = dx.reshape(sections, 2, seq, inner)
                owned = parts[0]
                for s in range(1, sections):
                    owned = jnp.where(
                        section == s, lax.ppermute(parts[s], "pipe", [(0, s)]), owned
                    )
                results[m] = owned.transpose(1, 0, 2).reshape(seq, 2 * inner)
    out_sum = value_sum = checks_v = checks_o = 0.0
    for m in range(micro):
        *_, dv, seen = kept[m]
        y_all = jnp.concatenate(y_from[m], axis=1)
        c_from = jnp.concatenate([c[m] for c in ctx_from], axis=0)
        dv_all = jnp.concatenate(dv_from[m], axis=0)
        xs = jnp.concatenate([x[m] for x in x_from], axis=0)
        out_sum = out_sum + jnp.stack(
            [lax.dot_general(y_all[h], c_from, TN, preferred_element_type=F32) for h in range(2)]
        )
        value_sum = value_sum + lax.dot_general(xs, dv_all, TN, preferred_element_type=F32)
        checks_v = checks_v + jnp.dot(
            seen_values[m, :n_checks], dv.astype(F32), precision=highest
        )
        checks_o = checks_o + jnp.dot(
            seen[:n_checks], context[m].astype(F32), precision=highest
        )
    out_sum = (out_sum * grad_scale).reshape(2, RING, rows, inner)
    value_sum = (value_sum * grad_scale).reshape(2, RING, rows, inner)
    grad_o = last_phase(ring_sum("x", out_sum))
    grad_v = last_phase(ring_sum("z", value_sum))
    check_sum = replica_sum(jnp.stack([checks_v, checks_o]) * (grad_scale * check_scale))
    return (grad_v[None], grad_o[None], check_sum[None], jnp.stack(results))


def solution(mesh):
    fine = Mesh(mesh.devices.reshape(4, 2, 4, 4), ("pipe",) + REPLICAS)
    return jax.shard_map(
        on_device,
        mesh=fine,
        in_specs=(
            P("pipe", None, REPLICAS, None),
            P("pipe", None, REPLICAS, None, None, None),
            P("pipe", None, None),
            P("pipe", None, None),
            P(None, REPLICAS, "pipe"),
            P(),
            P(),
        ),
        out_specs=(
            P("pipe", REPLICAS, None),
            P("pipe", REPLICAS, None),
            P("pipe", None, None, None),
            P(None, REPLICAS, "pipe"),
        ),
        check_vma=False,
    )
```

```python
import functools

import jax
import jax.numpy as jnp
from jax import lax
from jax.experimental import pallas as pl
from jax.experimental.pallas import tpu as pltpu
from jax.sharding import Mesh
from jax.sharding import PartitionSpec as P

F32 = jnp.float32
BF16 = jnp.bfloat16
NT = (((1,), (1,)), ((), ()))
TN = (((0,), (0,)), ((), ()))
NN = (((1,), (0,)), ((), ()))
REPLICAS = ("yh", "z", "x")
CHUNKS = 8
RING = 4
VMEM_LIMIT = 34


def shifted(array, axis, distance):
    size = lax.axis_size(axis)
    return lax.ppermute(array, axis, [(i, (i + distance) % size) for i in range(size)])


def total(*terms):
    result = terms[0].astype(F32)
    for term in terms[1:]:
        result = result + term.astype(F32)
    return result


def section_kernel(first, last, heads, head_dim, meta, token, *refs):
    sources = refs[: RING if first else 1]
    refs = refs[len(sources) :]
    probs, rows, w_out, w_value = refs[:4]
    outs = refs[:-11][-(7 + (1 if last is None else RING)) :]
    token_out, y0, y1, y2, y3, dv_out, seen_out = outs[:7]
    dy, dx, wo_in, wv_in, acc, dvals, weights_in, rows_in, seen, in_sems, out_sems = refs[-11:]
    seq, inner = acc.shape
    width = CHUNKS * inner
    token_out[0] = 0
    form = NT if first else NN

    @pl.when(meta[0] == 1)
    def _():
        loads = []
        for c in range(CHUNKS):
            if first:
                source = sources[c // 2].at[:, pl.ds((c % 2) * inner, inner)]
            else:
                source = sources[0].at[c]
            loads.append(pltpu.make_async_copy(source, dy.at[c], in_sems.at[c]))
        loads.append(pltpu.make_async_copy(rows, rows_in, in_sems.at[CHUNKS]))
        loads.append(pltpu.make_async_copy(probs.at[meta[1]], weights_in, in_sems.at[CHUNKS + 1]))
        upper, lower = [], []
        for c in range(CHUNKS):
            part = pl.ds(c * inner, inner)
            source = w_out.at[:, part] if first else w_out.at[c]
            upper.append(
                pltpu.make_async_copy(source, wo_in.at[c], in_sems.at[CHUNKS + 2 + c])
            )
            source = w_value.at[part] if first else w_value.at[c]
            lower.append(
                pltpu.make_async_copy(source, wv_in.at[c], in_sems.at[2 * CHUNKS + 2 + c])
            )
        loads[CHUNKS].start()
        for c in range(CHUNKS):
            loads[c].start()
            upper[c].start()
        loads[CHUNKS + 1].start()
        loads[CHUNKS].wait()
        for c in range(CHUNKS):
            loads[c].wait()
            upper[c].wait()
            lower[c].start()
            columns = slice(c * inner, (c + 1) * inner)
            part = lax.dot_general(dy[c], wo_in[c], form, preferred_element_type=F32)
            checks = lax.dot_general(rows_in[:, columns], dy[c], NT, preferred_element_type=F32)
            if c == 0:
                acc[...] = part
                seen[...] = checks
            else:
                acc[...] += part
                seen[...] += checks
        stores = [pltpu.make_async_copy(seen, seen_out, out_sems.at[0])]
        for ahead, kept in enumerate((y0, y1, y2, y3)):
            for half in range(2):
                chunk = half * RING + lax.rem(meta[2] + ahead, RING)
                stores.append(
                    pltpu.make_async_copy(dy.at[chunk], kept.at[half], out_sems.at[len(stores)])
                )
        for store in stores:
            store.start()
        loads[CHUNKS + 1].wait()
        dctx = acc[...].astype(BF16)
        query = lax.broadcasted_iota(jnp.int32, (seq, seq), 0)
        keys = lax.broadcasted_iota(jnp.int32, (seq, seq), 1)
        for head in range(heads):
            weights = jnp.where(query >= keys, weights_in[head].astype(F32), 0.0).astype(BF16)
            columns = slice(head * head_dim, (head + 1) * head_dim)
            part = lax.dot_general(weights, dctx[:, columns], TN, preferred_element_type=F32)
            dvals[:, columns] = part.astype(BF16)
        stores.append(pltpu.make_async_copy(dvals, dv_out, out_sems.at[len(stores)]))
        stores[-1].start()
        for c in range(CHUNKS):
            lower[c].wait()
            part = lax.dot_general(dvals[...], wv_in[c], form, preferred_element_type=F32)
            dx[c] = (dy[c].astype(F32) + part).astype(BF16)
            stores.append(
                pltpu.make_async_copy(
                    dx.at[c],
                    outs[7].at[c] if last is None else outs[7 + c // 2].at[last, c % 2],
                    out_sems.at[len(stores)],
                )
            )
            stores[-1].start()
        for store in stores:
            store.wait()


def section_step(meta, token, sources, probs, rows, w_out, w_value, kept, after=(), last=None, pieces=None):
    first = len(sources) > 1
    micro, heads, seq, _ = probs.shape
    inner = w_out.shape[-2]
    width = w_out.size // inner
    in_memory = pl.BlockSpec(memory_space=pltpu.HBM)
    in_smem = pl.BlockSpec(memory_space=pltpu.SMEM)
    operands = (meta, token) + tuple(sources) + (probs, rows, w_out, w_value)
    in_specs = [in_smem, in_smem] + [in_memory] * (len(sources) + 4)
    aliases = {}
    if kept is not None:
        aliases = {len(operands) + i: 1 + i for i in range(len(kept))}
        in_specs += [in_memory] * len(kept)
        operands += tuple(kept)
    if pieces is not None:
        aliases.update({len(operands) + i: 7 + i for i in range(RING)})
        in_specs += [in_memory] * RING
        operands += tuple(pieces)
    in_specs += [in_memory] * len(after)
    operands += tuple(after)
    copies = 1 + 2 * RING + 1 + CHUNKS
    token, *results = pl.pallas_call(
        functools.partial(section_kernel, first, last, heads, inner // heads),
        in_specs=in_specs,
        out_specs=[in_smem] + [in_memory] * (6 + (1 if last is None else RING)),
        out_shape=[
            jax.ShapeDtypeStruct((1,), jnp.int32),
        ]
        + [pltpu.HBM((2, seq, inner), BF16)] * RING
        + [
            pltpu.HBM((seq, inner), BF16),
            pltpu.HBM((rows.shape[0], seq), F32),
        ]
        + (
            [pltpu.HBM((CHUNKS, seq, inner), BF16)]
            if last is None
            else [pltpu.HBM((micro, 2, seq, inner), BF16)] * RING
        ),
        scratch_shapes=[
            pltpu.VMEM((CHUNKS, seq, inner), BF16),
            pltpu.VMEM((CHUNKS, seq, inner), BF16),
            pltpu.VMEM((CHUNKS, inner, inner), BF16),
            pltpu.VMEM((CHUNKS, inner, inner), BF16),
            pltpu.VMEM((seq, inner), F32),
            pltpu.VMEM((seq, inner), BF16),
            pltpu.VMEM((heads, seq, seq), BF16),
            pltpu.VMEM(rows.shape, BF16),
            pltpu.VMEM((rows.shape[0], seq), F32),
            pltpu.SemaphoreType.DMA((3 * CHUNKS + 2,)),
            pltpu.SemaphoreType.DMA((copies,)),
        ],
        input_output_aliases=aliases,
        cost_estimate=pl.CostEstimate(
            flops=4 * seq * width * inner, bytes_accessed=4 * width * inner, transcendentals=0
        ),
        compiler_params=pltpu.CompilerParams(vmem_limit_bytes=VMEM_LIMIT * 1024 * 1024),
    )(*operands)
    return token, results[6:], results[:6]


def turn_kernel(token, w_out, w_value, out_turned, value_turned, raw, turned, in_sems, out_sems):
    inner = w_out.shape[0]
    loads, stores = [], []
    for c in range(CHUNKS):
        part = pl.ds(c * inner, inner)
        loads.append(pltpu.make_async_copy(w_out.at[:, part], raw.at[c], in_sems.at[c]))
    for c in range(CHUNKS):
        part = pl.ds(c * inner, inner)
        place = CHUNKS + c
        loads.append(pltpu.make_async_copy(w_value.at[part], raw.at[place], in_sems.at[place]))
    for load in loads:
        load.start()
    for c, load in enumerate(loads):
        load.wait()
        turned[c] = raw[c].T
        target = out_turned if c < CHUNKS else value_turned
        stores.append(
            pltpu.make_async_copy(turned.at[c], target.at[c % CHUNKS], out_sems.at[c])
        )
        stores[-1].start()
    for store in stores:
        store.wait()


def turned_weights(token, w_out, w_value):
    inner = w_out.shape[0]
    in_memory = pl.BlockSpec(memory_space=pltpu.HBM)
    return pl.pallas_call(
        turn_kernel,
        in_specs=[pl.BlockSpec(memory_space=pltpu.SMEM)] + [in_memory] * 2,
        out_specs=[in_memory] * 2,
        out_shape=[pltpu.HBM((CHUNKS, inner, inner), BF16)] * 2,
        scratch_shapes=[
            pltpu.VMEM((2 * CHUNKS, inner, inner), BF16),
            pltpu.VMEM((2 * CHUNKS, inner, inner), BF16),
            pltpu.SemaphoreType.DMA((2 * CHUNKS,)),
            pltpu.SemaphoreType.DMA((2 * CHUNKS,)),
        ],
        cost_estimate=pl.CostEstimate(
            flops=0, bytes_accessed=8 * w_out.size, transcendentals=0
        ),
        compiler_params=pltpu.CompilerParams(vmem_limit_bytes=42 * 1024 * 1024),
    )(token, w_out, w_value)


def gate_kernel(*refs):
    pass


def gated(array, after):
    in_memory = pl.BlockSpec(memory_space=pltpu.HBM)
    return pl.pallas_call(
        gate_kernel,
        in_specs=[in_memory] * (1 + len(after)),
        out_specs=in_memory,
        out_shape=pltpu.HBM(array.shape, array.dtype),
        input_output_aliases={0: 0},
    )(array, *after)


def early_kernel(heads, head_dim, meta, token, inputs, probs, rows, w_value, *refs):
    token_out, ctx_out, seen_out, x0, x1, x2, x3 = refs[:7]
    x, cut, wv_in, weights_in, rows_in, ctx, seen, in_sems, out_sems = refs[7:]
    micro, seq, inner = ctx.shape
    width = x.shape[2]
    share = cut.shape[3] // CHUNKS
    token_out[0] = token[0]
    loads = []
    for m in range(micro):
        loads.append(pltpu.make_async_copy(inputs.at[meta[1 + m]], x.at[m], in_sems.at[2 * m]))
        loads.append(
            pltpu.make_async_copy(probs.at[meta[1 + m]], weights_in.at[m], in_sems.at[2 * m + 1])
        )
    loads.append(pltpu.make_async_copy(rows, rows_in, in_sems.at[2 * micro]))
    for c in range(CHUNKS):
        source = w_value.at[pl.ds(c * inner, inner)]
        loads.append(pltpu.make_async_copy(source, wv_in.at[c], in_sems.at[2 * micro + 1 + c]))
    for load in loads:
        load.start()
    loads[2 * micro].wait()
    stores = []
    query = lax.broadcasted_iota(jnp.int32, (seq, seq), 0)
    keys = lax.broadcasted_iota(jnp.int32, (seq, seq), 1)
    for m in range(micro):
        loads[2 * m].wait()
        for part in range(CHUNKS):
            for place in range(RING):
                start = (part * RING + place) * share
                cut[m, place, :, part * share : (part + 1) * share] = x[m, :, start : start + share]
        for ahead, out in enumerate((x0, x1, x2, x3)):
            place = lax.rem(meta[0] + ahead, RING)
            stores.append(
                pltpu.make_async_copy(cut.at[m, place], out.at[m], out_sems.at[len(stores)])
            )
            stores[-1].start()
    for m in range(micro):
        loads[2 * m + 1].wait()
        acc = None
        for c in range(CHUNKS):
            columns = slice(c * inner, (c + 1) * inner)
            block = x[m, :, columns]
            if m == 0:
                loads[2 * micro + 1 + c].wait()
            part = jnp.dot(block, wv_in[c], preferred_element_type=F32)
            checks = lax.dot_general(rows_in[:, columns], block, NT, preferred_element_type=F32)
            acc, checked = (part, checks) if c == 0 else (acc + part, checked + checks)
        seen[m] = checked
        values = acc.astype(BF16)
        for head in range(heads):
            weights = jnp.where(query >= keys, weights_in[m, head].astype(F32), 0.0).astype(BF16)
            columns = slice(head * head_dim, (head + 1) * head_dim)
            part = jnp.dot(weights, values[:, columns], preferred_element_type=F32)
            ctx[m, :, columns] = part.astype(BF16)
    stores.append(pltpu.make_async_copy(ctx, ctx_out, out_sems.at[len(stores)]))
    stores.append(pltpu.make_async_copy(seen, seen_out, out_sems.at[len(stores)]))
    for store in stores[-2:]:
        store.start()
    for store in stores:
        store.wait()


def early_step(meta, token, inputs, probs, rows, w_value):
    micro, seq, width = inputs.shape
    inner = w_value.shape[1]
    heads = probs.shape[1]
    in_memory = pl.BlockSpec(memory_space=pltpu.HBM)
    in_smem = pl.BlockSpec(memory_space=pltpu.SMEM)
    token, ctx, seen, *blocks = pl.pallas_call(
        functools.partial(early_kernel, heads, inner // heads),
        in_specs=[in_smem, in_smem] + [in_memory] * 4,
        out_specs=[in_smem] + [in_memory] * 6,
        out_shape=[
            jax.ShapeDtypeStruct((1,), jnp.int32),
            jax.ShapeDtypeStruct((micro, seq, inner), BF16),
            jax.ShapeDtypeStruct((micro, rows.shape[0], seq), F32),
        ]
        + [pltpu.HBM((micro, seq, width // RING), BF16)] * RING,
        scratch_shapes=[
            pltpu.VMEM((micro, seq, width), BF16),
            pltpu.VMEM((micro, RING, seq, width // RING), BF16),
            pltpu.VMEM((CHUNKS, inner, inner), BF16),
            pltpu.VMEM((micro, heads, seq, seq), BF16),
            pltpu.VMEM(rows.shape, BF16),
            pltpu.VMEM((micro, seq, inner), BF16),
            pltpu.VMEM((micro, rows.shape[0], seq), F32),
            pltpu.SemaphoreType.DMA((2 * micro + 1 + CHUNKS,)),
            pltpu.SemaphoreType.DMA((RING * micro + 2,)),
        ],
        cost_estimate=pl.CostEstimate(
            flops=8 * micro * seq * width * inner,
            bytes_accessed=4 * width * inner,
            transcendentals=0,
        ),
        compiler_params=pltpu.CompilerParams(vmem_limit_bytes=VMEM_LIMIT * 1024 * 1024),
    )(meta, token, inputs, probs, rows, w_value)
    return token, ctx, seen, blocks


def ring_sum(axis, parts):
    place = lax.axis_index(axis)

    def local(ahead, half):
        return lax.dynamic_index_in_dim(parts[half], (place + ahead) % RING, 0, False)

    up2 = shifted(local(2, 0).astype(BF16), axis, 1)
    down2 = shifted(local(2, 1).astype(BF16), axis, -1)
    up = jnp.stack([local(1, 1), total(local(1, 0), up2)]).astype(BF16)
    down = jnp.stack([local(3, 0), total(local(3, 1), down2)]).astype(BF16)
    up = shifted(up, axis, 1)
    down = shifted(down, axis, -1)
    sums = (total(local(0, 0), down[0], up[1]), total(local(0, 1), up[0], down[1]))
    return sums, (up2, down2)


def last_phase(parts, earlier):
    high = lax.axis_index("yh") == 1
    away = gated(jnp.where(high, parts[0], parts[1]).astype(BF16), [earlier])
    kept = jnp.where(high, parts[1], parts[0])
    return kept + shifted(away, "yh", 1).astype(F32)


def replica_sum(rows):
    for axis in ("x", "z"):
        rows = rows + shifted(rows, axis, 1)
        rows = rows + shifted(rows, axis, 2)
    return rows + shifted(rows, "yh", 1)


def exchanged(blocks, axis):
    return [blocks[0]] + [shifted(blocks[k], axis, d) for k, d in ((1, 1), (2, 2), (3, -1))]


def on_device(stash, attn, w_value, w_out, out_grad, order, check_rows):
    section = lax.axis_index("pipe")
    inputs = stash[0]
    probs = attn[0][:, 0]
    wv = w_value[0]
    wo = w_out[0]
    micro, seq, width = inputs.shape
    inner = wv.shape[1]
    heads = probs.shape[1]
    head_dim = inner // heads
    sections = lax.axis_size("pipe")
    replicas = lax.axis_size("yh") * lax.axis_size("z") * lax.axis_size("x")
    grad_scale = F32((micro * seq * replicas) ** -0.5)
    check_scale = F32(width**-0.5)
    highest = lax.Precision.HIGHEST
    n_checks = check_rows.shape[0]
    rows = width // replicas
    z_place, x_place = lax.axis_index("z"), lax.axis_index("x")

    in_hbm = lambda array: pltpu.with_memory_space_constraint(array, pltpu.HBM)
    wo, wv, inputs, probs = in_hbm(wo), in_hbm(wv), in_hbm(inputs), in_hbm(probs)
    check_bf = jnp.pad(check_rows, ((0, 16 - n_checks), (0, 0))).astype(BF16)

    arriving = []
    for m in range(micro):
        own = out_grad[m]
        gathered = [lax.ppermute(own, "pipe", [(s, sections - 1)]) for s in range(sections - 1)]
        arriving.append(tuple(gathered) + (own,))

    token = jnp.zeros((1,), jnp.int32)
    weights = (wo, wv)
    pieces = None
    kept = [None] * micro
    after, y_from, dv_from, early = [], [], [], {}
    for turn in range(sections):
        here = (section == sections - 1 - turn).astype(jnp.int32)
        for m in range(micro):
            meta = jnp.stack([here, order[m], z_place])
            waits = early.get((turn, m), ()) + tuple(after)
            token, sent, kept[m] = section_step(
                meta, token, arriving[m], probs, check_bf, *weights, kept[m], waits,
                m if turn == sections - 1 else None, pieces,
            )
            if turn == 0 and m == 0:
                places = jnp.concatenate([x_place[None], order])
                token, context, seen_values, blocks = early_step(
                    places, token, inputs, probs, check_bf, wv
                )
                x_from = exchanged(blocks, "x")
                ctx_from = exchanged([context] * RING, "z")
                early = {
                    (2, 0): (x_from[1], x_from[3]),
                    (2, 1): (x_from[2], ctx_from[1], ctx_from[3]),
                    (3, 0): (ctx_from[2],),
                }
            if turn == 0 and m == micro - 1:
                weights = turned_weights(token, wo, wv)
            if turn < sections - 1:
                pair = [(sections - 1 - turn, sections - 2 - turn)]
                arriving[m] = (lax.ppermute(sent[0], "pipe", pair),)
            else:
                pieces = sent
                *y_blocks, dv, _ = kept[m]
                dv_from.append(exchanged([dv] * RING, "x"))
                y_from.append(exchanged(y_blocks, "z"))
                after = dv_from[m][1:] + [y_from[m][1], y_from[m][3]]

    out_sum = value_sum = checks_v = checks_o = 0.0
    for m in range(micro):
        *_, dv, seen = kept[m]
        y_all = jnp.concatenate(y_from[m], axis=1)
        c_from = jnp.concatenate([c[m] for c in ctx_from], axis=0)
        dv_all = jnp.concatenate(dv_from[m], axis=0)
        xs = jnp.concatenate([x[m] for x in x_from], axis=0)
        out_sum = out_sum + jnp.stack(
            [lax.dot_general(y_all[h], c_from, TN, preferred_element_type=F32) for h in range(2)]
        )
        value_sum = value_sum + lax.dot_general(xs, dv_all, TN, preferred_element_type=F32)
        checks_v = checks_v + jnp.dot(
            seen_values[m, :n_checks], dv.astype(F32), precision=highest
        )
        checks_o = checks_o + jnp.dot(
            seen[:n_checks], context[m].astype(F32), precision=highest
        )
    out_sum = (out_sum * grad_scale).reshape(2, RING, rows, inner)
    value_sum = (value_sum * grad_scale).reshape(2, RING, rows, inner)
    came = {}
    earlier = dv_from[-1][1:]
    for s in (2, 3, 1):
        came[s] = lax.ppermute(gated(pieces[s], earlier), "pipe", [(0, s)])
        earlier = [came[s]]
    owned = pieces[0]
    for s in (1, 2, 3):
        owned = jnp.where(section == s, came[s], owned)
    owned = owned.transpose(0, 2, 1, 3).reshape(micro, seq, 2 * inner)
    value_parts, first = ring_sum("z", value_sum)
    out_parts, _ = ring_sum("x", out_sum)
    checks = jnp.stack([checks_v, checks_o]) * (grad_scale * check_scale)
    check_sum = replica_sum(gated(checks, first + (came[2],)))
    grad_v = last_phase(value_parts, came[3])
    grad_o = last_phase(out_parts, came[3])
    return (grad_v[None], grad_o[None], check_sum[None], owned)


def solution(mesh):
    fine = Mesh(mesh.devices.reshape(4, 2, 4, 4), ("pipe",) + REPLICAS)
    return jax.shard_map(
        on_device,
        mesh=fine,
        in_specs=(
            P("pipe", None, REPLICAS, None),
            P("pipe", None, REPLICAS, None, None, None),
            P("pipe", None, None),
            P("pipe", None, None),
            P(None, REPLICAS, "pipe"),
            P(),
            P(),
        ),
        out_specs=(
            P("pipe", REPLICAS, None),
            P("pipe", REPLICAS, None),
            P("pipe", None, None, None),
            P(None, REPLICAS, "pipe"),
        ),
        check_vma=False,
    )
```

```python
import functools

import jax
import jax.numpy as jnp
from jax import lax
from jax.experimental import pallas as pl
from jax.experimental.pallas import tpu as pltpu
from jax.sharding import Mesh
from jax.sharding import PartitionSpec as P

F32 = jnp.float32
BF16 = jnp.bfloat16
NT = (((1,), (1,)), ((), ()))
TN = (((0,), (0,)), ((), ()))
REPLICAS = ("yh", "z", "x")
CHUNKS = 8
RING = 4
VMEM_LIMIT = 34


def shifted(array, axis, distance):
    size = lax.axis_size(axis)
    return lax.ppermute(array, axis, [(i, (i + distance) % size) for i in range(size)])


def total(*terms):
    result = terms[0].astype(F32)
    for term in terms[1:]:
        result = result + term.astype(F32)
    return result


def section_kernel(first, last, heads, head_dim, meta, token, *refs):
    sources = refs[: RING if first else 1]
    refs = refs[len(sources) :]
    probs, rows, w_out, w_value = refs[:4]
    outs = refs[:-11][-(7 + (1 if last is None else RING)) :]
    token_out, y0, y1, y2, y3, dv_out, seen_out = outs[:7]
    dy, dx, wo_in, wv_in, acc, dvals, weights_in, rows_in, seen, in_sems, out_sems = refs[-11:]
    seq, inner = acc.shape
    width = CHUNKS * inner
    token_out[0] = 0

    @pl.when(meta[0] == 1)
    def _():
        loads = []
        for c in range(CHUNKS):
            if first:
                source = sources[c // 2].at[:, pl.ds((c % 2) * inner, inner)]
            else:
                source = sources[0].at[c]
            loads.append(pltpu.make_async_copy(source, dy.at[c], in_sems.at[c]))
        loads.append(pltpu.make_async_copy(rows, rows_in, in_sems.at[CHUNKS]))
        loads.append(pltpu.make_async_copy(probs.at[meta[1]], weights_in, in_sems.at[CHUNKS + 1]))
        upper, lower = [], []
        for c in range(CHUNKS):
            part = pl.ds(c * inner, inner)
            upper.append(
                pltpu.make_async_copy(w_out.at[:, part], wo_in.at[c], in_sems.at[CHUNKS + 2 + c])
            )
            lower.append(
                pltpu.make_async_copy(w_value.at[part], wv_in.at[c], in_sems.at[2 * CHUNKS + 2 + c])
            )
        loads[CHUNKS].start()
        for c in range(CHUNKS):
            loads[c].start()
            upper[c].start()
        loads[CHUNKS + 1].start()
        loads[CHUNKS].wait()
        for c in range(CHUNKS):
            loads[c].wait()
            upper[c].wait()
            lower[c].start()
            columns = slice(c * inner, (c + 1) * inner)
            part = lax.dot_general(dy[c], wo_in[c], NT, preferred_element_type=F32)
            checks = lax.dot_general(rows_in[:, columns], dy[c], NT, preferred_element_type=F32)
            if c == 0:
                acc[...] = part
                seen[...] = checks
            else:
                acc[...] += part
                seen[...] += checks
        stores = [pltpu.make_async_copy(seen, seen_out, out_sems.at[0])]
        for ahead, kept in enumerate((y0, y1, y2, y3)):
            for half in range(2):
                chunk = half * RING + lax.rem(meta[2] + ahead, RING)
                stores.append(
                    pltpu.make_async_copy(dy.at[chunk], kept.at[half], out_sems.at[len(stores)])
                )
        for store in stores:
            store.start()
        loads[CHUNKS + 1].wait()
        dctx = acc[...].astype(BF16)
        query = lax.broadcasted_iota(jnp.int32, (seq, seq), 0)
        keys = lax.broadcasted_iota(jnp.int32, (seq, seq), 1)
        for head in range(heads):
            weights = jnp.where(query >= keys, weights_in[head].astype(F32), 0.0).astype(BF16)
            columns = slice(head * head_dim, (head + 1) * head_dim)
            part = lax.dot_general(weights, dctx[:, columns], TN, preferred_element_type=F32)
            dvals[:, columns] = part.astype(BF16)
        stores.append(pltpu.make_async_copy(dvals, dv_out, out_sems.at[len(stores)]))
        stores[-1].start()
        for c in range(CHUNKS):
            lower[c].wait()
            part = lax.dot_general(dvals[...], wv_in[c], NT, preferred_element_type=F32)
            dx[c] = (dy[c].astype(F32) + part).astype(BF16)
            stores.append(
                pltpu.make_async_copy(
                    dx.at[c],
                    outs[7].at[c] if last is None else outs[7 + c // 2].at[last, c % 2],
                    out_sems.at[len(stores)],
                )
            )
            stores[-1].start()
        for store in stores:
            store.wait()


def section_step(meta, token, sources, probs, rows, w_out, w_value, kept, after=(), last=None, pieces=None):
    first = len(sources) > 1
    micro, heads, seq, _ = probs.shape
    inner, width = w_out.shape
    in_memory = pl.BlockSpec(memory_space=pltpu.HBM)
    in_smem = pl.BlockSpec(memory_space=pltpu.SMEM)
    operands = (meta, token) + tuple(sources) + (probs, rows, w_out, w_value)
    in_specs = [in_smem, in_smem] + [in_memory] * (len(sources) + 4)
    aliases = {}
    if kept is not None:
        aliases = {len(operands) + i: 1 + i for i in range(len(kept))}
        in_specs += [in_memory] * len(kept)
        operands += tuple(kept)
    if pieces is not None:
        aliases.update({len(operands) + i: 7 + i for i in range(RING)})
        in_specs += [in_memory] * RING
        operands += tuple(pieces)
    in_specs += [pl.BlockSpec(memory_space=pl.ANY)] * len(after)
    operands += tuple(after)
    copies = 1 + 2 * RING + 1 + CHUNKS
    token, *results = pl.pallas_call(
        functools.partial(section_kernel, first, last, heads, inner // heads),
        in_specs=in_specs,
        out_specs=[in_smem] + [in_memory] * (6 + (1 if last is None else RING)),
        out_shape=[
            jax.ShapeDtypeStruct((1,), jnp.int32),
        ]
        + [pltpu.HBM((2, seq, inner), BF16)] * RING
        + [
            pltpu.HBM((seq, inner), BF16),
            pltpu.HBM((rows.shape[0], seq), F32),
        ]
        + (
            [pltpu.HBM((CHUNKS, seq, inner), BF16)]
            if last is None
            else [pltpu.HBM((micro, 2, seq, inner), BF16)] * RING
        ),
        scratch_shapes=[
            pltpu.VMEM((CHUNKS, seq, inner), BF16),
            pltpu.VMEM((CHUNKS, seq, inner), BF16),
            pltpu.VMEM((CHUNKS, inner, inner), BF16),
            pltpu.VMEM((CHUNKS, inner, inner), BF16),
            pltpu.VMEM((seq, inner), F32),
            pltpu.VMEM((seq, inner), BF16),
            pltpu.VMEM((heads, seq, seq), BF16),
            pltpu.VMEM(rows.shape, BF16),
            pltpu.VMEM((rows.shape[0], seq), F32),
            pltpu.SemaphoreType.DMA((3 * CHUNKS + 2,)),
            pltpu.SemaphoreType.DMA((copies,)),
        ],
        input_output_aliases=aliases,
        cost_estimate=pl.CostEstimate(
            flops=4 * seq * width * inner, bytes_accessed=4 * width * inner, transcendentals=0
        ),
        compiler_params=pltpu.CompilerParams(vmem_limit_bytes=VMEM_LIMIT * 1024 * 1024),
    )(*operands)
    return token, results[6:], results[:6]


def gate_kernel(*refs):
    pass


def gated(array, after):
    in_memory = pl.BlockSpec(memory_space=pltpu.HBM)
    return pl.pallas_call(
        gate_kernel,
        in_specs=[in_memory] + [pl.BlockSpec(memory_space=pl.ANY)] * len(after),
        out_specs=in_memory,
        out_shape=pltpu.HBM(array.shape, array.dtype),
        input_output_aliases={0: 0},
        compiler_params=pltpu.CompilerParams(vmem_limit_bytes=1024 * 1024),
    )(array, *after)


def early_kernel(heads, head_dim, meta, token, inputs, probs, rows, w_value, *refs):
    token_out, ctx_out, seen_out, x0, x1, x2, x3 = refs[:7]
    x, cut, wv_in, weights_in, rows_in, ctx, seen, in_sems, out_sems = refs[7:]
    micro, seq, inner = ctx.shape
    width = x.shape[2]
    share = cut.shape[3] // CHUNKS
    token_out[0] = token[0]
    loads = []
    for m in range(micro):
        loads.append(pltpu.make_async_copy(inputs.at[meta[1 + m]], x.at[m], in_sems.at[2 * m]))
        loads.append(
            pltpu.make_async_copy(probs.at[meta[1 + m]], weights_in.at[m], in_sems.at[2 * m + 1])
        )
    loads.append(pltpu.make_async_copy(rows, rows_in, in_sems.at[2 * micro]))
    for c in range(CHUNKS):
        source = w_value.at[pl.ds(c * inner, inner)]
        loads.append(pltpu.make_async_copy(source, wv_in.at[c], in_sems.at[2 * micro + 1 + c]))
    for load in loads:
        load.start()
    loads[2 * micro].wait()
    stores = []
    query = lax.broadcasted_iota(jnp.int32, (seq, seq), 0)
    keys = lax.broadcasted_iota(jnp.int32, (seq, seq), 1)
    for m in range(micro):
        loads[2 * m].wait()
        for part in range(CHUNKS):
            for place in range(RING):
                start = (part * RING + place) * share
                cut[m, place, :, part * share : (part + 1) * share] = x[m, :, start : start + share]
        for ahead, out in enumerate((x0, x1, x2, x3)):
            place = lax.rem(meta[0] + ahead, RING)
            stores.append(
                pltpu.make_async_copy(cut.at[m, place], out.at[m], out_sems.at[len(stores)])
            )
            stores[-1].start()
    for m in range(micro):
        loads[2 * m + 1].wait()
        acc = None
        for c in range(CHUNKS):
            columns = slice(c * inner, (c + 1) * inner)
            block = x[m, :, columns]
            if m == 0:
                loads[2 * micro + 1 + c].wait()
            part = jnp.dot(block, wv_in[c], preferred_element_type=F32)
            checks = lax.dot_general(rows_in[:, columns], block, NT, preferred_element_type=F32)
            acc, checked = (part, checks) if c == 0 else (acc + part, checked + checks)
        seen[m] = checked
        values = acc.astype(BF16)
        for head in range(heads):
            weights = jnp.where(query >= keys, weights_in[m, head].astype(F32), 0.0).astype(BF16)
            columns = slice(head * head_dim, (head + 1) * head_dim)
            part = jnp.dot(weights, values[:, columns], preferred_element_type=F32)
            ctx[m, :, columns] = part.astype(BF16)
    stores.append(pltpu.make_async_copy(ctx, ctx_out, out_sems.at[len(stores)]))
    stores.append(pltpu.make_async_copy(seen, seen_out, out_sems.at[len(stores)]))
    for store in stores[-2:]:
        store.start()
    for store in stores:
        store.wait()


def early_step(meta, token, inputs, probs, rows, w_value):
    micro, seq, width = inputs.shape
    inner = w_value.shape[1]
    heads = probs.shape[1]
    in_memory = pl.BlockSpec(memory_space=pltpu.HBM)
    in_smem = pl.BlockSpec(memory_space=pltpu.SMEM)
    token, ctx, seen, *blocks = pl.pallas_call(
        functools.partial(early_kernel, heads, inner // heads),
        in_specs=[in_smem, in_smem] + [in_memory] * 4,
        out_specs=[in_smem] + [in_memory] * 6,
        out_shape=[
            jax.ShapeDtypeStruct((1,), jnp.int32),
            jax.ShapeDtypeStruct((micro, seq, inner), BF16),
            jax.ShapeDtypeStruct((micro, rows.shape[0], seq), F32),
        ]
        + [pltpu.HBM((micro, seq, width // RING), BF16)] * RING,
        scratch_shapes=[
            pltpu.VMEM((micro, seq, width), BF16),
            pltpu.VMEM((micro, RING, seq, width // RING), BF16),
            pltpu.VMEM((CHUNKS, inner, inner), BF16),
            pltpu.VMEM((micro, heads, seq, seq), BF16),
            pltpu.VMEM(rows.shape, BF16),
            pltpu.VMEM((micro, seq, inner), BF16),
            pltpu.VMEM((micro, rows.shape[0], seq), F32),
            pltpu.SemaphoreType.DMA((2 * micro + 1 + CHUNKS,)),
            pltpu.SemaphoreType.DMA((RING * micro + 2,)),
        ],
        cost_estimate=pl.CostEstimate(
            flops=8 * micro * seq * width * inner,
            bytes_accessed=4 * width * inner,
            transcendentals=0,
        ),
        compiler_params=pltpu.CompilerParams(vmem_limit_bytes=VMEM_LIMIT * 1024 * 1024),
    )(meta, token, inputs, probs, rows, w_value)
    return token, ctx, seen, blocks


def product_kernel(of_value, m, last, meta, *refs):
    left, right, refs = refs[:RING], refs[RING : 2 * RING], refs[2 * RING :]
    before = refs[0] if m else None
    refs = refs[-1:] if last is None else refs[-4:]
    inner = right[0].shape[-1]
    rows = inner // RING
    for half in range(2):
        total = before[half] if m else None
        for k in range(RING):
            if of_value:
                part = left[k][m, :, half * inner : (half + 1) * inner], right[k][...]
            else:
                part = left[k][half], right[k][m]
            part = lax.dot_general(*part, TN, preferred_element_type=F32)
            total = part if total is None else total + part
        if last is None:
            refs[0][half] = total
        else:
            *away2, terms, acc = refs
            acc[...] = total * last
            for ahead in range(RING):
                start = lax.rem(meta[0] + ahead, RING) * rows
                term = acc[pl.ds(pl.multiple_of(start, rows), rows), :].astype(BF16)
                terms[half, ahead] = term
                if ahead == 2:
                    away2[half][...] = term


def products(of_value, m, last, place, left, right, before, after=()):
    inner = right[0].shape[-1]
    rows = inner // RING
    in_vmem = pl.BlockSpec(memory_space=pltpu.VMEM)
    operands = list(left) + list(right) + ([before] if m else [])
    if last is None:
        shapes = [jax.ShapeDtypeStruct((2, inner, inner), F32)]
        scratch = []
    else:
        shapes = [jax.ShapeDtypeStruct((rows, inner), BF16)] * 2
        shapes += [jax.ShapeDtypeStruct((2, RING, rows, inner), BF16)]
        scratch = [pltpu.VMEM((inner, inner), F32)]
    return pl.pallas_call(
        functools.partial(product_kernel, of_value, m, last),
        in_specs=[pl.BlockSpec(memory_space=pltpu.SMEM)]
        + [in_vmem] * len(operands)
        + [pl.BlockSpec(memory_space=pl.ANY)] * len(after),
        out_specs=[in_vmem] * len(shapes),
        out_shape=shapes,
        scratch_shapes=scratch,
        cost_estimate=pl.CostEstimate(
            flops=32 * inner * inner * 160, bytes_accessed=16 * inner * inner, transcendentals=0
        ),
        compiler_params=pltpu.CompilerParams(vmem_limit_bytes=24 * 1024 * 1024),
    )(place[None], *operands, *after)


def second_kernel(terms, up2, down2, up, down):
    up[0] = terms[1, 1]
    up[1] = total(terms[0, 1], up2[...]).astype(BF16)
    down[0] = terms[0, 3]
    down[1] = total(terms[1, 3], down2[...]).astype(BF16)


def third_kernel(meta, terms, up, down, *refs):
    away, kept = refs[-2:]
    low = total(terms[0, 0], down[0], up[1])
    high = total(terms[1, 0], up[0], down[1])

    @pl.when(meta[0] == 0)
    def _():
        kept[...] = low
        away[...] = high.astype(BF16)

    @pl.when(meta[0] == 1)
    def _():
        kept[...] = high
        away[...] = low.astype(BF16)


def ring_first(axis, up2, down2, terms):
    _, _, rows, inner = terms.shape
    in_vmem = pl.BlockSpec(memory_space=pltpu.VMEM)
    return pl.pallas_call(
        second_kernel,
        in_specs=[in_vmem] * 3,
        out_specs=[in_vmem] * 2,
        out_shape=[jax.ShapeDtypeStruct((2, rows, inner), BF16)] * 2,
        compiler_params=pltpu.CompilerParams(vmem_limit_bytes=8 * 1024 * 1024),
    )(terms, shifted(up2, axis, 1), shifted(down2, axis, -1))


def ring_last(axis, up, down, terms, after):
    _, _, rows, inner = terms.shape
    in_vmem = pl.BlockSpec(memory_space=pltpu.VMEM)
    in_smem = pl.BlockSpec(memory_space=pltpu.SMEM)
    away, kept = pl.pallas_call(
        third_kernel,
        in_specs=[in_smem] + [in_vmem] * 3 + [pl.BlockSpec(memory_space=pl.ANY)] * len(after),
        out_specs=[in_vmem] * 2,
        out_shape=[
            jax.ShapeDtypeStruct((rows, inner), BF16),
            jax.ShapeDtypeStruct((rows, inner), F32),
        ],
        compiler_params=pltpu.CompilerParams(vmem_limit_bytes=8 * 1024 * 1024),
    )(lax.axis_index("yh")[None], terms, shifted(up, axis, 1), shifted(down, axis, -1), *after)
    return kept + shifted(away, "yh", 1).astype(F32)


def ring_total(rows):
    for axis in ("x", "z"):
        rows = rows + shifted(rows, axis, 1)
        rows = rows + shifted(rows, axis, 2)
    return rows


def exchanged(blocks, axis):
    return [blocks[0]] + [shifted(blocks[k], axis, d) for k, d in ((1, 1), (2, 2), (3, -1))]


def on_device(stash, attn, w_value, w_out, out_grad, order, check_rows):
    section = lax.axis_index("pipe")
    inputs = stash[0]
    probs = attn[0][:, 0]
    wv = w_value[0]
    wo = w_out[0]
    micro, seq, width = inputs.shape
    inner = wv.shape[1]
    heads = probs.shape[1]
    head_dim = inner // heads
    sections = lax.axis_size("pipe")
    replicas = lax.axis_size("yh") * lax.axis_size("z") * lax.axis_size("x")
    grad_scale = (micro * seq * replicas) ** -0.5
    check_scale = width**-0.5
    highest = lax.Precision.HIGHEST
    n_checks = check_rows.shape[0]
    rows = width // replicas
    z_place, x_place = lax.axis_index("z"), lax.axis_index("x")

    in_hbm = lambda array: pltpu.with_memory_space_constraint(array, pltpu.HBM)
    wo, wv, inputs, probs = in_hbm(wo), in_hbm(wv), in_hbm(inputs), in_hbm(probs)
    check_bf = jnp.pad(check_rows, ((0, 16 - n_checks), (0, 0))).astype(BF16)

    arriving = []
    for m in range(micro):
        own = out_grad[m]
        gathered = [lax.ppermute(own, "pipe", [(s, sections - 1)]) for s in range(sections - 1)]
        arriving.append(tuple(gathered) + (own,))

    token = jnp.zeros((1,), jnp.int32)
    pieces = None
    kept = [None] * micro
    after, y_from, dv_from, early = [], [], [], {}
    for turn in range(sections):
        here = (section == sections - 1 - turn).astype(jnp.int32)
        for m in range(micro):
            meta = jnp.stack([here, order[m], z_place])
            waits = early.get((turn, m), ()) + tuple(after)
            token, sent, kept[m] = section_step(
                meta, token, arriving[m], probs, check_bf, wo, wv, kept[m], waits,
                m if turn == sections - 1 else None, pieces,
            )
            if turn == 0 and m == 0:
                places = jnp.concatenate([x_place[None], order])
                token, context, seen_values, blocks = early_step(
                    places, token, inputs, probs, check_bf, wv
                )
                x_from = exchanged(blocks, "x")
                ctx_from = exchanged([context] * RING, "z")
                early = {
                    (2, 0): (x_from[1], x_from[3]),
                    (2, 1): (x_from[2], ctx_from[1], ctx_from[3]),
                    (3, 1): (ctx_from[2],),
                }
            if turn < sections - 1:
                pair = [(sections - 1 - turn, sections - 2 - turn)]
                arriving[m] = (lax.ppermute(sent[0], "pipe", pair),)
            else:
                pieces = sent
                *y_blocks, dv, _ = kept[m]
                dv_from.append(exchanged([dv] * RING, "x"))
                y_from.append(exchanged(y_blocks, "z"))
                after = dv_from[m][1:]

    checks_v = checks_o = 0.0
    out_sum = value_sum = [None]
    for m in range(micro):
        *_, dv, seen = kept[m]
        checks_v = checks_v + jnp.dot(
            seen_values[m, :n_checks], dv.astype(F32), precision=highest
        )
        checks_o = checks_o + jnp.dot(
            seen[:n_checks], context[m].astype(F32), precision=highest
        )
        last = grad_scale if m == micro - 1 else None
        value_sum = products(True, m, last, z_place, x_from, dv_from[m], value_sum[0])
        waits = dv_from[m][1:] if m else ()
        out_sum = products(False, m, last, x_place, y_from[m], ctx_from, out_sum[0], waits)
    value_next = ring_first("z", *value_sum)
    out_next = ring_first("x", *out_sum)
    came = {}
    for s, earlier in ((2, [out_sum[0], value_sum[0]]), (3, out_next[:1]), (1, value_next[:1])):
        came[s] = lax.ppermute(gated(pieces[s], earlier), "pipe", [(0, s)])
    owned = pieces[0]
    for s in (1, 2, 3):
        owned = jnp.where(section == s, came[s], owned)
    owned = owned.transpose(0, 2, 1, 3).reshape(micro, seq, 2 * inner)
    checks = jnp.stack([checks_v, checks_o]) * (grad_scale * check_scale)
    checks = ring_total(gated(checks, out_next[:1]))
    grad_v = ring_last("z", *value_next, value_sum[2], [came[2]])
    grad_o = ring_last("x", *out_next, out_sum[2], [came[3]])
    check_sum = checks + shifted(checks, "yh", 1)
    return (grad_v[None], grad_o[None], check_sum[None], owned)


def solution(mesh):
    fine = Mesh(mesh.devices.reshape(4, 2, 4, 4), ("pipe",) + REPLICAS)
    return jax.shard_map(
        on_device,
        mesh=fine,
        in_specs=(
            P("pipe", None, REPLICAS, None),
            P("pipe", None, REPLICAS, None, None, None),
            P("pipe", None, None),
            P("pipe", None, None),
            P(None, REPLICAS, "pipe"),
            P(),
            P(),
        ),
        out_specs=(
            P("pipe", REPLICAS, None),
            P("pipe", REPLICAS, None),
            P("pipe", None, None, None),
            P(None, REPLICAS, "pipe"),
        ),
        check_vma=False,
    )
```

```python
import functools

import jax
import jax.numpy as jnp
from jax import lax
from jax.experimental import pallas as pl
from jax.experimental.pallas import tpu as pltpu
from jax.sharding import Mesh
from jax.sharding import PartitionSpec as P

F32 = jnp.float32
BF16 = jnp.bfloat16
NT = (((1,), (1,)), ((), ()))
TN = (((0,), (0,)), ((), ()))
REPLICAS = ("yh", "z", "x")
CHUNKS = 8
RING = 4
VMEM_LIMIT = 34


def shifted(array, axis, distance):
    size = lax.axis_size(axis)
    return lax.ppermute(array, axis, [(i, (i + distance) % size) for i in range(size)])


def total(*terms):
    result = terms[0].astype(F32)
    for term in terms[1:]:
        result = result + term.astype(F32)
    return result


def section_kernel(first, last, heads, head_dim, meta, token, *refs):
    sources = refs[: RING if first else 1]
    refs = refs[len(sources) :]
    probs, rows, w_out, w_value = refs[:4]
    outs = refs[:-11][-(7 + (1 if last is None else RING)) :]
    token_out, y0, y1, y2, y3, dv_out, seen_out = outs[:7]
    dy, dx, wo_in, wv_in, acc, dvals, weights_in, rows_in, seen, in_sems, out_sems = refs[-11:]
    seq, inner = acc.shape
    width = CHUNKS * inner
    token_out[0] = 0

    @pl.when(meta[0] == 1)
    def _():
        loads = []
        for c in range(CHUNKS):
            if first:
                source = sources[c // 2].at[:, pl.ds((c % 2) * inner, inner)]
            else:
                source = sources[0].at[c]
            loads.append(pltpu.make_async_copy(source, dy.at[c], in_sems.at[c]))
        loads.append(pltpu.make_async_copy(rows, rows_in, in_sems.at[CHUNKS]))
        loads.append(pltpu.make_async_copy(probs.at[meta[1]], weights_in, in_sems.at[CHUNKS + 1]))
        upper, lower = [], []
        for c in range(CHUNKS):
            part = pl.ds(c * inner, inner)
            upper.append(
                pltpu.make_async_copy(w_out.at[:, part], wo_in.at[c], in_sems.at[CHUNKS + 2 + c])
            )
            lower.append(
                pltpu.make_async_copy(w_value.at[part], wv_in.at[c], in_sems.at[2 * CHUNKS + 2 + c])
            )
        loads[CHUNKS].start()
        for c in range(CHUNKS):
            loads[c].start()
            upper[c].start()
        loads[CHUNKS + 1].start()
        loads[CHUNKS].wait()
        for c in range(CHUNKS):
            loads[c].wait()
            upper[c].wait()
            lower[c].start()
            columns = slice(c * inner, (c + 1) * inner)
            part = lax.dot_general(dy[c], wo_in[c], NT, preferred_element_type=F32)
            checks = lax.dot_general(rows_in[:, columns], dy[c], NT, preferred_element_type=F32)
            if c == 0:
                acc[...] = part
                seen[...] = checks
            else:
                acc[...] += part
                seen[...] += checks
        stores = [pltpu.make_async_copy(seen, seen_out, out_sems.at[0])]
        for ahead, kept in enumerate((y0, y1, y2, y3)):
            for half in range(2):
                chunk = half * RING + lax.rem(meta[2] + ahead, RING)
                stores.append(
                    pltpu.make_async_copy(dy.at[chunk], kept.at[half], out_sems.at[len(stores)])
                )
        for store in stores:
            store.start()
        loads[CHUNKS + 1].wait()
        dctx = acc[...].astype(BF16)
        query = lax.broadcasted_iota(jnp.int32, (seq, seq), 0)
        keys = lax.broadcasted_iota(jnp.int32, (seq, seq), 1)
        for head in range(heads):
            weights = jnp.where(query >= keys, weights_in[head].astype(F32), 0.0).astype(BF16)
            columns = slice(head * head_dim, (head + 1) * head_dim)
            part = lax.dot_general(weights, dctx[:, columns], TN, preferred_element_type=F32)
            dvals[:, columns] = part.astype(BF16)
        stores.append(pltpu.make_async_copy(dvals, dv_out, out_sems.at[len(stores)]))
        stores[-1].start()
        for c in range(CHUNKS):
            lower[c].wait()
            part = lax.dot_general(dvals[...], wv_in[c], NT, preferred_element_type=F32)
            dx[c] = (dy[c].astype(F32) + part).astype(BF16)
            stores.append(
                pltpu.make_async_copy(
                    dx.at[c],
                    outs[7].at[c] if last is None else outs[7 + c // 2].at[last, c % 2],
                    out_sems.at[len(stores)],
                )
            )
            stores[-1].start()
        for store in stores:
            store.wait()


def section_step(meta, token, sources, probs, rows, w_out, w_value, kept, after=(), last=None, pieces=None):
    first = len(sources) > 1
    micro, heads, seq, _ = probs.shape
    inner, width = w_out.shape
    in_memory = pl.BlockSpec(memory_space=pltpu.HBM)
    in_smem = pl.BlockSpec(memory_space=pltpu.SMEM)
    operands = (meta, token) + tuple(sources) + (probs, rows, w_out, w_value)
    in_specs = [in_smem, in_smem] + [in_memory] * (len(sources) + 4)
    aliases = {}
    if kept is not None:
        aliases = {len(operands) + i: 1 + i for i in range(len(kept))}
        in_specs += [in_memory] * len(kept)
        operands += tuple(kept)
    if pieces is not None:
        aliases.update({len(operands) + i: 7 + i for i in range(RING)})
        in_specs += [in_memory] * RING
        operands += tuple(pieces)
    in_specs += [pl.BlockSpec(memory_space=pl.ANY)] * len(after)
    operands += tuple(after)
    copies = 1 + 2 * RING + 1 + CHUNKS
    token, *results = pl.pallas_call(
        functools.partial(section_kernel, first, last, heads, inner // heads),
        in_specs=in_specs,
        out_specs=[in_smem] + [in_memory] * (6 + (1 if last is None else RING)),
        out_shape=[
            jax.ShapeDtypeStruct((1,), jnp.int32),
        ]
        + [pltpu.HBM((2, seq, inner), BF16)] * RING
        + [
            pltpu.HBM((seq, inner), BF16),
            pltpu.HBM((rows.shape[0], seq), F32),
        ]
        + (
            [pltpu.HBM((CHUNKS, seq, inner), BF16)]
            if last is None
            else [pltpu.HBM((micro, 2, seq, inner), BF16)] * RING
        ),
        scratch_shapes=[
            pltpu.VMEM((CHUNKS, seq, inner), BF16),
            pltpu.VMEM((CHUNKS, seq, inner), BF16),
            pltpu.VMEM((CHUNKS, inner, inner), BF16),
            pltpu.VMEM((CHUNKS, inner, inner), BF16),
            pltpu.VMEM((seq, inner), F32),
            pltpu.VMEM((seq, inner), BF16),
            pltpu.VMEM((heads, seq, seq), BF16),
            pltpu.VMEM(rows.shape, BF16),
            pltpu.VMEM((rows.shape[0], seq), F32),
            pltpu.SemaphoreType.DMA((3 * CHUNKS + 2,)),
            pltpu.SemaphoreType.DMA((copies,)),
        ],
        input_output_aliases=aliases,
        cost_estimate=pl.CostEstimate(
            flops=4 * seq * width * inner, bytes_accessed=4 * width * inner, transcendentals=0
        ),
        compiler_params=pltpu.CompilerParams(vmem_limit_bytes=VMEM_LIMIT * 1024 * 1024),
    )(*operands)
    return token, results[6:], results[:6]


def gate_kernel(*refs):
    pass


def gated(array, after):
    in_memory = pl.BlockSpec(memory_space=pltpu.HBM)
    return pl.pallas_call(
        gate_kernel,
        in_specs=[in_memory] + [pl.BlockSpec(memory_space=pl.ANY)] * len(after),
        out_specs=in_memory,
        out_shape=pltpu.HBM(array.shape, array.dtype),
        input_output_aliases={0: 0},
        compiler_params=pltpu.CompilerParams(vmem_limit_bytes=1024 * 1024),
    )(array, *after)


def early_kernel(heads, head_dim, meta, token, inputs, probs, rows, w_value, *refs):
    token_out, ctx_out, seen_out, x0, x1, x2, x3 = refs[:7]
    x, cut, wv_in, weights_in, rows_in, ctx, seen, in_sems, out_sems = refs[7:]
    micro, seq, inner = ctx.shape
    width = x.shape[2]
    share = cut.shape[3] // CHUNKS
    token_out[0] = token[0]
    loads = []
    for m in range(micro):
        loads.append(pltpu.make_async_copy(inputs.at[meta[1 + m]], x.at[m], in_sems.at[2 * m]))
        loads.append(
            pltpu.make_async_copy(probs.at[meta[1 + m]], weights_in.at[m], in_sems.at[2 * m + 1])
        )
    loads.append(pltpu.make_async_copy(rows, rows_in, in_sems.at[2 * micro]))
    for c in range(CHUNKS):
        source = w_value.at[pl.ds(c * inner, inner)]
        loads.append(pltpu.make_async_copy(source, wv_in.at[c], in_sems.at[2 * micro + 1 + c]))
    for load in loads:
        load.start()
    loads[2 * micro].wait()
    stores = []
    query = lax.broadcasted_iota(jnp.int32, (seq, seq), 0)
    keys = lax.broadcasted_iota(jnp.int32, (seq, seq), 1)
    for m in range(micro):
        loads[2 * m].wait()
        for part in range(CHUNKS):
            for place in range(RING):
                start = (part * RING + place) * share
                cut[m, place, :, part * share : (part + 1) * share] = x[m, :, start : start + share]
        for ahead, out in enumerate((x0, x1, x2, x3)):
            place = lax.rem(meta[0] + ahead, RING)
            stores.append(
                pltpu.make_async_copy(cut.at[m, place], out.at[m], out_sems.at[len(stores)])
            )
            stores[-1].start()
    for m in range(micro):
        loads[2 * m + 1].wait()
        acc = None
        for c in range(CHUNKS):
            columns = slice(c * inner, (c + 1) * inner)
            block = x[m, :, columns]
            if m == 0:
                loads[2 * micro + 1 + c].wait()
            part = jnp.dot(block, wv_in[c], preferred_element_type=F32)
            checks = lax.dot_general(rows_in[:, columns], block, NT, preferred_element_type=F32)
            acc, checked = (part, checks) if c == 0 else (acc + part, checked + checks)
        seen[m] = checked
        values = acc.astype(BF16)
        for head in range(heads):
            weights = jnp.where(query >= keys, weights_in[m, head].astype(F32), 0.0).astype(BF16)
            columns = slice(head * head_dim, (head + 1) * head_dim)
            part = jnp.dot(weights, values[:, columns], preferred_element_type=F32)
            ctx[m, :, columns] = part.astype(BF16)
    stores.append(pltpu.make_async_copy(ctx, ctx_out, out_sems.at[len(stores)]))
    stores.append(pltpu.make_async_copy(seen, seen_out, out_sems.at[len(stores)]))
    for store in stores[-2:]:
        store.start()
    for store in stores:
        store.wait()


def early_step(meta, token, inputs, probs, rows, w_value):
    micro, seq, width = inputs.shape
    inner = w_value.shape[1]
    heads = probs.shape[1]
    in_memory = pl.BlockSpec(memory_space=pltpu.HBM)
    in_smem = pl.BlockSpec(memory_space=pltpu.SMEM)
    token, ctx, seen, *blocks = pl.pallas_call(
        functools.partial(early_kernel, heads, inner // heads),
        in_specs=[in_smem, in_smem] + [in_memory] * 4,
        out_specs=[in_smem] + [in_memory] * 6,
        out_shape=[
            jax.ShapeDtypeStruct((1,), jnp.int32),
            jax.ShapeDtypeStruct((micro, seq, inner), BF16),
            jax.ShapeDtypeStruct((micro, rows.shape[0], seq), F32),
        ]
        + [pltpu.HBM((micro, seq, width // RING), BF16)] * RING,
        scratch_shapes=[
            pltpu.VMEM((micro, seq, width), BF16),
            pltpu.VMEM((micro, RING, seq, width // RING), BF16),
            pltpu.VMEM((CHUNKS, inner, inner), BF16),
            pltpu.VMEM((micro, heads, seq, seq), BF16),
            pltpu.VMEM(rows.shape, BF16),
            pltpu.VMEM((micro, seq, inner), BF16),
            pltpu.VMEM((micro, rows.shape[0], seq), F32),
            pltpu.SemaphoreType.DMA((2 * micro + 1 + CHUNKS,)),
            pltpu.SemaphoreType.DMA((RING * micro + 2,)),
        ],
        cost_estimate=pl.CostEstimate(
            flops=8 * micro * seq * width * inner,
            bytes_accessed=4 * width * inner,
            transcendentals=0,
        ),
        compiler_params=pltpu.CompilerParams(vmem_limit_bytes=VMEM_LIMIT * 1024 * 1024),
    )(meta, token, inputs, probs, rows, w_value)
    return token, ctx, seen, blocks


def product_kernel(of_value, m, last, meta, *refs):
    left, right, refs = refs[:RING], refs[RING : 2 * RING], refs[2 * RING :]
    before = refs[0] if m else None
    refs = refs[-1:] if last is None else refs[-4:]
    inner = right[0].shape[-1]
    rows = inner // RING
    for half in range(2):
        total = before[half] if m else None
        for k in range(RING):
            if of_value:
                part = left[k][m, :, half * inner : (half + 1) * inner], right[k][...]
            else:
                part = left[k][half], right[k][m]
            part = lax.dot_general(*part, TN, preferred_element_type=F32)
            total = part if total is None else total + part
        if last is None:
            refs[0][half] = total
        else:
            *away2, terms, acc = refs
            acc[...] = total * last
            for ahead in range(RING):
                start = lax.rem(meta[0] + ahead, RING) * rows
                term = acc[pl.ds(pl.multiple_of(start, rows), rows), :].astype(BF16)
                terms[half, ahead] = term
                if ahead == 2:
                    away2[half][...] = term


def products(of_value, m, last, place, left, right, before, after=()):
    inner = right[0].shape[-1]
    rows = inner // RING
    in_vmem = pl.BlockSpec(memory_space=pltpu.VMEM)
    operands = list(left) + list(right) + ([before] if m else [])
    if last is None:
        shapes = [jax.ShapeDtypeStruct((2, inner, inner), F32)]
        scratch = []
    else:
        shapes = [jax.ShapeDtypeStruct((rows, inner), BF16)] * 2
        shapes += [jax.ShapeDtypeStruct((2, RING, rows, inner), BF16)]
        scratch = [pltpu.VMEM((inner, inner), F32)]
    return pl.pallas_call(
        functools.partial(product_kernel, of_value, m, last),
        in_specs=[pl.BlockSpec(memory_space=pltpu.SMEM)]
        + [in_vmem] * len(operands)
        + [pl.BlockSpec(memory_space=pl.ANY)] * len(after),
        out_specs=[in_vmem] * len(shapes),
        out_shape=shapes,
        scratch_shapes=scratch,
        cost_estimate=pl.CostEstimate(
            flops=32 * inner * inner * 160, bytes_accessed=16 * inner * inner, transcendentals=0
        ),
        compiler_params=pltpu.CompilerParams(vmem_limit_bytes=24 * 1024 * 1024),
    )(place[None], *operands, *after)


def second_kernel(terms, up2, down2, up, down):
    up[0] = terms[1, 1]
    up[1] = total(terms[0, 1], up2[...]).astype(BF16)
    down[0] = terms[0, 3]
    down[1] = total(terms[1, 3], down2[...]).astype(BF16)


def third_kernel(meta, terms, up, down, *refs):
    away, kept = refs[-2:]
    low = total(terms[0, 0], down[0], up[1])
    high = total(terms[1, 0], up[0], down[1])

    @pl.when(meta[0] == 0)
    def _():
        kept[...] = low
        away[...] = high.astype(BF16)

    @pl.when(meta[0] == 1)
    def _():
        kept[...] = high
        away[...] = low.astype(BF16)


def ring_first(axis, up2, down2, terms):
    _, _, rows, inner = terms.shape
    in_vmem = pl.BlockSpec(memory_space=pltpu.VMEM)
    return pl.pallas_call(
        second_kernel,
        in_specs=[in_vmem] * 3,
        out_specs=[in_vmem] * 2,
        out_shape=[jax.ShapeDtypeStruct((2, rows, inner), BF16)] * 2,
        compiler_params=pltpu.CompilerParams(vmem_limit_bytes=8 * 1024 * 1024),
    )(terms, shifted(up2, axis, 1), shifted(down2, axis, -1))


def ring_last(axis, up, down, terms, after):
    _, _, rows, inner = terms.shape
    in_vmem = pl.BlockSpec(memory_space=pltpu.VMEM)
    in_smem = pl.BlockSpec(memory_space=pltpu.SMEM)
    return pl.pallas_call(
        third_kernel,
        in_specs=[in_smem] + [in_vmem] * 3 + [pl.BlockSpec(memory_space=pl.ANY)] * len(after),
        out_specs=[in_vmem] * 2,
        out_shape=[
            jax.ShapeDtypeStruct((rows, inner), BF16),
            jax.ShapeDtypeStruct((rows, inner), F32),
        ],
        compiler_params=pltpu.CompilerParams(vmem_limit_bytes=8 * 1024 * 1024),
    )(lax.axis_index("yh")[None], terms, shifted(up, axis, 1), shifted(down, axis, -1), *after)


def ring_total(rows):
    for axis in ("x", "z"):
        rows = rows + shifted(rows, axis, 1)
        rows = rows + shifted(rows, axis, 2)
    return rows


def exchanged(blocks, axis):
    return [blocks[0]] + [shifted(blocks[k], axis, d) for k, d in ((1, 1), (2, 2), (3, -1))]


def on_device(stash, attn, w_value, w_out, out_grad, order, check_rows):
    section = lax.axis_index("pipe")
    inputs = stash[0]
    probs = attn[0][:, 0]
    wv = w_value[0]
    wo = w_out[0]
    micro, seq, width = inputs.shape
    inner = wv.shape[1]
    heads = probs.shape[1]
    head_dim = inner // heads
    sections = lax.axis_size("pipe")
    replicas = lax.axis_size("yh") * lax.axis_size("z") * lax.axis_size("x")
    grad_scale = (micro * seq * replicas) ** -0.5
    check_scale = width**-0.5
    highest = lax.Precision.HIGHEST
    n_checks = check_rows.shape[0]
    rows = width // replicas
    z_place, x_place = lax.axis_index("z"), lax.axis_index("x")

    in_hbm = lambda array: pltpu.with_memory_space_constraint(array, pltpu.HBM)
    wo, wv, inputs, probs = in_hbm(wo), in_hbm(wv), in_hbm(inputs), in_hbm(probs)
    check_bf = jnp.pad(check_rows, ((0, 16 - n_checks), (0, 0))).astype(BF16)

    arriving = []
    for m in range(micro):
        own = out_grad[m]
        gathered = [lax.ppermute(own, "pipe", [(s, sections - 1)]) for s in range(sections - 1)]
        arriving.append(tuple(gathered) + (own,))

    token = jnp.zeros((1,), jnp.int32)
    pieces = None
    kept = [None] * micro
    after, y_from, dv_from, early = [], [], [], {}
    for turn in range(sections):
        here = (section == sections - 1 - turn).astype(jnp.int32)
        for m in range(micro):
            meta = jnp.stack([here, order[m], z_place])
            waits = early.get((turn, m), ()) + tuple(after)
            token, sent, kept[m] = section_step(
                meta, token, arriving[m], probs, check_bf, wo, wv, kept[m], waits,
                m if turn == sections - 1 else None, pieces,
            )
            if turn == 0 and m == 0:
                places = jnp.concatenate([x_place[None], order])
                token, context, seen_values, blocks = early_step(
                    places, token, inputs, probs, check_bf, wv
                )
                x_from = exchanged(blocks, "x")
                ctx_from = exchanged([context] * RING, "z")
                early = {
                    (2, 0): (x_from[1], x_from[3]),
                    (2, 1): (x_from[2], ctx_from[1], ctx_from[3]),
                    (3, 1): (ctx_from[2],),
                }
            if turn < sections - 1:
                pair = [(sections - 1 - turn, sections - 2 - turn)]
                arriving[m] = (lax.ppermute(sent[0], "pipe", pair),)
            else:
                pieces = sent
                *y_blocks, dv, _ = kept[m]
                dv_from.append(exchanged([dv] * RING, "x"))
                y_from.append(exchanged(y_blocks, "z"))
                after = dv_from[m][1:]

    checks_v = checks_o = 0.0
    out_sum = value_sum = [None]
    for m in range(micro):
        *_, dv, seen = kept[m]
        checks_v = checks_v + jnp.dot(
            seen_values[m, :n_checks], dv.astype(F32), precision=highest
        )
        checks_o = checks_o + jnp.dot(
            seen[:n_checks], context[m].astype(F32), precision=highest
        )
        last = grad_scale if m == micro - 1 else None
        value_sum = products(True, m, last, z_place, x_from, dv_from[m], value_sum[0])
        waits = dv_from[m][1:] if m else ()
        out_sum = products(False, m, last, x_place, y_from[m], ctx_from, out_sum[0], waits)
    value_next = ring_first("z", *value_sum)
    out_next = ring_first("x", *out_sum)
    came = {}
    came[2] = lax.ppermute(gated(pieces[2], value_next[:1]), "pipe", [(0, 2)])
    value_away, value_kept = ring_last("z", *value_next, value_sum[2], [came[2]])
    came[3] = lax.ppermute(gated(pieces[3], out_next[:1]), "pipe", [(0, 3)])
    out_away, out_kept = ring_last("x", *out_next, out_sum[2], [came[3]])
    came[1] = lax.ppermute(gated(pieces[1], [value_away]), "pipe", [(0, 1)])
    owned = pieces[0]
    for s in (1, 2, 3):
        owned = jnp.where(section == s, came[s], owned)
    owned = owned.transpose(0, 2, 1, 3).reshape(micro, seq, 2 * inner)
    checks = jnp.stack([checks_v, checks_o]) * (grad_scale * check_scale)
    checks = ring_total(gated(checks, [value_away, out_next[0]]))
    grad_v = value_kept + shifted(value_away, "yh", 1).astype(F32)
    grad_o = out_kept + shifted(out_away, "yh", 1).astype(F32)
    check_sum = checks + shifted(checks, "yh", 1)
    return (grad_v[None], grad_o[None], check_sum[None], owned)


def solution(mesh):
    fine = Mesh(mesh.devices.reshape(4, 2, 4, 4), ("pipe",) + REPLICAS)
    return jax.shard_map(
        on_device,
        mesh=fine,
        in_specs=(
            P("pipe", None, REPLICAS, None),
            P("pipe", None, REPLICAS, None, None, None),
            P("pipe", None, None),
            P("pipe", None, None),
            P(None, REPLICAS, "pipe"),
            P(),
            P(),
        ),
        out_specs=(
            P("pipe", REPLICAS, None),
            P("pipe", REPLICAS, None),
            P("pipe", None, None, None),
            P(None, REPLICAS, "pipe"),
        ),
        check_vma=False,
    )
```

```python
import functools

import jax
import jax.numpy as jnp
from jax import lax
from jax.experimental import pallas as pl
from jax.experimental.pallas import tpu as pltpu
from jax.sharding import Mesh
from jax.sharding import PartitionSpec as P

F32 = jnp.float32
BF16 = jnp.bfloat16
NT = (((1,), (1,)), ((), ()))
TN = (((0,), (0,)), ((), ()))
REPLICAS = ("yh", "z", "x")
CHUNKS = 8
RING = 4
VMEM_LIMIT = 34


def shifted(array, axis, distance):
    size = lax.axis_size(axis)
    return lax.ppermute(array, axis, [(i, (i + distance) % size) for i in range(size)])


def total(*terms):
    result = terms[0].astype(F32)
    for term in terms[1:]:
        result = result + term.astype(F32)
    return result


def section_kernel(first, last, heads, head_dim, meta, token, *refs):
    sources = refs[: RING if first else 1]
    refs = refs[len(sources) :]
    probs, rows, w_out, w_value = refs[:4]
    outs = refs[:-11][-(7 + (1 if last is None else RING)) :]
    token_out, y0, y1, y2, y3, dv_out, seen_out = outs[:7]
    dy, dx, wo_in, wv_in, acc, dvals, weights_in, rows_in, seen, in_sems, out_sems = refs[-11:]
    seq, inner = acc.shape
    width = CHUNKS * inner
    token_out[0] = 0

    @pl.when(meta[0] == 1)
    def _():
        loads = []
        for c in range(CHUNKS):
            if first:
                source = sources[c // 2].at[:, pl.ds((c % 2) * inner, inner)]
            else:
                source = sources[0].at[c]
            loads.append(pltpu.make_async_copy(source, dy.at[c], in_sems.at[c]))
        loads.append(pltpu.make_async_copy(rows, rows_in, in_sems.at[CHUNKS]))
        loads.append(pltpu.make_async_copy(probs.at[meta[1]], weights_in, in_sems.at[CHUNKS + 1]))
        upper, lower = [], []
        for c in range(CHUNKS):
            part = pl.ds(c * inner, inner)
            upper.append(
                pltpu.make_async_copy(w_out.at[:, part], wo_in.at[c], in_sems.at[CHUNKS + 2 + c])
            )
            lower.append(
                pltpu.make_async_copy(w_value.at[part], wv_in.at[c], in_sems.at[2 * CHUNKS + 2 + c])
            )
        loads[CHUNKS].start()
        for c in range(CHUNKS):
            loads[c].start()
            upper[c].start()
        loads[CHUNKS + 1].start()
        loads[CHUNKS].wait()
        for c in range(CHUNKS):
            loads[c].wait()
            upper[c].wait()
            lower[c].start()
            columns = slice(c * inner, (c + 1) * inner)
            part = lax.dot_general(dy[c], wo_in[c], NT, preferred_element_type=F32)
            checks = lax.dot_general(rows_in[:, columns], dy[c], NT, preferred_element_type=F32)
            if c == 0:
                acc[...] = part
                seen[...] = checks
            else:
                acc[...] += part
                seen[...] += checks
        stores = [pltpu.make_async_copy(seen, seen_out, out_sems.at[0])]
        for ahead, kept in enumerate((y0, y1, y2, y3)):
            for half in range(2):
                chunk = half * RING + lax.rem(meta[2] + ahead, RING)
                stores.append(
                    pltpu.make_async_copy(dy.at[chunk], kept.at[half], out_sems.at[len(stores)])
                )
        for store in stores:
            store.start()
        loads[CHUNKS + 1].wait()
        dctx = acc[...].astype(BF16)
        query = lax.broadcasted_iota(jnp.int32, (seq, seq), 0)
        keys = lax.broadcasted_iota(jnp.int32, (seq, seq), 1)
        for head in range(heads):
            weights = jnp.where(query >= keys, weights_in[head].astype(F32), 0.0).astype(BF16)
            columns = slice(head * head_dim, (head + 1) * head_dim)
            part = lax.dot_general(weights, dctx[:, columns], TN, preferred_element_type=F32)
            dvals[:, columns] = part.astype(BF16)
        stores.append(pltpu.make_async_copy(dvals, dv_out, out_sems.at[len(stores)]))
        stores[-1].start()
        for c in range(CHUNKS):
            lower[c].wait()
            part = lax.dot_general(dvals[...], wv_in[c], NT, preferred_element_type=F32)
            dx[c] = (dy[c].astype(F32) + part).astype(BF16)
            stores.append(
                pltpu.make_async_copy(
                    dx.at[c],
                    outs[7].at[c] if last is None else outs[7 + c // 2].at[last, c % 2],
                    out_sems.at[len(stores)],
                )
            )
            stores[-1].start()
        for store in stores:
            store.wait()


def section_step(meta, token, sources, probs, rows, w_out, w_value, kept, after=(), last=None, pieces=None):
    first = len(sources) > 1
    micro, heads, seq, _ = probs.shape
    inner, width = w_out.shape
    in_memory = pl.BlockSpec(memory_space=pltpu.HBM)
    in_smem = pl.BlockSpec(memory_space=pltpu.SMEM)
    operands = (meta, token) + tuple(sources) + (probs, rows, w_out, w_value)
    in_specs = [in_smem, in_smem] + [in_memory] * (len(sources) + 4)
    aliases = {}
    if kept is not None:
        aliases = {len(operands) + i: 1 + i for i in range(len(kept))}
        in_specs += [in_memory] * len(kept)
        operands += tuple(kept)
    if pieces is not None:
        aliases.update({len(operands) + i: 7 + i for i in range(RING)})
        in_specs += [in_memory] * RING
        operands += tuple(pieces)
    in_specs += [pl.BlockSpec(memory_space=pl.ANY)] * len(after)
    operands += tuple(after)
    copies = 1 + 2 * RING + 1 + CHUNKS
    token, *results = pl.pallas_call(
        functools.partial(section_kernel, first, last, heads, inner // heads),
        in_specs=in_specs,
        out_specs=[in_smem] + [in_memory] * (6 + (1 if last is None else RING)),
        out_shape=[
            jax.ShapeDtypeStruct((1,), jnp.int32),
        ]
        + [pltpu.HBM((2, seq, inner), BF16)] * RING
        + [
            pltpu.HBM((seq, inner), BF16),
            pltpu.HBM((rows.shape[0], seq), F32),
        ]
        + (
            [pltpu.HBM((CHUNKS, seq, inner), BF16)]
            if last is None
            else [pltpu.HBM((micro, 2, seq, inner), BF16)] * RING
        ),
        scratch_shapes=[
            pltpu.VMEM((CHUNKS, seq, inner), BF16),
            pltpu.VMEM((CHUNKS, seq, inner), BF16),
            pltpu.VMEM((CHUNKS, inner, inner), BF16),
            pltpu.VMEM((CHUNKS, inner, inner), BF16),
            pltpu.VMEM((seq, inner), F32),
            pltpu.VMEM((seq, inner), BF16),
            pltpu.VMEM((heads, seq, seq), BF16),
            pltpu.VMEM(rows.shape, BF16),
            pltpu.VMEM((rows.shape[0], seq), F32),
            pltpu.SemaphoreType.DMA((3 * CHUNKS + 2,)),
            pltpu.SemaphoreType.DMA((copies,)),
        ],
        input_output_aliases=aliases,
        cost_estimate=pl.CostEstimate(
            flops=4 * seq * width * inner, bytes_accessed=4 * width * inner, transcendentals=0
        ),
        compiler_params=pltpu.CompilerParams(vmem_limit_bytes=VMEM_LIMIT * 1024 * 1024),
    )(*operands)
    return token, results[6:], results[:6]


def gate_kernel(*refs):
    pass


def gated(array, after):
    in_memory = pl.BlockSpec(memory_space=pltpu.HBM)
    return pl.pallas_call(
        gate_kernel,
        in_specs=[in_memory] + [pl.BlockSpec(memory_space=pl.ANY)] * len(after),
        out_specs=in_memory,
        out_shape=pltpu.HBM(array.shape, array.dtype),
        input_output_aliases={0: 0},
        compiler_params=pltpu.CompilerParams(vmem_limit_bytes=1024 * 1024),
    )(array, *after)


def early_kernel(heads, head_dim, meta, token, inputs, probs, rows, w_value, *refs):
    token_out, ctx_out, seen_out, x0, x1, x2, x3 = refs[:7]
    x, cut, wv_in, weights_in, rows_in, ctx, seen, in_sems, out_sems = refs[7:]
    micro, seq, inner = ctx.shape
    width = x.shape[2]
    share = cut.shape[3] // CHUNKS
    token_out[0] = token[0]
    loads = []
    for m in range(micro):
        loads.append(pltpu.make_async_copy(inputs.at[meta[1 + m]], x.at[m], in_sems.at[2 * m]))
        loads.append(
            pltpu.make_async_copy(probs.at[meta[1 + m]], weights_in.at[m], in_sems.at[2 * m + 1])
        )
    loads.append(pltpu.make_async_copy(rows, rows_in, in_sems.at[2 * micro]))
    for c in range(CHUNKS):
        source = w_value.at[pl.ds(c * inner, inner)]
        loads.append(pltpu.make_async_copy(source, wv_in.at[c], in_sems.at[2 * micro + 1 + c]))
    for load in loads:
        load.start()
    loads[2 * micro].wait()
    stores = []
    query = lax.broadcasted_iota(jnp.int32, (seq, seq), 0)
    keys = lax.broadcasted_iota(jnp.int32, (seq, seq), 1)
    for m in range(micro):
        loads[2 * m].wait()
        for part in range(CHUNKS):
            for place in range(RING):
                start = (part * RING + place) * share
                cut[m, place, :, part * share : (part + 1) * share] = x[m, :, start : start + share]
        for ahead, out in enumerate((x0, x1, x2, x3)):
            place = lax.rem(meta[0] + ahead, RING)
            stores.append(
                pltpu.make_async_copy(cut.at[m, place], out.at[m], out_sems.at[len(stores)])
            )
            stores[-1].start()
    for m in range(micro):
        loads[2 * m + 1].wait()
        acc = None
        for c in range(CHUNKS):
            columns = slice(c * inner, (c + 1) * inner)
            block = x[m, :, columns]
            if m == 0:
                loads[2 * micro + 1 + c].wait()
            part = jnp.dot(block, wv_in[c], preferred_element_type=F32)
            checks = lax.dot_general(rows_in[:, columns], block, NT, preferred_element_type=F32)
            acc, checked = (part, checks) if c == 0 else (acc + part, checked + checks)
        seen[m] = checked
        values = acc.astype(BF16)
        for head in range(heads):
            weights = jnp.where(query >= keys, weights_in[m, head].astype(F32), 0.0).astype(BF16)
            columns = slice(head * head_dim, (head + 1) * head_dim)
            part = jnp.dot(weights, values[:, columns], preferred_element_type=F32)
            ctx[m, :, columns] = part.astype(BF16)
    stores.append(pltpu.make_async_copy(ctx, ctx_out, out_sems.at[len(stores)]))
    stores.append(pltpu.make_async_copy(seen, seen_out, out_sems.at[len(stores)]))
    for store in stores[-2:]:
        store.start()
    for store in stores:
        store.wait()


def early_step(meta, token, inputs, probs, rows, w_value):
    micro, seq, width = inputs.shape
    inner = w_value.shape[1]
    heads = probs.shape[1]
    in_memory = pl.BlockSpec(memory_space=pltpu.HBM)
    in_smem = pl.BlockSpec(memory_space=pltpu.SMEM)
    token, ctx, seen, *blocks = pl.pallas_call(
        functools.partial(early_kernel, heads, inner // heads),
        in_specs=[in_smem, in_smem] + [in_memory] * 4,
        out_specs=[in_smem] + [in_memory] * 6,
        out_shape=[
            jax.ShapeDtypeStruct((1,), jnp.int32),
            jax.ShapeDtypeStruct((micro, seq, inner), BF16),
            jax.ShapeDtypeStruct((micro, rows.shape[0], seq), F32),
        ]
        + [pltpu.HBM((micro, seq, width // RING), BF16)] * RING,
        scratch_shapes=[
            pltpu.VMEM((micro, seq, width), BF16),
            pltpu.VMEM((micro, RING, seq, width // RING), BF16),
            pltpu.VMEM((CHUNKS, inner, inner), BF16),
            pltpu.VMEM((micro, heads, seq, seq), BF16),
            pltpu.VMEM(rows.shape, BF16),
            pltpu.VMEM((micro, seq, inner), BF16),
            pltpu.VMEM((micro, rows.shape[0], seq), F32),
            pltpu.SemaphoreType.DMA((2 * micro + 1 + CHUNKS,)),
            pltpu.SemaphoreType.DMA((RING * micro + 2,)),
        ],
        cost_estimate=pl.CostEstimate(
            flops=8 * micro * seq * width * inner,
            bytes_accessed=4 * width * inner,
            transcendentals=0,
        ),
        compiler_params=pltpu.CompilerParams(vmem_limit_bytes=VMEM_LIMIT * 1024 * 1024),
    )(meta, token, inputs, probs, rows, w_value)
    return token, ctx, seen, blocks


def product_kernel(of_value, m, last, meta, *refs):
    left, right, refs = refs[:RING], refs[RING : 2 * RING], refs[2 * RING :]
    before = refs[0] if m else None
    refs = refs[-1:] if last is None else refs[-4:]
    inner = right[0].shape[-1]
    rows = inner // RING
    for half in range(2):
        total = before[half] if m else None
        for k in range(RING):
            if of_value:
                part = left[k][m, :, half * inner : (half + 1) * inner], right[k][...]
            else:
                part = left[k][half], right[k][m]
            part = lax.dot_general(*part, TN, preferred_element_type=F32)
            total = part if total is None else total + part
        if last is None:
            refs[0][half] = total
        else:
            *away2, terms, acc = refs
            acc[...] = total * last
            for ahead in range(RING):
                start = lax.rem(meta[0] + ahead, RING) * rows
                term = acc[pl.ds(pl.multiple_of(start, rows), rows), :].astype(BF16)
                terms[half, ahead] = term
                if ahead == 2:
                    away2[half][...] = term


def products(of_value, m, last, place, left, right, before, after=()):
    inner = right[0].shape[-1]
    rows = inner // RING
    in_vmem = pl.BlockSpec(memory_space=pltpu.VMEM)
    operands = list(left) + list(right) + ([before] if m else [])
    if last is None:
        shapes = [jax.ShapeDtypeStruct((2, inner, inner), F32)]
        scratch = []
    else:
        shapes = [jax.ShapeDtypeStruct((rows, inner), BF16)] * 2
        shapes += [jax.ShapeDtypeStruct((2, RING, rows, inner), BF16)]
        scratch = [pltpu.VMEM((inner, inner), F32)]
    return pl.pallas_call(
        functools.partial(product_kernel, of_value, m, last),
        in_specs=[pl.BlockSpec(memory_space=pltpu.SMEM)]
        + [in_vmem] * len(operands)
        + [pl.BlockSpec(memory_space=pl.ANY)] * len(after),
        out_specs=[in_vmem] * len(shapes),
        out_shape=shapes,
        scratch_shapes=scratch,
        cost_estimate=pl.CostEstimate(
            flops=inner * inner, bytes_accessed=inner, transcendentals=0
        ),
        compiler_params=pltpu.CompilerParams(vmem_limit_bytes=24 * 1024 * 1024),
    )(place[None], *operands, *after)


def second_kernel(terms, up2, down2, *refs):
    up, down = refs[-2:]
    up[0] = terms[1, 1]
    up[1] = total(terms[0, 1], up2[...]).astype(BF16)
    down[0] = terms[0, 3]
    down[1] = total(terms[1, 3], down2[...]).astype(BF16)


def third_kernel(meta, terms, up, down, away, kept):
    low = total(terms[0, 0], down[0], up[1])
    high = total(terms[1, 0], up[0], down[1])

    @pl.when(meta[0] == 0)
    def _():
        kept[...] = low
        away[...] = high.astype(BF16)

    @pl.when(meta[0] == 1)
    def _():
        kept[...] = high
        away[...] = low.astype(BF16)


def ring_first(axis, up2, down2, terms, after):
    _, _, rows, inner = terms.shape
    in_vmem = pl.BlockSpec(memory_space=pltpu.VMEM)
    return pl.pallas_call(
        second_kernel,
        in_specs=[in_vmem] * 3 + [pl.BlockSpec(memory_space=pl.ANY)] * len(after),
        out_specs=[in_vmem] * 2,
        out_shape=[jax.ShapeDtypeStruct((2, rows, inner), BF16)] * 2,
        compiler_params=pltpu.CompilerParams(vmem_limit_bytes=8 * 1024 * 1024),
    )(terms, shifted(up2, axis, 1), shifted(down2, axis, -1), *after)


def ring_last(up, down, terms):
    _, _, rows, inner = terms.shape
    in_vmem = pl.BlockSpec(memory_space=pltpu.VMEM)
    in_smem = pl.BlockSpec(memory_space=pltpu.SMEM)
    return pl.pallas_call(
        third_kernel,
        in_specs=[in_smem] + [in_vmem] * 3,
        out_specs=[in_vmem] * 2,
        out_shape=[
            jax.ShapeDtypeStruct((rows, inner), BF16),
            jax.ShapeDtypeStruct((rows, inner), F32),
        ],
        compiler_params=pltpu.CompilerParams(vmem_limit_bytes=8 * 1024 * 1024),
    )(lax.axis_index("yh")[None], terms, up, down)


def ring_total(axis, rows):
    rows = rows + shifted(rows, axis, 1)
    return rows + shifted(rows, axis, 2)


def arrived(axis, blocks):
    up, down = blocks
    return shifted(up, axis, 1), shifted(down, axis, -1)


def exchanged(blocks, axis):
    return [blocks[0]] + [shifted(blocks[k], axis, d) for k, d in ((1, 1), (2, 2), (3, -1))]


def on_device(stash, attn, w_value, w_out, out_grad, order, check_rows):
    section = lax.axis_index("pipe")
    inputs = stash[0]
    probs = attn[0][:, 0]
    wv = w_value[0]
    wo = w_out[0]
    micro, seq, width = inputs.shape
    inner = wv.shape[1]
    heads = probs.shape[1]
    head_dim = inner // heads
    sections = lax.axis_size("pipe")
    replicas = lax.axis_size("yh") * lax.axis_size("z") * lax.axis_size("x")
    grad_scale = (micro * seq * replicas) ** -0.5
    check_scale = width**-0.5
    highest = lax.Precision.HIGHEST
    n_checks = check_rows.shape[0]
    rows = width // replicas
    z_place, x_place = lax.axis_index("z"), lax.axis_index("x")

    in_hbm = lambda array: pltpu.with_memory_space_constraint(array, pltpu.HBM)
    wo, wv, inputs, probs = in_hbm(wo), in_hbm(wv), in_hbm(inputs), in_hbm(probs)
    check_bf = jnp.pad(check_rows, ((0, 16 - n_checks), (0, 0))).astype(BF16)

    arriving = []
    for m in range(micro):
        own = out_grad[m]
        gathered = [lax.ppermute(own, "pipe", [(s, sections - 1)]) for s in range(sections - 1)]
        arriving.append(tuple(gathered) + (own,))

    token = jnp.zeros((1,), jnp.int32)
    pieces = None
    kept = [None] * micro
    after, y_from, dv_from, early = [], [], [], {}
    for turn in range(sections):
        here = (section == sections - 1 - turn).astype(jnp.int32)
        for m in range(micro):
            meta = jnp.stack([here, order[m], z_place])
            waits = early.get((turn, m), ()) + tuple(after)
            token, sent, kept[m] = section_step(
                meta, token, arriving[m], probs, check_bf, wo, wv, kept[m], waits,
                m if turn == sections - 1 else None, pieces,
            )
            if turn == 0 and m == 0:
                places = jnp.concatenate([x_place[None], order])
                token, context, seen_values, blocks = early_step(
                    places, token, inputs, probs, check_bf, wv
                )
                x_from = exchanged(blocks, "x")
                ctx_from = exchanged([context] * RING, "z")
                early = {
                    (2, 0): (x_from[1], x_from[3]),
                    (2, 1): (x_from[2], ctx_from[1], ctx_from[3]),
                    (3, 1): (ctx_from[2],),
                }
            if turn < sections - 1:
                pair = [(sections - 1 - turn, sections - 2 - turn)]
                arriving[m] = (lax.ppermute(sent[0], "pipe", pair),)
            else:
                pieces = sent
                *y_blocks, dv, _ = kept[m]
                dv_from.append(exchanged([dv] * RING, "x"))
                y_from.append(exchanged(y_blocks, "z"))
                after = dv_from[m][1:] + [y_from[m][1]]

    checks_v = checks_o = 0.0
    for m in range(micro):
        *_, dv, seen = kept[m]
        checks_v = checks_v + jnp.dot(
            seen_values[m, :n_checks], dv.astype(F32), precision=highest
        )
        checks_o = checks_o + jnp.dot(
            seen[:n_checks], context[m].astype(F32), precision=highest
        )
    checks_x = ring_total("x", jnp.stack([checks_v, checks_o]) * (grad_scale * check_scale))
    checks_z = ring_total("z", checks_x)
    out_sum = value_sum = [None]
    for m in range(micro):
        last = grad_scale if m == micro - 1 else None
        value_sum = products(True, m, last, z_place, x_from, dv_from[m], value_sum[0])
        waits = dv_from[m][1:] + [checks_x] if m else ()
        out_sum = products(False, m, last, x_place, y_from[m], ctx_from, out_sum[0], waits)
    value_up, value_down = arrived("z", ring_first("z", *value_sum, []))
    out_up, out_down = arrived("x", ring_first("x", *out_sum, [checks_z]))
    came = {}
    for s in (2, 3, 1):
        came[s] = lax.ppermute(gated(pieces[s], [value_up]), "pipe", [(0, s)])
    owned = pieces[0]
    for s in (1, 2, 3):
        owned = jnp.where(section == s, came[s], owned)
    owned = owned.transpose(0, 2, 1, 3).reshape(micro, seq, 2 * inner)
    value_away, value_kept = ring_last(value_up, value_down, value_sum[2])
    out_away, out_kept = ring_last(out_up, out_down, out_sum[2])
    grad_v = value_kept + shifted(value_away, "yh", 1).astype(F32)
    grad_o = out_kept + shifted(out_away, "yh", 1).astype(F32)
    check_sum = checks_z + shifted(checks_z, "yh", 1)
    return (grad_v[None], grad_o[None], check_sum[None], owned)


def solution(mesh):
    fine = Mesh(mesh.devices.reshape(4, 2, 4, 4), ("pipe",) + REPLICAS)
    return jax.shard_map(
        on_device,
        mesh=fine,
        in_specs=(
            P("pipe", None, REPLICAS, None),
            P("pipe", None, REPLICAS, None, None, None),
            P("pipe", None, None),
            P("pipe", None, None),
            P(None, REPLICAS, "pipe"),
            P(),
            P(),
        ),
        out_specs=(
            P("pipe", REPLICAS, None),
            P("pipe", REPLICAS, None),
            P("pipe", None, None, None),
            P(None, REPLICAS, "pipe"),
        ),
        check_vma=False,
    )
```

```python
import functools

import jax
import jax.numpy as jnp
from jax import lax
from jax.experimental import pallas as pl
from jax.experimental.pallas import tpu as pltpu
from jax.sharding import Mesh
from jax.sharding import PartitionSpec as P

F32 = jnp.float32
BF16 = jnp.bfloat16
NT = (((1,), (1,)), ((), ()))
TN = (((0,), (0,)), ((), ()))
REPLICAS = ("yh", "z", "x")
CHUNKS = 8
RING = 4
VMEM_LIMIT = 34


def shifted(array, axis, distance):
    size = lax.axis_size(axis)
    return lax.ppermute(array, axis, [(i, (i + distance) % size) for i in range(size)])


def total(*terms):
    result = terms[0].astype(F32)
    for term in terms[1:]:
        result = result + term.astype(F32)
    return result


def section_kernel(first, last, heads, head_dim, meta, token, *refs):
    sources = refs[: RING if first else 1]
    refs = refs[len(sources) :]
    probs, rows, w_out, w_value = refs[:4]
    outs = refs[:-11][-(7 + (1 if last is None else RING)) :]
    token_out, y0, y1, y2, y3, dv_out, seen_out = outs[:7]
    dy, dx, wo_in, wv_in, acc, dvals, weights_in, rows_in, seen, in_sems, out_sems = refs[-11:]
    seq, inner = acc.shape
    width = CHUNKS * inner
    token_out[0] = 0

    @pl.when(meta[0] == 1)
    def _():
        loads = []
        for c in range(CHUNKS):
            if first:
                source = sources[c // 2].at[:, pl.ds((c % 2) * inner, inner)]
            else:
                source = sources[0].at[c]
            loads.append(pltpu.make_async_copy(source, dy.at[c], in_sems.at[c]))
        loads.append(pltpu.make_async_copy(rows, rows_in, in_sems.at[CHUNKS]))
        loads.append(pltpu.make_async_copy(probs.at[meta[1]], weights_in, in_sems.at[CHUNKS + 1]))
        upper, lower = [], []
        for c in range(CHUNKS):
            part = pl.ds(c * inner, inner)
            upper.append(
                pltpu.make_async_copy(w_out.at[:, part], wo_in.at[c], in_sems.at[CHUNKS + 2 + c])
            )
            lower.append(
                pltpu.make_async_copy(w_value.at[part], wv_in.at[c], in_sems.at[2 * CHUNKS + 2 + c])
            )
        loads[CHUNKS].start()
        for c in range(CHUNKS):
            loads[c].start()
            upper[c].start()
        loads[CHUNKS + 1].start()
        loads[CHUNKS].wait()
        for c in range(CHUNKS):
            loads[c].wait()
            upper[c].wait()
            lower[c].start()
            columns = slice(c * inner, (c + 1) * inner)
            part = lax.dot_general(dy[c], wo_in[c], NT, preferred_element_type=F32)
            checks = lax.dot_general(rows_in[:, columns], dy[c], NT, preferred_element_type=F32)
            if c == 0:
                acc[...] = part
                seen[...] = checks
            else:
                acc[...] += part
                seen[...] += checks
        stores = [pltpu.make_async_copy(seen, seen_out, out_sems.at[0])]
        for ahead, kept in enumerate((y0, y1, y2, y3)):
            for half in range(2):
                chunk = half * RING + lax.rem(meta[2] + ahead, RING)
                stores.append(
                    pltpu.make_async_copy(dy.at[chunk], kept.at[half], out_sems.at[len(stores)])
                )
        for store in stores:
            store.start()
        loads[CHUNKS + 1].wait()
        dctx = acc[...].astype(BF16)
        query = lax.broadcasted_iota(jnp.int32, (seq, seq), 0)
        keys = lax.broadcasted_iota(jnp.int32, (seq, seq), 1)
        for head in range(heads):
            weights = jnp.where(query >= keys, weights_in[head].astype(F32), 0.0).astype(BF16)
            columns = slice(head * head_dim, (head + 1) * head_dim)
            part = lax.dot_general(weights, dctx[:, columns], TN, preferred_element_type=F32)
            dvals[:, columns] = part.astype(BF16)
        stores.append(pltpu.make_async_copy(dvals, dv_out, out_sems.at[len(stores)]))
        stores[-1].start()
        for c in range(CHUNKS):
            lower[c].wait()
            part = lax.dot_general(dvals[...], wv_in[c], NT, preferred_element_type=F32)
            dx[c] = (dy[c].astype(F32) + part).astype(BF16)
            stores.append(
                pltpu.make_async_copy(
                    dx.at[c],
                    outs[7].at[c] if last is None else outs[7 + c // 2].at[last, c % 2],
                    out_sems.at[len(stores)],
                )
            )
            stores[-1].start()
        for store in stores:
            store.wait()


def section_step(meta, token, sources, probs, rows, w_out, w_value, kept, after=(), last=None, pieces=None):
    first = len(sources) > 1
    micro, heads, seq, _ = probs.shape
    inner, width = w_out.shape
    in_memory = pl.BlockSpec(memory_space=pltpu.HBM)
    in_smem = pl.BlockSpec(memory_space=pltpu.SMEM)
    operands = (meta, token) + tuple(sources) + (probs, rows, w_out, w_value)
    in_specs = [in_smem, in_smem] + [in_memory] * (len(sources) + 4)
    aliases = {}
    if kept is not None:
        aliases = {len(operands) + i: 1 + i for i in range(len(kept))}
        in_specs += [in_memory] * len(kept)
        operands += tuple(kept)
    if pieces is not None:
        aliases.update({len(operands) + i: 7 + i for i in range(RING)})
        in_specs += [in_memory] * RING
        operands += tuple(pieces)
    in_specs += [pl.BlockSpec(memory_space=pl.ANY)] * len(after)
    operands += tuple(after)
    copies = 1 + 2 * RING + 1 + CHUNKS
    token, *results = pl.pallas_call(
        functools.partial(section_kernel, first, last, heads, inner // heads),
        in_specs=in_specs,
        out_specs=[in_smem] + [in_memory] * (6 + (1 if last is None else RING)),
        out_shape=[
            jax.ShapeDtypeStruct((1,), jnp.int32),
        ]
        + [pltpu.HBM((2, seq, inner), BF16)] * RING
        + [
            pltpu.HBM((seq, inner), BF16),
            pltpu.HBM((rows.shape[0], seq), F32),
        ]
        + (
            [pltpu.HBM((CHUNKS, seq, inner), BF16)]
            if last is None
            else [pltpu.HBM((micro, 2, seq, inner), BF16)] * RING
        ),
        scratch_shapes=[
            pltpu.VMEM((CHUNKS, seq, inner), BF16),
            pltpu.VMEM((CHUNKS, seq, inner), BF16),
            pltpu.VMEM((CHUNKS, inner, inner), BF16),
            pltpu.VMEM((CHUNKS, inner, inner), BF16),
            pltpu.VMEM((seq, inner), F32),
            pltpu.VMEM((seq, inner), BF16),
            pltpu.VMEM((heads, seq, seq), BF16),
            pltpu.VMEM(rows.shape, BF16),
            pltpu.VMEM((rows.shape[0], seq), F32),
            pltpu.SemaphoreType.DMA((3 * CHUNKS + 2,)),
            pltpu.SemaphoreType.DMA((copies,)),
        ],
        input_output_aliases=aliases,
        cost_estimate=pl.CostEstimate(
            flops=4 * seq * width * inner, bytes_accessed=4 * width * inner, transcendentals=0
        ),
        compiler_params=pltpu.CompilerParams(vmem_limit_bytes=VMEM_LIMIT * 1024 * 1024),
    )(*operands)
    return token, results[6:], results[:6]


def gate_kernel(*refs):
    pass


def gated(array, after):
    in_memory = pl.BlockSpec(memory_space=pltpu.HBM)
    return pl.pallas_call(
        gate_kernel,
        in_specs=[in_memory] + [pl.BlockSpec(memory_space=pl.ANY)] * len(after),
        out_specs=in_memory,
        out_shape=pltpu.HBM(array.shape, array.dtype),
        input_output_aliases={0: 0},
        compiler_params=pltpu.CompilerParams(vmem_limit_bytes=1024 * 1024),
    )(array, *after)


def early_kernel(heads, head_dim, meta, token, inputs, probs, rows, w_value, *refs):
    token_out, ctx_out, seen_out, x0, x1, x2, x3 = refs[:7]
    x, cut, wv_in, weights_in, rows_in, ctx, seen, in_sems, out_sems = refs[7:]
    micro, seq, inner = ctx.shape
    width = x.shape[2]
    share = cut.shape[3] // CHUNKS
    token_out[0] = token[0]
    loads = []
    for m in range(micro):
        loads.append(pltpu.make_async_copy(inputs.at[meta[1 + m]], x.at[m], in_sems.at[2 * m]))
        loads.append(
            pltpu.make_async_copy(probs.at[meta[1 + m]], weights_in.at[m], in_sems.at[2 * m + 1])
        )
    loads.append(pltpu.make_async_copy(rows, rows_in, in_sems.at[2 * micro]))
    for c in range(CHUNKS):
        source = w_value.at[pl.ds(c * inner, inner)]
        loads.append(pltpu.make_async_copy(source, wv_in.at[c], in_sems.at[2 * micro + 1 + c]))
    for load in loads:
        load.start()
    loads[2 * micro].wait()
    stores = []
    query = lax.broadcasted_iota(jnp.int32, (seq, seq), 0)
    keys = lax.broadcasted_iota(jnp.int32, (seq, seq), 1)
    for m in range(micro):
        loads[2 * m].wait()
        for part in range(CHUNKS):
            for place in range(RING):
                start = (part * RING + place) * share
                cut[m, place, :, part * share : (part + 1) * share] = x[m, :, start : start + share]
        for ahead, out in enumerate((x0, x1, x2, x3)):
            place = lax.rem(meta[0] + ahead, RING)
            stores.append(
                pltpu.make_async_copy(cut.at[m, place], out.at[m], out_sems.at[len(stores)])
            )
            stores[-1].start()
    for m in range(micro):
        loads[2 * m + 1].wait()
        acc = None
        for c in range(CHUNKS):
            columns = slice(c * inner, (c + 1) * inner)
            block = x[m, :, columns]
            if m == 0:
                loads[2 * micro + 1 + c].wait()
            part = jnp.dot(block, wv_in[c], preferred_element_type=F32)
            checks = lax.dot_general(rows_in[:, columns], block, NT, preferred_element_type=F32)
            acc, checked = (part, checks) if c == 0 else (acc + part, checked + checks)
        seen[m] = checked
        values = acc.astype(BF16)
        for head in range(heads):
            weights = jnp.where(query >= keys, weights_in[m, head].astype(F32), 0.0).astype(BF16)
            columns = slice(head * head_dim, (head + 1) * head_dim)
            part = jnp.dot(weights, values[:, columns], preferred_element_type=F32)
            ctx[m, :, columns] = part.astype(BF16)
    stores.append(pltpu.make_async_copy(ctx, ctx_out, out_sems.at[len(stores)]))
    stores.append(pltpu.make_async_copy(seen, seen_out, out_sems.at[len(stores)]))
    for store in stores[-2:]:
        store.start()
    for store in stores:
        store.wait()


def early_step(meta, token, inputs, probs, rows, w_value):
    micro, seq, width = inputs.shape
    inner = w_value.shape[1]
    heads = probs.shape[1]
    in_memory = pl.BlockSpec(memory_space=pltpu.HBM)
    in_smem = pl.BlockSpec(memory_space=pltpu.SMEM)
    token, ctx, seen, *blocks = pl.pallas_call(
        functools.partial(early_kernel, heads, inner // heads),
        in_specs=[in_smem, in_smem] + [in_memory] * 4,
        out_specs=[in_smem] + [in_memory] * 6,
        out_shape=[
            jax.ShapeDtypeStruct((1,), jnp.int32),
            jax.ShapeDtypeStruct((micro, seq, inner), BF16),
            jax.ShapeDtypeStruct((micro, rows.shape[0], seq), F32),
        ]
        + [pltpu.HBM((micro, seq, width // RING), BF16)] * RING,
        scratch_shapes=[
            pltpu.VMEM((micro, seq, width), BF16),
            pltpu.VMEM((micro, RING, seq, width // RING), BF16),
            pltpu.VMEM((CHUNKS, inner, inner), BF16),
            pltpu.VMEM((micro, heads, seq, seq), BF16),
            pltpu.VMEM(rows.shape, BF16),
            pltpu.VMEM((micro, seq, inner), BF16),
            pltpu.VMEM((micro, rows.shape[0], seq), F32),
            pltpu.SemaphoreType.DMA((2 * micro + 1 + CHUNKS,)),
            pltpu.SemaphoreType.DMA((RING * micro + 2,)),
        ],
        cost_estimate=pl.CostEstimate(
            flops=8 * micro * seq * width * inner,
            bytes_accessed=4 * width * inner,
            transcendentals=0,
        ),
        compiler_params=pltpu.CompilerParams(vmem_limit_bytes=VMEM_LIMIT * 1024 * 1024),
    )(meta, token, inputs, probs, rows, w_value)
    return token, ctx, seen, blocks


def product_kernel(of_value, m, last, meta, *refs):
    left, right, refs = refs[:RING], refs[RING : 2 * RING], refs[2 * RING :]
    before = refs[0] if m else None
    refs = refs[-1:] if last is None else refs[-4:]
    inner = right[0].shape[-1]
    rows = inner // RING
    for half in range(2):
        total = before[half] if m else None
        for k in range(RING):
            if of_value:
                part = left[k][m, :, half * inner : (half + 1) * inner], right[k][...]
            else:
                part = left[k][half], right[k][m]
            part = lax.dot_general(*part, TN, preferred_element_type=F32)
            total = part if total is None else total + part
        if last is None:
            refs[0][half] = total
        else:
            *away2, terms, acc = refs
            acc[...] = total * last
            for ahead in range(RING):
                start = lax.rem(meta[0] + ahead, RING) * rows
                term = acc[pl.ds(pl.multiple_of(start, rows), rows), :].astype(BF16)
                terms[half, ahead] = term
                if ahead == 2:
                    away2[half][...] = term


def products(of_value, m, last, place, left, right, before, after=()):
    inner = right[0].shape[-1]
    rows = inner // RING
    in_vmem = pl.BlockSpec(memory_space=pltpu.VMEM)
    operands = list(left) + list(right) + ([before] if m else [])
    if last is None:
        shapes = [jax.ShapeDtypeStruct((2, inner, inner), F32)]
        scratch = []
    else:
        shapes = [jax.ShapeDtypeStruct((rows, inner), BF16)] * 2
        shapes += [jax.ShapeDtypeStruct((2, RING, rows, inner), BF16)]
        scratch = [pltpu.VMEM((inner, inner), F32)]
    return pl.pallas_call(
        functools.partial(product_kernel, of_value, m, last),
        in_specs=[pl.BlockSpec(memory_space=pltpu.SMEM)]
        + [in_vmem] * len(operands)
        + [pl.BlockSpec(memory_space=pl.ANY)] * len(after),
        out_specs=[in_vmem] * len(shapes),
        out_shape=shapes,
        scratch_shapes=scratch,
        cost_estimate=pl.CostEstimate(
            flops=32 * inner * inner * 160, bytes_accessed=16 * inner * inner, transcendentals=0
        ),
        compiler_params=pltpu.CompilerParams(vmem_limit_bytes=24 * 1024 * 1024),
    )(place[None], *operands, *after)


def second_kernel(terms, up2, down2, up, down):
    up[0] = terms[1, 1]
    up[1] = total(terms[0, 1], up2[...]).astype(BF16)
    down[0] = terms[0, 3]
    down[1] = total(terms[1, 3], down2[...]).astype(BF16)


def third_kernel(meta, terms, up, down, away, kept):
    low = total(terms[0, 0], down[0], up[1])
    high = total(terms[1, 0], up[0], down[1])

    @pl.when(meta[0] == 0)
    def _():
        kept[...] = low
        away[...] = high.astype(BF16)

    @pl.when(meta[0] == 1)
    def _():
        kept[...] = high
        away[...] = low.astype(BF16)


def ring_first(axis, up2, down2, terms):
    _, _, rows, inner = terms.shape
    in_vmem = pl.BlockSpec(memory_space=pltpu.VMEM)
    return pl.pallas_call(
        second_kernel,
        in_specs=[in_vmem] * 3,
        out_specs=[in_vmem] * 2,
        out_shape=[jax.ShapeDtypeStruct((2, rows, inner), BF16)] * 2,
        compiler_params=pltpu.CompilerParams(vmem_limit_bytes=8 * 1024 * 1024),
    )(terms, shifted(up2, axis, 1), shifted(down2, axis, -1))


def arrived(axis, blocks):
    up, down = blocks
    return shifted(up, axis, 1), shifted(down, axis, -1)


def ring_last(up, down, terms):
    _, _, rows, inner = terms.shape
    in_vmem = pl.BlockSpec(memory_space=pltpu.VMEM)
    in_smem = pl.BlockSpec(memory_space=pltpu.SMEM)
    return pl.pallas_call(
        third_kernel,
        in_specs=[in_smem] + [in_vmem] * 3,
        out_specs=[in_vmem] * 2,
        out_shape=[
            jax.ShapeDtypeStruct((rows, inner), BF16),
            jax.ShapeDtypeStruct((rows, inner), F32),
        ],
        compiler_params=pltpu.CompilerParams(vmem_limit_bytes=8 * 1024 * 1024),
    )(lax.axis_index("yh")[None], terms, up, down)


def ring_total(axis, rows):
    rows = rows + shifted(rows, axis, 1)
    return rows + shifted(rows, axis, 2)


def exchanged(blocks, axis):
    return [blocks[0]] + [shifted(blocks[k], axis, d) for k, d in ((1, 1), (2, 2), (3, -1))]


def on_device(stash, attn, w_value, w_out, out_grad, order, check_rows):
    section = lax.axis_index("pipe")
    inputs = stash[0]
    probs = attn[0][:, 0]
    wv = w_value[0]
    wo = w_out[0]
    micro, seq, width = inputs.shape
    inner = wv.shape[1]
    heads = probs.shape[1]
    head_dim = inner // heads
    sections = lax.axis_size("pipe")
    replicas = lax.axis_size("yh") * lax.axis_size("z") * lax.axis_size("x")
    grad_scale = (micro * seq * replicas) ** -0.5
    check_scale = width**-0.5
    highest = lax.Precision.HIGHEST
    n_checks = check_rows.shape[0]
    rows = width // replicas
    z_place, x_place = lax.axis_index("z"), lax.axis_index("x")

    in_hbm = lambda array: pltpu.with_memory_space_constraint(array, pltpu.HBM)
    wo, wv, inputs, probs = in_hbm(wo), in_hbm(wv), in_hbm(inputs), in_hbm(probs)
    check_bf = jnp.pad(check_rows, ((0, 16 - n_checks), (0, 0))).astype(BF16)

    arriving = []
    for m in range(micro):
        own = out_grad[m]
        gathered = [lax.ppermute(own, "pipe", [(s, sections - 1)]) for s in range(sections - 1)]
        arriving.append(tuple(gathered) + (own,))

    token = jnp.zeros((1,), jnp.int32)
    pieces = None
    kept = [None] * micro
    after, y_from, dv_from, early = [], [], [], {}
    for turn in range(sections):
        here = (section == sections - 1 - turn).astype(jnp.int32)
        for m in range(micro):
            meta = jnp.stack([here, order[m], z_place])
            waits = early.get((turn, m), ()) + tuple(after)
            token, sent, kept[m] = section_step(
                meta, token, arriving[m], probs, check_bf, wo, wv, kept[m], waits,
                m if turn == sections - 1 else None, pieces,
            )
            if turn == 0 and m == 0:
                places = jnp.concatenate([x_place[None], order])
                token, context, seen_values, blocks = early_step(
                    places, token, inputs, probs, check_bf, wv
                )
                x_from = exchanged(blocks, "x")
                ctx_from = exchanged([context] * RING, "z")
                early = {
                    (2, 0): (x_from[1], x_from[3]),
                    (2, 1): (x_from[2], ctx_from[1], ctx_from[3]),
                    (3, 1): (ctx_from[2],),
                }
            if turn < sections - 1:
                pair = [(sections - 1 - turn, sections - 2 - turn)]
                arriving[m] = (lax.ppermute(sent[0], "pipe", pair),)
            else:
                pieces = sent
                *y_blocks, dv, _ = kept[m]
                dv_from.append(exchanged([dv] * RING, "x"))
                y_from.append(exchanged(y_blocks, "z"))
                after = dv_from[m][1:]

    checks_v = checks_o = 0.0
    out_sum = value_sum = [None]
    for m in range(micro):
        *_, dv, seen = kept[m]
        checks_v = checks_v + jnp.dot(
            seen_values[m, :n_checks], dv.astype(F32), precision=highest
        )
        checks_o = checks_o + jnp.dot(
            seen[:n_checks], context[m].astype(F32), precision=highest
        )
        last = grad_scale if m == micro - 1 else None
        late = y_from[m][1:] if m else ()
        value_sum = products(True, m, last, z_place, x_from, dv_from[m], value_sum[0], late)
        waits = dv_from[m][1:] if m else ()
        out_sum = products(False, m, last, x_place, y_from[m], ctx_from, out_sum[0], waits)
    value_next = ring_first("z", *value_sum)
    out_next = ring_first("x", *out_sum)
    value_up, value_down = arrived("z", value_next)
    out_up, out_down = arrived("x", out_next)
    value_away, value_kept = ring_last(value_up, value_down, value_sum[2])
    out_away, out_kept = ring_last(out_up, out_down, out_sum[2])
    came = {}
    for s in (2, 3, 1):
        came[s] = lax.ppermute(gated(pieces[s], [value_up]), "pipe", [(0, s)])
    owned = pieces[0]
    for s in (1, 2, 3):
        owned = jnp.where(section == s, came[s], owned)
    owned = owned.transpose(0, 2, 1, 3).reshape(micro, seq, 2 * inner)
    checks = jnp.stack([checks_v, checks_o]) * (grad_scale * check_scale)
    checks = ring_total("x", gated(checks, [value_away]))
    checks = ring_total("z", gated(checks, [came[2]]))
    grad_v = value_kept + shifted(value_away, "yh", 1).astype(F32)
    grad_o = out_kept + shifted(out_away, "yh", 1).astype(F32)
    check_sum = checks + shifted(gated(checks, [came[3]]), "yh", 1)
    return (grad_v[None], grad_o[None], check_sum[None], owned)


def solution(mesh):
    fine = Mesh(mesh.devices.reshape(4, 2, 4, 4), ("pipe",) + REPLICAS)
    return jax.shard_map(
        on_device,
        mesh=fine,
        in_specs=(
            P("pipe", None, REPLICAS, None),
            P("pipe", None, REPLICAS, None, None, None),
            P("pipe", None, None),
            P("pipe", None, None),
            P(None, REPLICAS, "pipe"),
            P(),
            P(),
        ),
        out_specs=(
            P("pipe", REPLICAS, None),
            P("pipe", REPLICAS, None),
            P("pipe", None, None, None),
            P(None, REPLICAS, "pipe"),
        ),
        check_vma=False,
    )
```

```python
import functools

import jax
import jax.numpy as jnp
from jax import lax
from jax.experimental import pallas as pl
from jax.experimental.pallas import tpu as pltpu
from jax.sharding import Mesh
from jax.sharding import PartitionSpec as P

F32 = jnp.float32
BF16 = jnp.bfloat16
NT = (((1,), (1,)), ((), ()))
TN = (((0,), (0,)), ((), ()))
REPLICAS = ("yh", "z", "x")
CHUNKS = 8
RING = 4
VMEM_LIMIT = 34


def shifted(array, axis, distance):
    size = lax.axis_size(axis)
    return lax.ppermute(array, axis, [(i, (i + distance) % size) for i in range(size)])


def total(*terms):
    result = terms[0].astype(F32)
    for term in terms[1:]:
        result = result + term.astype(F32)
    return result


def section_kernel(first, last, heads, head_dim, meta, token, *refs):
    sources = refs[: RING if first else 1]
    refs = refs[len(sources) :]
    probs, rows, w_out, w_value = refs[:4]
    outs = refs[:-11][-(7 + (1 if last is None else RING)) :]
    token_out, y0, y1, y2, y3, dv_out, seen_out = outs[:7]
    dy, dx, wo_in, wv_in, acc, dvals, weights_in, rows_in, seen, in_sems, out_sems = refs[-11:]
    seq, inner = acc.shape
    width = CHUNKS * inner
    token_out[0] = 0

    @pl.when(meta[0] == 1)
    def _():
        loads = []
        for c in range(CHUNKS):
            if first:
                source = sources[c // 2].at[:, pl.ds((c % 2) * inner, inner)]
            else:
                source = sources[0].at[c]
            loads.append(pltpu.make_async_copy(source, dy.at[c], in_sems.at[c]))
        loads.append(pltpu.make_async_copy(rows, rows_in, in_sems.at[CHUNKS]))
        loads.append(pltpu.make_async_copy(probs.at[meta[1]], weights_in, in_sems.at[CHUNKS + 1]))
        upper, lower = [], []
        for c in range(CHUNKS):
            part = pl.ds(c * inner, inner)
            upper.append(
                pltpu.make_async_copy(w_out.at[:, part], wo_in.at[c], in_sems.at[CHUNKS + 2 + c])
            )
            lower.append(
                pltpu.make_async_copy(w_value.at[part], wv_in.at[c], in_sems.at[2 * CHUNKS + 2 + c])
            )
        loads[CHUNKS].start()
        for c in range(CHUNKS):
            loads[c].start()
            upper[c].start()
        loads[CHUNKS + 1].start()
        loads[CHUNKS].wait()
        for c in range(CHUNKS):
            loads[c].wait()
            upper[c].wait()
            lower[c].start()
            columns = slice(c * inner, (c + 1) * inner)
            part = lax.dot_general(dy[c], wo_in[c], NT, preferred_element_type=F32)
            checks = lax.dot_general(rows_in[:, columns], dy[c], NT, preferred_element_type=F32)
            if c == 0:
                acc[...] = part
                seen[...] = checks
            else:
                acc[...] += part
                seen[...] += checks
        stores = [pltpu.make_async_copy(seen, seen_out, out_sems.at[0])]
        for ahead, kept in enumerate((y0, y1, y2, y3)):
            for half in range(2):
                chunk = half * RING + lax.rem(meta[2] + ahead, RING)
                stores.append(
                    pltpu.make_async_copy(dy.at[chunk], kept.at[half], out_sems.at[len(stores)])
                )
        for store in stores:
            store.start()
        loads[CHUNKS + 1].wait()
        dctx = acc[...].astype(BF16)
        query = lax.broadcasted_iota(jnp.int32, (seq, seq), 0)
        keys = lax.broadcasted_iota(jnp.int32, (seq, seq), 1)
        for head in range(heads):
            weights = jnp.where(query >= keys, weights_in[head].astype(F32), 0.0).astype(BF16)
            columns = slice(head * head_dim, (head + 1) * head_dim)
            part = lax.dot_general(weights, dctx[:, columns], TN, preferred_element_type=F32)
            dvals[:, columns] = part.astype(BF16)
        stores.append(pltpu.make_async_copy(dvals, dv_out, out_sems.at[len(stores)]))
        stores[-1].start()
        for c in range(CHUNKS):
            lower[c].wait()
            part = lax.dot_general(dvals[...], wv_in[c], NT, preferred_element_type=F32)
            dx[c] = (dy[c].astype(F32) + part).astype(BF16)
            stores.append(
                pltpu.make_async_copy(
                    dx.at[c],
                    outs[7].at[c] if last is None else outs[7 + c // 2].at[last, c % 2],
                    out_sems.at[len(stores)],
                )
            )
            stores[-1].start()
        for store in stores:
            store.wait()


def section_step(meta, token, sources, probs, rows, w_out, w_value, kept, after=(), last=None, pieces=None):
    first = len(sources) > 1
    micro, heads, seq, _ = probs.shape
    inner, width = w_out.shape
    in_memory = pl.BlockSpec(memory_space=pltpu.HBM)
    in_smem = pl.BlockSpec(memory_space=pltpu.SMEM)
    operands = (meta, token) + tuple(sources) + (probs, rows, w_out, w_value)
    in_specs = [in_smem, in_smem] + [in_memory] * (len(sources) + 4)
    aliases = {}
    if kept is not None:
        aliases = {len(operands) + i: 1 + i for i in range(len(kept))}
        in_specs += [in_memory] * len(kept)
        operands += tuple(kept)
    if pieces is not None:
        aliases.update({len(operands) + i: 7 + i for i in range(RING)})
        in_specs += [in_memory] * RING
        operands += tuple(pieces)
    in_specs += [pl.BlockSpec(memory_space=pl.ANY)] * len(after)
    operands += tuple(after)
    copies = 1 + 2 * RING + 1 + CHUNKS
    token, *results = pl.pallas_call(
        functools.partial(section_kernel, first, last, heads, inner // heads),
        in_specs=in_specs,
        out_specs=[in_smem] + [in_memory] * (6 + (1 if last is None else RING)),
        out_shape=[
            jax.ShapeDtypeStruct((1,), jnp.int32),
        ]
        + [pltpu.HBM((2, seq, inner), BF16)] * RING
        + [
            pltpu.HBM((seq, inner), BF16),
            pltpu.HBM((rows.shape[0], seq), F32),
        ]
        + (
            [pltpu.HBM((CHUNKS, seq, inner), BF16)]
            if last is None
            else [pltpu.HBM((micro, 2, seq, inner), BF16)] * RING
        ),
        scratch_shapes=[
            pltpu.VMEM((CHUNKS, seq, inner), BF16),
            pltpu.VMEM((CHUNKS, seq, inner), BF16),
            pltpu.VMEM((CHUNKS, inner, inner), BF16),
            pltpu.VMEM((CHUNKS, inner, inner), BF16),
            pltpu.VMEM((seq, inner), F32),
            pltpu.VMEM((seq, inner), BF16),
            pltpu.VMEM((heads, seq, seq), BF16),
            pltpu.VMEM(rows.shape, BF16),
            pltpu.VMEM((rows.shape[0], seq), F32),
            pltpu.SemaphoreType.DMA((3 * CHUNKS + 2,)),
            pltpu.SemaphoreType.DMA((copies,)),
        ],
        input_output_aliases=aliases,
        cost_estimate=pl.CostEstimate(
            flops=4 * seq * width * inner, bytes_accessed=4 * width * inner, transcendentals=0
        ),
        compiler_params=pltpu.CompilerParams(vmem_limit_bytes=VMEM_LIMIT * 1024 * 1024),
    )(*operands)
    return token, results[6:], results[:6]


def gate_kernel(*refs):
    pass


def gated(array, after):
    in_memory = pl.BlockSpec(memory_space=pltpu.HBM)
    return pl.pallas_call(
        gate_kernel,
        in_specs=[in_memory] + [pl.BlockSpec(memory_space=pl.ANY)] * len(after),
        out_specs=in_memory,
        out_shape=pltpu.HBM(array.shape, array.dtype),
        input_output_aliases={0: 0},
        compiler_params=pltpu.CompilerParams(vmem_limit_bytes=1024 * 1024),
    )(array, *after)


def early_kernel(heads, head_dim, meta, token, inputs, probs, rows, w_value, *refs):
    token_out, ctx_out, seen_out, x0, x1, x2, x3 = refs[:7]
    x, cut, wv_in, weights_in, rows_in, ctx, seen, in_sems, out_sems = refs[7:]
    micro, seq, inner = ctx.shape
    width = x.shape[2]
    share = cut.shape[3] // CHUNKS
    token_out[0] = token[0]
    loads = []
    for m in range(micro):
        loads.append(pltpu.make_async_copy(inputs.at[meta[1 + m]], x.at[m], in_sems.at[2 * m]))
        loads.append(
            pltpu.make_async_copy(probs.at[meta[1 + m]], weights_in.at[m], in_sems.at[2 * m + 1])
        )
    loads.append(pltpu.make_async_copy(rows, rows_in, in_sems.at[2 * micro]))
    for c in range(CHUNKS):
        source = w_value.at[pl.ds(c * inner, inner)]
        loads.append(pltpu.make_async_copy(source, wv_in.at[c], in_sems.at[2 * micro + 1 + c]))
    for load in loads:
        load.start()
    loads[2 * micro].wait()
    stores = []
    query = lax.broadcasted_iota(jnp.int32, (seq, seq), 0)
    keys = lax.broadcasted_iota(jnp.int32, (seq, seq), 1)
    for m in range(micro):
        loads[2 * m].wait()
        for part in range(CHUNKS):
            for place in range(RING):
                start = (part * RING + place) * share
                cut[m, place, :, part * share : (part + 1) * share] = x[m, :, start : start + share]
        for ahead, out in enumerate((x0, x1, x2, x3)):
            place = lax.rem(meta[0] + ahead, RING)
            stores.append(
                pltpu.make_async_copy(cut.at[m, place], out.at[m], out_sems.at[len(stores)])
            )
            stores[-1].start()
    for m in range(micro):
        loads[2 * m + 1].wait()
        acc = None
        for c in range(CHUNKS):
            columns = slice(c * inner, (c + 1) * inner)
            block = x[m, :, columns]
            if m == 0:
                loads[2 * micro + 1 + c].wait()
            part = jnp.dot(block, wv_in[c], preferred_element_type=F32)
            checks = lax.dot_general(rows_in[:, columns], block, NT, preferred_element_type=F32)
            acc, checked = (part, checks) if c == 0 else (acc + part, checked + checks)
        seen[m] = checked
        values = acc.astype(BF16)
        for head in range(heads):
            weights = jnp.where(query >= keys, weights_in[m, head].astype(F32), 0.0).astype(BF16)
            columns = slice(head * head_dim, (head + 1) * head_dim)
            part = jnp.dot(weights, values[:, columns], preferred_element_type=F32)
            ctx[m, :, columns] = part.astype(BF16)
    stores.append(pltpu.make_async_copy(ctx, ctx_out, out_sems.at[len(stores)]))
    stores.append(pltpu.make_async_copy(seen, seen_out, out_sems.at[len(stores)]))
    for store in stores[-2:]:
        store.start()
    for store in stores:
        store.wait()


def early_step(meta, token, inputs, probs, rows, w_value):
    micro, seq, width = inputs.shape
    inner = w_value.shape[1]
    heads = probs.shape[1]
    in_memory = pl.BlockSpec(memory_space=pltpu.HBM)
    in_smem = pl.BlockSpec(memory_space=pltpu.SMEM)
    token, ctx, seen, *blocks = pl.pallas_call(
        functools.partial(early_kernel, heads, inner // heads),
        in_specs=[in_smem, in_smem] + [in_memory] * 4,
        out_specs=[in_smem] + [in_memory] * 6,
        out_shape=[
            jax.ShapeDtypeStruct((1,), jnp.int32),
            jax.ShapeDtypeStruct((micro, seq, inner), BF16),
            jax.ShapeDtypeStruct((micro, rows.shape[0], seq), F32),
        ]
        + [pltpu.HBM((micro, seq, width // RING), BF16)] * RING,
        scratch_shapes=[
            pltpu.VMEM((micro, seq, width), BF16),
            pltpu.VMEM((micro, RING, seq, width // RING), BF16),
            pltpu.VMEM((CHUNKS, inner, inner), BF16),
            pltpu.VMEM((micro, heads, seq, seq), BF16),
            pltpu.VMEM(rows.shape, BF16),
            pltpu.VMEM((micro, seq, inner), BF16),
            pltpu.VMEM((micro, rows.shape[0], seq), F32),
            pltpu.SemaphoreType.DMA((2 * micro + 1 + CHUNKS,)),
            pltpu.SemaphoreType.DMA((RING * micro + 2,)),
        ],
        cost_estimate=pl.CostEstimate(
            flops=8 * micro * seq * width * inner,
            bytes_accessed=4 * width * inner,
            transcendentals=0,
        ),
        compiler_params=pltpu.CompilerParams(vmem_limit_bytes=VMEM_LIMIT * 1024 * 1024),
    )(meta, token, inputs, probs, rows, w_value)
    return token, ctx, seen, blocks


def product_kernel(of_value, m, last, meta, *refs):
    left, right, refs = refs[:RING], refs[RING : 2 * RING], refs[2 * RING :]
    before = refs[0] if m else None
    refs = refs[-1:] if last is None else refs[-4:]
    inner = right[0].shape[-1]
    rows = inner // RING
    for half in range(2):
        total = before[half] if m else None
        for k in range(RING):
            if of_value:
                part = left[k][m, :, half * inner : (half + 1) * inner], right[k][...]
            else:
                part = left[k][half], right[k][m]
            part = lax.dot_general(*part, TN, preferred_element_type=F32)
            total = part if total is None else total + part
        if last is None:
            refs[0][half] = total
        else:
            *away2, terms, acc = refs
            acc[...] = total * last
            for ahead in range(RING):
                start = lax.rem(meta[0] + ahead, RING) * rows
                term = acc[pl.ds(pl.multiple_of(start, rows), rows), :].astype(BF16)
                terms[half, ahead] = term
                if ahead == 2:
                    away2[half][...] = term


def products(of_value, m, last, place, left, right, before, after=()):
    inner = right[0].shape[-1]
    rows = inner // RING
    in_vmem = pl.BlockSpec(memory_space=pltpu.VMEM)
    operands = list(left) + list(right) + ([before] if m else [])
    if last is None:
        shapes = [jax.ShapeDtypeStruct((2, inner, inner), F32)]
        scratch = []
    else:
        shapes = [jax.ShapeDtypeStruct((rows, inner), BF16)] * 2
        shapes += [jax.ShapeDtypeStruct((2, RING, rows, inner), BF16)]
        scratch = [pltpu.VMEM((inner, inner), F32)]
    return pl.pallas_call(
        functools.partial(product_kernel, of_value, m, last),
        in_specs=[pl.BlockSpec(memory_space=pltpu.SMEM)]
        + [in_vmem] * len(operands)
        + [pl.BlockSpec(memory_space=pl.ANY)] * len(after),
        out_specs=[in_vmem] * len(shapes),
        out_shape=shapes,
        scratch_shapes=scratch,
        cost_estimate=pl.CostEstimate(
            flops=32 * inner * inner * 160, bytes_accessed=16 * inner * inner, transcendentals=0
        ),
        compiler_params=pltpu.CompilerParams(vmem_limit_bytes=24 * 1024 * 1024),
    )(place[None], *operands, *after)


def second_kernel(terms, up2, down2, up, down):
    up[0] = terms[1, 1]
    up[1] = total(terms[0, 1], up2[...]).astype(BF16)
    down[0] = terms[0, 3]
    down[1] = total(terms[1, 3], down2[...]).astype(BF16)


def third_kernel(meta, terms, up, down, away, kept):
    low = total(terms[0, 0], down[0], up[1])
    high = total(terms[1, 0], up[0], down[1])

    @pl.when(meta[0] == 0)
    def _():
        kept[...] = low
        away[...] = high.astype(BF16)

    @pl.when(meta[0] == 1)
    def _():
        kept[...] = high
        away[...] = low.astype(BF16)


def ring_first(axis, up2, down2, terms):
    _, _, rows, inner = terms.shape
    in_vmem = pl.BlockSpec(memory_space=pltpu.VMEM)
    return pl.pallas_call(
        second_kernel,
        in_specs=[in_vmem] * 3,
        out_specs=[in_vmem] * 2,
        out_shape=[jax.ShapeDtypeStruct((2, rows, inner), BF16)] * 2,
        compiler_params=pltpu.CompilerParams(vmem_limit_bytes=8 * 1024 * 1024),
    )(terms, shifted(up2, axis, 1), shifted(down2, axis, -1))


def arrived(axis, blocks):
    up, down = blocks
    return shifted(up, axis, 1), shifted(down, axis, -1)


def ring_last(up, down, terms):
    _, _, rows, inner = terms.shape
    in_vmem = pl.BlockSpec(memory_space=pltpu.VMEM)
    in_smem = pl.BlockSpec(memory_space=pltpu.SMEM)
    return pl.pallas_call(
        third_kernel,
        in_specs=[in_smem] + [in_vmem] * 3,
        out_specs=[in_vmem] * 2,
        out_shape=[
            jax.ShapeDtypeStruct((rows, inner), BF16),
            jax.ShapeDtypeStruct((rows, inner), F32),
        ],
        compiler_params=pltpu.CompilerParams(vmem_limit_bytes=8 * 1024 * 1024),
    )(lax.axis_index("yh")[None], terms, up, down)


def ring_total(rows):
    for axis in ("x", "z"):
        rows = rows + shifted(rows, axis, 1)
        rows = rows + shifted(rows, axis, 2)
    return rows


def exchanged(blocks, axis):
    return [blocks[0]] + [shifted(blocks[k], axis, d) for k, d in ((1, 1), (2, 2), (3, -1))]


def on_device(stash, attn, w_value, w_out, out_grad, order, check_rows):
    section = lax.axis_index("pipe")
    inputs = stash[0]
    probs = attn[0][:, 0]
    wv = w_value[0]
    wo = w_out[0]
    micro, seq, width = inputs.shape
    inner = wv.shape[1]
    heads = probs.shape[1]
    head_dim = inner // heads
    sections = lax.axis_size("pipe")
    replicas = lax.axis_size("yh") * lax.axis_size("z") * lax.axis_size("x")
    grad_scale = (micro * seq * replicas) ** -0.5
    check_scale = width**-0.5
    highest = lax.Precision.HIGHEST
    n_checks = check_rows.shape[0]
    rows = width // replicas
    z_place, x_place = lax.axis_index("z"), lax.axis_index("x")

    in_hbm = lambda array: pltpu.with_memory_space_constraint(array, pltpu.HBM)
    wo, wv, inputs, probs = in_hbm(wo), in_hbm(wv), in_hbm(inputs), in_hbm(probs)
    check_bf = jnp.pad(check_rows, ((0, 16 - n_checks), (0, 0))).astype(BF16)

    arriving = []
    for m in range(micro):
        own = out_grad[m]
        gathered = [lax.ppermute(own, "pipe", [(s, sections - 1)]) for s in range(sections - 1)]
        arriving.append(tuple(gathered) + (own,))

    token = jnp.zeros((1,), jnp.int32)
    pieces = None
    kept = [None] * micro
    after, y_from, dv_from, early = [], [], [], {}
    for turn in range(sections):
        here = (section == sections - 1 - turn).astype(jnp.int32)
        for m in range(micro):
            meta = jnp.stack([here, order[m], z_place])
            waits = early.get((turn, m), ()) + tuple(after)
            token, sent, kept[m] = section_step(
                meta, token, arriving[m], probs, check_bf, wo, wv, kept[m], waits,
                m if turn == sections - 1 else None, pieces,
            )
            if turn == 0 and m == 0:
                places = jnp.concatenate([x_place[None], order])
                token, context, seen_values, blocks = early_step(
                    places, token, inputs, probs, check_bf, wv
                )
                x_from = exchanged(blocks, "x")
                ctx_from = exchanged([context] * RING, "z")
                early = {
                    (2, 0): (x_from[1], x_from[3]),
                    (2, 1): (x_from[2], ctx_from[1], ctx_from[3]),
                    (3, 1): (ctx_from[2],),
                }
            if turn < sections - 1:
                pair = [(sections - 1 - turn, sections - 2 - turn)]
                arriving[m] = (lax.ppermute(sent[0], "pipe", pair),)
            else:
                pieces = sent
                *y_blocks, dv, _ = kept[m]
                dv_from.append(exchanged([dv] * RING, "x"))
                y_from.append(exchanged(y_blocks, "z"))
                after = dv_from[m][1:]

    checks_v = checks_o = 0.0
    out_sum = value_sum = [None]
    for m in range(micro):
        *_, dv, seen = kept[m]
        checks_v = checks_v + jnp.dot(
            seen_values[m, :n_checks], dv.astype(F32), precision=highest
        )
        checks_o = checks_o + jnp.dot(
            seen[:n_checks], context[m].astype(F32), precision=highest
        )
        last = grad_scale if m == micro - 1 else None
        value_sum = products(True, m, last, z_place, x_from, dv_from[m], value_sum[0])
        waits = dv_from[m][1:] if m else ()
        out_sum = products(False, m, last, x_place, y_from[m], ctx_from, out_sum[0], waits)
    value_next = ring_first("z", *value_sum)
    out_next = ring_first("x", *out_sum)
    value_up, value_down = arrived("z", value_next)
    out_up, out_down = arrived("x", out_next)
    value_away, value_kept = ring_last(value_up, value_down, value_sum[2])
    out_away, out_kept = ring_last(out_up, out_down, out_sum[2])
    came = {}
    for s in (2, 3, 1):
        came[s] = lax.ppermute(gated(pieces[s], [value_up]), "pipe", [(0, s)])
    owned = pieces[0]
    for s in (1, 2, 3):
        owned = jnp.where(section == s, came[s], owned)
    owned = owned.transpose(0, 2, 1, 3).reshape(micro, seq, 2 * inner)
    checks = jnp.stack([checks_v, checks_o]) * (grad_scale * check_scale)
    checks = ring_total(gated(checks, [value_away, out_next[0]]))
    grad_v = value_kept + shifted(value_away, "yh", 1).astype(F32)
    grad_o = out_kept + shifted(out_away, "yh", 1).astype(F32)
    check_sum = checks + shifted(checks, "yh", 1)
    return (grad_v[None], grad_o[None], check_sum[None], owned)


def solution(mesh):
    fine = Mesh(mesh.devices.reshape(4, 2, 4, 4), ("pipe",) + REPLICAS)
    return jax.shard_map(
        on_device,
        mesh=fine,
        in_specs=(
            P("pipe", None, REPLICAS, None),
            P("pipe", None, REPLICAS, None, None, None),
            P("pipe", None, None),
            P("pipe", None, None),
            P(None, REPLICAS, "pipe"),
            P(),
            P(),
        ),
        out_specs=(
            P("pipe", REPLICAS, None),
            P("pipe", REPLICAS, None),
            P("pipe", None, None, None),
            P(None, REPLICAS, "pipe"),
        ),
        check_vma=False,
    )
```

```python
import functools

import jax
import jax.numpy as jnp
from jax import lax
from jax.experimental import pallas as pl
from jax.experimental.pallas import tpu as pltpu
from jax.sharding import Mesh
from jax.sharding import PartitionSpec as P

F32 = jnp.float32
BF16 = jnp.bfloat16
NT = (((1,), (1,)), ((), ()))
TN = (((0,), (0,)), ((), ()))
REPLICAS = ("yh", "z", "x")
CHUNKS = 8
RING = 4
VMEM_LIMIT = 34


def shifted(array, axis, distance):
    size = lax.axis_size(axis)
    return lax.ppermute(array, axis, [(i, (i + distance) % size) for i in range(size)])


def total(*terms):
    result = terms[0].astype(F32)
    for term in terms[1:]:
        result = result + term.astype(F32)
    return result


def section_kernel(first, last, heads, head_dim, meta, token, *refs):
    sources = refs[: RING if first else 1]
    refs = refs[len(sources) :]
    probs, rows, w_out, w_value = refs[:4]
    outs = refs[:-11][-(7 + (1 if last is None else RING)) :]
    token_out, y0, y1, y2, y3, dv_out, seen_out = outs[:7]
    dy, dx, wo_in, wv_in, acc, dvals, weights_in, rows_in, seen, in_sems, out_sems = refs[-11:]
    seq, inner = acc.shape
    width = CHUNKS * inner
    token_out[0] = 0

    @pl.when(meta[0] == 1)
    def _():
        loads = []
        for c in range(CHUNKS):
            if first:
                source = sources[c // 2].at[:, pl.ds((c % 2) * inner, inner)]
            else:
                source = sources[0].at[c]
            loads.append(pltpu.make_async_copy(source, dy.at[c], in_sems.at[c]))
        loads.append(pltpu.make_async_copy(rows, rows_in, in_sems.at[CHUNKS]))
        loads.append(pltpu.make_async_copy(probs.at[meta[1]], weights_in, in_sems.at[CHUNKS + 1]))
        upper, lower = [], []
        for c in range(CHUNKS):
            part = pl.ds(c * inner, inner)
            upper.append(
                pltpu.make_async_copy(w_out.at[:, part], wo_in.at[c], in_sems.at[CHUNKS + 2 + c])
            )
            lower.append(
                pltpu.make_async_copy(w_value.at[part], wv_in.at[c], in_sems.at[2 * CHUNKS + 2 + c])
            )
        loads[CHUNKS].start()
        for c in range(CHUNKS):
            loads[c].start()
            upper[c].start()
        loads[CHUNKS + 1].start()
        loads[CHUNKS].wait()
        for c in range(CHUNKS):
            loads[c].wait()
            upper[c].wait()
            lower[c].start()
            columns = slice(c * inner, (c + 1) * inner)
            part = lax.dot_general(dy[c], wo_in[c], NT, preferred_element_type=F32)
            checks = lax.dot_general(rows_in[:, columns], dy[c], NT, preferred_element_type=F32)
            if c == 0:
                acc[...] = part
                seen[...] = checks
            else:
                acc[...] += part
                seen[...] += checks
        stores = [pltpu.make_async_copy(seen, seen_out, out_sems.at[0])]
        for ahead, kept in enumerate((y0, y1, y2, y3)):
            for half in range(2):
                chunk = half * RING + lax.rem(meta[2] + ahead, RING)
                stores.append(
                    pltpu.make_async_copy(dy.at[chunk], kept.at[half], out_sems.at[len(stores)])
                )
        for store in stores:
            store.start()
        loads[CHUNKS + 1].wait()
        dctx = acc[...].astype(BF16)
        query = lax.broadcasted_iota(jnp.int32, (seq, seq), 0)
        keys = lax.broadcasted_iota(jnp.int32, (seq, seq), 1)
        for head in range(heads):
            weights = jnp.where(query >= keys, weights_in[head].astype(F32), 0.0).astype(BF16)
            columns = slice(head * head_dim, (head + 1) * head_dim)
            part = lax.dot_general(weights, dctx[:, columns], TN, preferred_element_type=F32)
            dvals[:, columns] = part.astype(BF16)
        stores.append(pltpu.make_async_copy(dvals, dv_out, out_sems.at[len(stores)]))
        stores[-1].start()
        for c in range(CHUNKS):
            lower[c].wait()
            part = lax.dot_general(dvals[...], wv_in[c], NT, preferred_element_type=F32)
            dx[c] = (dy[c].astype(F32) + part).astype(BF16)
            stores.append(
                pltpu.make_async_copy(
                    dx.at[c],
                    outs[7].at[c] if last is None else outs[7 + c // 2].at[last, c % 2],
                    out_sems.at[len(stores)],
                )
            )
            stores[-1].start()
        for store in stores:
            store.wait()


def section_step(meta, token, sources, probs, rows, w_out, w_value, kept, after=(), last=None, pieces=None):
    first = len(sources) > 1
    micro, heads, seq, _ = probs.shape
    inner, width = w_out.shape
    in_memory = pl.BlockSpec(memory_space=pltpu.HBM)
    in_smem = pl.BlockSpec(memory_space=pltpu.SMEM)
    operands = (meta, token) + tuple(sources) + (probs, rows, w_out, w_value)
    in_specs = [in_smem, in_smem] + [in_memory] * (len(sources) + 4)
    aliases = {}
    if kept is not None:
        aliases = {len(operands) + i: 1 + i for i in range(len(kept))}
        in_specs += [in_memory] * len(kept)
        operands += tuple(kept)
    if pieces is not None:
        aliases.update({len(operands) + i: 7 + i for i in range(RING)})
        in_specs += [in_memory] * RING
        operands += tuple(pieces)
    in_specs += [pl.BlockSpec(memory_space=pl.ANY)] * len(after)
    operands += tuple(after)
    copies = 1 + 2 * RING + 1 + CHUNKS
    token, *results = pl.pallas_call(
        functools.partial(section_kernel, first, last, heads, inner // heads),
        in_specs=in_specs,
        out_specs=[in_smem] + [in_memory] * (6 + (1 if last is None else RING)),
        out_shape=[
            jax.ShapeDtypeStruct((1,), jnp.int32),
        ]
        + [pltpu.HBM((2, seq, inner), BF16)] * RING
        + [
            pltpu.HBM((seq, inner), BF16),
            pltpu.HBM((rows.shape[0], seq), F32),
        ]
        + (
            [pltpu.HBM((CHUNKS, seq, inner), BF16)]
            if last is None
            else [pltpu.HBM((micro, 2, seq, inner), BF16)] * RING
        ),
        scratch_shapes=[
            pltpu.VMEM((CHUNKS, seq, inner), BF16),
            pltpu.VMEM((CHUNKS, seq, inner), BF16),
            pltpu.VMEM((CHUNKS, inner, inner), BF16),
            pltpu.VMEM((CHUNKS, inner, inner), BF16),
            pltpu.VMEM((seq, inner), F32),
            pltpu.VMEM((seq, inner), BF16),
            pltpu.VMEM((heads, seq, seq), BF16),
            pltpu.VMEM(rows.shape, BF16),
            pltpu.VMEM((rows.shape[0], seq), F32),
            pltpu.SemaphoreType.DMA((3 * CHUNKS + 2,)),
            pltpu.SemaphoreType.DMA((copies,)),
        ],
        input_output_aliases=aliases,
        cost_estimate=pl.CostEstimate(
            flops=4 * seq * width * inner, bytes_accessed=4 * width * inner, transcendentals=0
        ),
        compiler_params=pltpu.CompilerParams(vmem_limit_bytes=VMEM_LIMIT * 1024 * 1024),
    )(*operands)
    return token, results[6:], results[:6]


def gate_kernel(*refs):
    pass


def gated(array, after):
    in_memory = pl.BlockSpec(memory_space=pltpu.HBM)
    return pl.pallas_call(
        gate_kernel,
        in_specs=[in_memory] + [pl.BlockSpec(memory_space=pl.ANY)] * len(after),
        out_specs=in_memory,
        out_shape=pltpu.HBM(array.shape, array.dtype),
        input_output_aliases={0: 0},
        compiler_params=pltpu.CompilerParams(vmem_limit_bytes=1024 * 1024),
    )(array, *after)


def early_kernel(heads, head_dim, meta, token, inputs, probs, rows, w_value, *refs):
    token_out, ctx_out, seen_out, x0, x1, x2, x3 = refs[:7]
    x, cut, wv_in, weights_in, rows_in, ctx, seen, in_sems, out_sems = refs[7:]
    micro, seq, inner = ctx.shape
    width = x.shape[2]
    share = cut.shape[3] // CHUNKS
    token_out[0] = token[0]
    loads = []
    for m in range(micro):
        loads.append(pltpu.make_async_copy(inputs.at[meta[1 + m]], x.at[m], in_sems.at[2 * m]))
        loads.append(
            pltpu.make_async_copy(probs.at[meta[1 + m]], weights_in.at[m], in_sems.at[2 * m + 1])
        )
    loads.append(pltpu.make_async_copy(rows, rows_in, in_sems.at[2 * micro]))
    for c in range(CHUNKS):
        source = w_value.at[pl.ds(c * inner, inner)]
        loads.append(pltpu.make_async_copy(source, wv_in.at[c], in_sems.at[2 * micro + 1 + c]))
    for load in loads:
        load.start()
    loads[2 * micro].wait()
    stores = []
    query = lax.broadcasted_iota(jnp.int32, (seq, seq), 0)
    keys = lax.broadcasted_iota(jnp.int32, (seq, seq), 1)
    for m in range(micro):
        loads[2 * m].wait()
        for part in range(CHUNKS):
            for place in range(RING):
                start = (part * RING + place) * share
                cut[m, place, :, part * share : (part + 1) * share] = x[m, :, start : start + share]
        for ahead, out in enumerate((x0, x1, x2, x3)):
            place = lax.rem(meta[0] + ahead, RING)
            stores.append(
                pltpu.make_async_copy(cut.at[m, place], out.at[m], out_sems.at[len(stores)])
            )
            stores[-1].start()
    for m in range(micro):
        loads[2 * m + 1].wait()
        acc = None
        for c in range(CHUNKS):
            columns = slice(c * inner, (c + 1) * inner)
            block = x[m, :, columns]
            if m == 0:
                loads[2 * micro + 1 + c].wait()
            part = jnp.dot(block, wv_in[c], preferred_element_type=F32)
            checks = lax.dot_general(rows_in[:, columns], block, NT, preferred_element_type=F32)
            acc, checked = (part, checks) if c == 0 else (acc + part, checked + checks)
        seen[m] = checked
        values = acc.astype(BF16)
        for head in range(heads):
            weights = jnp.where(query >= keys, weights_in[m, head].astype(F32), 0.0).astype(BF16)
            columns = slice(head * head_dim, (head + 1) * head_dim)
            part = jnp.dot(weights, values[:, columns], preferred_element_type=F32)
            ctx[m, :, columns] = part.astype(BF16)
    stores.append(pltpu.make_async_copy(ctx, ctx_out, out_sems.at[len(stores)]))
    stores.append(pltpu.make_async_copy(seen, seen_out, out_sems.at[len(stores)]))
    for store in stores[-2:]:
        store.start()
    for store in stores:
        store.wait()


def early_step(meta, token, inputs, probs, rows, w_value):
    micro, seq, width = inputs.shape
    inner = w_value.shape[1]
    heads = probs.shape[1]
    in_memory = pl.BlockSpec(memory_space=pltpu.HBM)
    in_smem = pl.BlockSpec(memory_space=pltpu.SMEM)
    token, ctx, seen, *blocks = pl.pallas_call(
        functools.partial(early_kernel, heads, inner // heads),
        in_specs=[in_smem, in_smem] + [in_memory] * 4,
        out_specs=[in_smem] + [in_memory] * 6,
        out_shape=[
            jax.ShapeDtypeStruct((1,), jnp.int32),
            jax.ShapeDtypeStruct((micro, seq, inner), BF16),
            jax.ShapeDtypeStruct((micro, rows.shape[0], seq), F32),
        ]
        + [pltpu.HBM((micro, seq, width // RING), BF16)] * RING,
        scratch_shapes=[
            pltpu.VMEM((micro, seq, width), BF16),
            pltpu.VMEM((micro, RING, seq, width // RING), BF16),
            pltpu.VMEM((CHUNKS, inner, inner), BF16),
            pltpu.VMEM((micro, heads, seq, seq), BF16),
            pltpu.VMEM(rows.shape, BF16),
            pltpu.VMEM((micro, seq, inner), BF16),
            pltpu.VMEM((micro, rows.shape[0], seq), F32),
            pltpu.SemaphoreType.DMA((2 * micro + 1 + CHUNKS,)),
            pltpu.SemaphoreType.DMA((RING * micro + 2,)),
        ],
        cost_estimate=pl.CostEstimate(
            flops=8 * micro * seq * width * inner,
            bytes_accessed=4 * width * inner,
            transcendentals=0,
        ),
        compiler_params=pltpu.CompilerParams(vmem_limit_bytes=VMEM_LIMIT * 1024 * 1024),
    )(meta, token, inputs, probs, rows, w_value)
    return token, ctx, seen, blocks


def product_kernel(of_value, m, last, meta, *refs):
    left, right, refs = refs[:RING], refs[RING : 2 * RING], refs[2 * RING :]
    before = refs[0] if m else None
    refs = refs[-1:] if last is None else refs[-4:]
    inner = right[0].shape[-1]
    rows = inner // RING
    for half in range(2):
        total = before[half] if m else None
        for k in range(RING):
            if of_value:
                part = left[k][m, :, half * inner : (half + 1) * inner], right[k][...]
            else:
                part = left[k][half], right[k][m]
            part = lax.dot_general(*part, TN, preferred_element_type=F32)
            total = part if total is None else total + part
        if last is None:
            refs[0][half] = total
        else:
            *away2, terms, acc = refs
            acc[...] = total * last
            for ahead in range(RING):
                start = lax.rem(meta[0] + ahead, RING) * rows
                term = acc[pl.ds(pl.multiple_of(start, rows), rows), :].astype(BF16)
                terms[half, ahead] = term
                if ahead == 2:
                    away2[half][...] = term


def products(of_value, m, last, place, left, right, before, after=()):
    inner = right[0].shape[-1]
    rows = inner // RING
    in_vmem = pl.BlockSpec(memory_space=pltpu.VMEM)
    operands = list(left) + list(right) + ([before] if m else [])
    if last is None:
        shapes = [jax.ShapeDtypeStruct((2, inner, inner), F32)]
        scratch = []
    else:
        shapes = [jax.ShapeDtypeStruct((rows, inner), BF16)] * 2
        shapes += [jax.ShapeDtypeStruct((2, RING, rows, inner), BF16)]
        scratch = [pltpu.VMEM((inner, inner), F32)]
    return pl.pallas_call(
        functools.partial(product_kernel, of_value, m, last),
        in_specs=[pl.BlockSpec(memory_space=pltpu.SMEM)]
        + [in_vmem] * len(operands)
        + [pl.BlockSpec(memory_space=pl.ANY)] * len(after),
        out_specs=[in_vmem] * len(shapes),
        out_shape=shapes,
        scratch_shapes=scratch,
        cost_estimate=pl.CostEstimate(
            flops=32 * inner * inner * 160, bytes_accessed=16 * inner * inner, transcendentals=0
        ),
        compiler_params=pltpu.CompilerParams(vmem_limit_bytes=24 * 1024 * 1024),
    )(place[None], *operands, *after)


def second_kernel(terms, up2, down2, up, down):
    up[0] = terms[1, 1]
    up[1] = total(terms[0, 1], up2[...]).astype(BF16)
    down[0] = terms[0, 3]
    down[1] = total(terms[1, 3], down2[...]).astype(BF16)


def third_kernel(meta, terms, up, down, *refs):
    away, kept = refs[-2:]
    low = total(terms[0, 0], down[0], up[1])
    high = total(terms[1, 0], up[0], down[1])

    @pl.when(meta[0] == 0)
    def _():
        kept[...] = low
        away[...] = high.astype(BF16)

    @pl.when(meta[0] == 1)
    def _():
        kept[...] = high
        away[...] = low.astype(BF16)


def ring_first(axis, up2, down2, terms):
    _, _, rows, inner = terms.shape
    in_vmem = pl.BlockSpec(memory_space=pltpu.VMEM)
    return pl.pallas_call(
        second_kernel,
        in_specs=[in_vmem] * 3,
        out_specs=[in_vmem] * 2,
        out_shape=[jax.ShapeDtypeStruct((2, rows, inner), BF16)] * 2,
        compiler_params=pltpu.CompilerParams(vmem_limit_bytes=8 * 1024 * 1024),
    )(terms, shifted(up2, axis, 1), shifted(down2, axis, -1))


def ring_last(axis, up, down, terms, after):
    _, _, rows, inner = terms.shape
    in_vmem = pl.BlockSpec(memory_space=pltpu.VMEM)
    in_smem = pl.BlockSpec(memory_space=pltpu.SMEM)
    return pl.pallas_call(
        third_kernel,
        in_specs=[in_smem] + [in_vmem] * 3 + [pl.BlockSpec(memory_space=pl.ANY)] * len(after),
        out_specs=[in_vmem] * 2,
        out_shape=[
            jax.ShapeDtypeStruct((rows, inner), BF16),
            jax.ShapeDtypeStruct((rows, inner), F32),
        ],
        compiler_params=pltpu.CompilerParams(vmem_limit_bytes=8 * 1024 * 1024),
    )(lax.axis_index("yh")[None], terms, shifted(up, axis, 1), shifted(down, axis, -1), *after)


def ring_total(rows):
    for axis in ("x", "z"):
        rows = rows + shifted(rows, axis, 1)
        rows = rows + shifted(rows, axis, 2)
    return rows


def exchanged(blocks, axis):
    return [blocks[0]] + [shifted(blocks[k], axis, d) for k, d in ((1, 1), (2, 2), (3, -1))]


def on_device(stash, attn, w_value, w_out, out_grad, order, check_rows):
    section = lax.axis_index("pipe")
    inputs = stash[0]
    probs = attn[0][:, 0]
    wv = w_value[0]
    wo = w_out[0]
    micro, seq, width = inputs.shape
    inner = wv.shape[1]
    heads = probs.shape[1]
    head_dim = inner // heads
    sections = lax.axis_size("pipe")
    replicas = lax.axis_size("yh") * lax.axis_size("z") * lax.axis_size("x")
    grad_scale = (micro * seq * replicas) ** -0.5
    check_scale = width**-0.5
    highest = lax.Precision.HIGHEST
    n_checks = check_rows.shape[0]
    rows = width // replicas
    z_place, x_place = lax.axis_index("z"), lax.axis_index("x")

    in_hbm = lambda array: pltpu.with_memory_space_constraint(array, pltpu.HBM)
    wo, wv, inputs, probs = in_hbm(wo), in_hbm(wv), in_hbm(inputs), in_hbm(probs)
    check_bf = jnp.pad(check_rows, ((0, 16 - n_checks), (0, 0))).astype(BF16)

    arriving = []
    for m in range(micro):
        own = out_grad[m]
        gathered = [lax.ppermute(own, "pipe", [(s, sections - 1)]) for s in range(sections - 1)]
        arriving.append(tuple(gathered) + (own,))

    token = jnp.zeros((1,), jnp.int32)
    pieces = None
    kept = [None] * micro
    after, y_from, dv_from, early = [], [], [], {}
    for turn in range(sections):
        here = (section == sections - 1 - turn).astype(jnp.int32)
        for m in range(micro):
            meta = jnp.stack([here, order[m], z_place])
            waits = early.get((turn, m), ()) + tuple(after)
            token, sent, kept[m] = section_step(
                meta, token, arriving[m], probs, check_bf, wo, wv, kept[m], waits,
                m if turn == sections - 1 else None, pieces,
            )
            if turn == 0 and m == 0:
                places = jnp.concatenate([x_place[None], order])
                token, context, seen_values, blocks = early_step(
                    places, token, inputs, probs, check_bf, wv
                )
                x_from = exchanged(blocks, "x")
                ctx_from = exchanged([context] * RING, "z")
                early = {
                    (2, 0): (x_from[1], x_from[3]),
                    (2, 1): (x_from[2], ctx_from[1], ctx_from[3]),
                    (3, 1): (ctx_from[2],),
                }
            if turn < sections - 1:
                pair = [(sections - 1 - turn, sections - 2 - turn)]
                arriving[m] = (lax.ppermute(sent[0], "pipe", pair),)
            else:
                pieces = sent
                *y_blocks, dv, _ = kept[m]
                dv_from.append(exchanged([dv] * RING, "x"))
                y_from.append(exchanged(y_blocks, "z"))
                after = dv_from[m][1:]

    checks_v = checks_o = 0.0
    out_sum = value_sum = [None]
    for m in range(micro):
        *_, dv, seen = kept[m]
        checks_v = checks_v + jnp.dot(
            seen_values[m, :n_checks], dv.astype(F32), precision=highest
        )
        checks_o = checks_o + jnp.dot(
            seen[:n_checks], context[m].astype(F32), precision=highest
        )
        last = grad_scale if m == micro - 1 else None
        value_sum = products(True, m, last, z_place, x_from, dv_from[m], value_sum[0])
        waits = dv_from[m][1:] if m else ()
        out_sum = products(False, m, last, x_place, y_from[m], ctx_from, out_sum[0], waits)
    value_next = ring_first("z", *value_sum)
    out_next = ring_first("x", *out_sum)
    came = {}
    came[3] = lax.ppermute(gated(pieces[3], value_next[:1]), "pipe", [(0, 3)])
    value_away, value_kept = ring_last("z", *value_next, value_sum[2], [came[3]])
    came[1] = lax.ppermute(gated(pieces[1], out_next[:1]), "pipe", [(0, 1)])
    out_away, out_kept = ring_last("x", *out_next, out_sum[2], [came[1]])
    came[2] = lax.ppermute(gated(pieces[2], [value_away]), "pipe", [(0, 2)])
    owned = pieces[0]
    for s in (1, 2, 3):
        owned = jnp.where(section == s, came[s], owned)
    owned = owned.transpose(0, 2, 1, 3).reshape(micro, seq, 2 * inner)
    checks = jnp.stack([checks_v, checks_o]) * (grad_scale * check_scale)
    checks = ring_total(gated(checks, [value_away, out_next[0]]))
    grad_v = value_kept + shifted(value_away, "yh", 1).astype(F32)
    grad_o = out_kept + shifted(out_away, "yh", 1).astype(F32)
    check_sum = checks + shifted(checks, "yh", 1)
    return (grad_v[None], grad_o[None], check_sum[None], owned)


def solution(mesh):
    fine = Mesh(mesh.devices.reshape(4, 2, 4, 4), ("pipe",) + REPLICAS)
    return jax.shard_map(
        on_device,
        mesh=fine,
        in_specs=(
            P("pipe", None, REPLICAS, None),
            P("pipe", None, REPLICAS, None, None, None),
            P("pipe", None, None),
            P("pipe", None, None),
            P(None, REPLICAS, "pipe"),
            P(),
            P(),
        ),
        out_specs=(
            P("pipe", REPLICAS, None),
            P("pipe", REPLICAS, None),
            P("pipe", None, None, None),
            P(None, REPLICAS, "pipe"),
        ),
        check_vma=False,
    )
```

```python
import functools

import jax
import jax.numpy as jnp
from jax import lax
from jax.experimental import pallas as pl
from jax.experimental.pallas import tpu as pltpu
from jax.sharding import Mesh
from jax.sharding import PartitionSpec as P

F32 = jnp.float32
BF16 = jnp.bfloat16
NT = (((1,), (1,)), ((), ()))
TN = (((0,), (0,)), ((), ()))
REPLICAS = ("yh", "z", "x")
CHUNKS = 8
RING = 4
VMEM_LIMIT = 34


def shifted(array, axis, distance):
    size = lax.axis_size(axis)
    return lax.ppermute(array, axis, [(i, (i + distance) % size) for i in range(size)])


def total(*terms):
    result = terms[0].astype(F32)
    for term in terms[1:]:
        result = result + term.astype(F32)
    return result


def section_kernel(first, last, heads, head_dim, meta, token, *refs):
    sources = refs[: RING if first else 1]
    refs = refs[len(sources) :]
    probs, rows, w_out, w_value = refs[:4]
    outs = refs[:-11][-(7 + (1 if last is None else RING)) :]
    token_out, y0, y1, y2, y3, dv_out, seen_out = outs[:7]
    dy, dx, wo_in, wv_in, acc, dvals, weights_in, rows_in, seen, in_sems, out_sems = refs[-11:]
    seq, inner = acc.shape
    width = CHUNKS * inner
    token_out[0] = 0

    @pl.when(meta[0] == 1)
    def _():
        loads = []
        for c in range(CHUNKS):
            if first:
                source = sources[c // 2].at[:, pl.ds((c % 2) * inner, inner)]
            else:
                source = sources[0].at[c]
            loads.append(pltpu.make_async_copy(source, dy.at[c], in_sems.at[c]))
        loads.append(pltpu.make_async_copy(rows, rows_in, in_sems.at[CHUNKS]))
        loads.append(pltpu.make_async_copy(probs.at[meta[1]], weights_in, in_sems.at[CHUNKS + 1]))
        upper, lower = [], []
        for c in range(CHUNKS):
            part = pl.ds(c * inner, inner)
            upper.append(
                pltpu.make_async_copy(w_out.at[:, part], wo_in.at[c], in_sems.at[CHUNKS + 2 + c])
            )
            lower.append(
                pltpu.make_async_copy(w_value.at[part], wv_in.at[c], in_sems.at[2 * CHUNKS + 2 + c])
            )
        loads[CHUNKS].start()
        for c in range(CHUNKS):
            loads[c].start()
            upper[c].start()
        loads[CHUNKS + 1].start()
        loads[CHUNKS].wait()
        for c in range(CHUNKS):
            loads[c].wait()
            upper[c].wait()
            lower[c].start()
            columns = slice(c * inner, (c + 1) * inner)
            part = lax.dot_general(dy[c], wo_in[c], NT, preferred_element_type=F32)
            checks = lax.dot_general(rows_in[:, columns], dy[c], NT, preferred_element_type=F32)
            if c == 0:
                acc[...] = part
                seen[...] = checks
            else:
                acc[...] += part
                seen[...] += checks
        stores = [pltpu.make_async_copy(seen, seen_out, out_sems.at[0])]
        for ahead, kept in enumerate((y0, y1, y2, y3)):
            for half in range(2):
                chunk = half * RING + lax.rem(meta[2] + ahead, RING)
                stores.append(
                    pltpu.make_async_copy(dy.at[chunk], kept.at[half], out_sems.at[len(stores)])
                )
        for store in stores:
            store.start()
        loads[CHUNKS + 1].wait()
        dctx = acc[...].astype(BF16)
        query = lax.broadcasted_iota(jnp.int32, (seq, seq), 0)
        keys = lax.broadcasted_iota(jnp.int32, (seq, seq), 1)
        for head in range(heads):
            weights = jnp.where(query >= keys, weights_in[head].astype(F32), 0.0).astype(BF16)
            columns = slice(head * head_dim, (head + 1) * head_dim)
            part = lax.dot_general(weights, dctx[:, columns], TN, preferred_element_type=F32)
            dvals[:, columns] = part.astype(BF16)
        stores.append(pltpu.make_async_copy(dvals, dv_out, out_sems.at[len(stores)]))
        stores[-1].start()
        for c in range(CHUNKS):
            lower[c].wait()
            part = lax.dot_general(dvals[...], wv_in[c], NT, preferred_element_type=F32)
            dx[c] = (dy[c].astype(F32) + part).astype(BF16)
            stores.append(
                pltpu.make_async_copy(
                    dx.at[c],
                    outs[7].at[c] if last is None else outs[7 + c // 2].at[last, c % 2],
                    out_sems.at[len(stores)],
                )
            )
            stores[-1].start()
        for store in stores:
            store.wait()


def section_step(meta, token, sources, probs, rows, w_out, w_value, kept, after=(), last=None, pieces=None):
    first = len(sources) > 1
    micro, heads, seq, _ = probs.shape
    inner, width = w_out.shape
    in_memory = pl.BlockSpec(memory_space=pltpu.HBM)
    in_smem = pl.BlockSpec(memory_space=pltpu.SMEM)
    operands = (meta, token) + tuple(sources) + (probs, rows, w_out, w_value)
    in_specs = [in_smem, in_smem] + [in_memory] * (len(sources) + 4)
    aliases = {}
    if kept is not None:
        aliases = {len(operands) + i: 1 + i for i in range(len(kept))}
        in_specs += [in_memory] * len(kept)
        operands += tuple(kept)
    if pieces is not None:
        aliases.update({len(operands) + i: 7 + i for i in range(RING)})
        in_specs += [in_memory] * RING
        operands += tuple(pieces)
    in_specs += [pl.BlockSpec(memory_space=pl.ANY)] * len(after)
    operands += tuple(after)
    copies = 1 + 2 * RING + 1 + CHUNKS
    token, *results = pl.pallas_call(
        functools.partial(section_kernel, first, last, heads, inner // heads),
        in_specs=in_specs,
        out_specs=[in_smem] + [in_memory] * (6 + (1 if last is None else RING)),
        out_shape=[
            jax.ShapeDtypeStruct((1,), jnp.int32),
        ]
        + [pltpu.HBM((2, seq, inner), BF16)] * RING
        + [
            pltpu.HBM((seq, inner), BF16),
            pltpu.HBM((rows.shape[0], seq), F32),
        ]
        + (
            [pltpu.HBM((CHUNKS, seq, inner), BF16)]
            if last is None
            else [pltpu.HBM((micro, 2, seq, inner), BF16)] * RING
        ),
        scratch_shapes=[
            pltpu.VMEM((CHUNKS, seq, inner), BF16),
            pltpu.VMEM((CHUNKS, seq, inner), BF16),
            pltpu.VMEM((CHUNKS, inner, inner), BF16),
            pltpu.VMEM((CHUNKS, inner, inner), BF16),
            pltpu.VMEM((seq, inner), F32),
            pltpu.VMEM((seq, inner), BF16),
            pltpu.VMEM((heads, seq, seq), BF16),
            pltpu.VMEM(rows.shape, BF16),
            pltpu.VMEM((rows.shape[0], seq), F32),
            pltpu.SemaphoreType.DMA((3 * CHUNKS + 2,)),
            pltpu.SemaphoreType.DMA((copies,)),
        ],
        input_output_aliases=aliases,
        cost_estimate=pl.CostEstimate(
            flops=4 * seq * width * inner, bytes_accessed=4 * width * inner, transcendentals=0
        ),
        compiler_params=pltpu.CompilerParams(vmem_limit_bytes=VMEM_LIMIT * 1024 * 1024),
    )(*operands)
    return token, results[6:], results[:6]


def gate_kernel(*refs):
    pass


def gated(array, after):
    in_memory = pl.BlockSpec(memory_space=pltpu.HBM)
    return pl.pallas_call(
        gate_kernel,
        in_specs=[in_memory] + [pl.BlockSpec(memory_space=pl.ANY)] * len(after),
        out_specs=in_memory,
        out_shape=pltpu.HBM(array.shape, array.dtype),
        input_output_aliases={0: 0},
        compiler_params=pltpu.CompilerParams(vmem_limit_bytes=1024 * 1024),
    )(array, *after)


def early_kernel(heads, head_dim, meta, token, inputs, probs, rows, w_value, *refs):
    token_out, ctx_out, seen_out, x0, x1, x2, x3 = refs[:7]
    x, cut, wv_in, weights_in, rows_in, ctx, seen, in_sems, out_sems = refs[7:]
    micro, seq, inner = ctx.shape
    width = x.shape[2]
    share = cut.shape[3] // CHUNKS
    token_out[0] = token[0]
    loads = []
    for m in range(micro):
        loads.append(pltpu.make_async_copy(inputs.at[meta[1 + m]], x.at[m], in_sems.at[2 * m]))
        loads.append(
            pltpu.make_async_copy(probs.at[meta[1 + m]], weights_in.at[m], in_sems.at[2 * m + 1])
        )
    loads.append(pltpu.make_async_copy(rows, rows_in, in_sems.at[2 * micro]))
    for c in range(CHUNKS):
        source = w_value.at[pl.ds(c * inner, inner)]
        loads.append(pltpu.make_async_copy(source, wv_in.at[c], in_sems.at[2 * micro + 1 + c]))
    for load in loads:
        load.start()
    loads[2 * micro].wait()
    stores = []
    query = lax.broadcasted_iota(jnp.int32, (seq, seq), 0)
    keys = lax.broadcasted_iota(jnp.int32, (seq, seq), 1)
    for m in range(micro):
        loads[2 * m].wait()
        for part in range(CHUNKS):
            for place in range(RING):
                start = (part * RING + place) * share
                cut[m, place, :, part * share : (part + 1) * share] = x[m, :, start : start + share]
        for ahead, out in enumerate((x0, x1, x2, x3)):
            place = lax.rem(meta[0] + ahead, RING)
            stores.append(
                pltpu.make_async_copy(cut.at[m, place], out.at[m], out_sems.at[len(stores)])
            )
            stores[-1].start()
    for m in range(micro):
        loads[2 * m + 1].wait()
        acc = None
        for c in range(CHUNKS):
            columns = slice(c * inner, (c + 1) * inner)
            block = x[m, :, columns]
            if m == 0:
                loads[2 * micro + 1 + c].wait()
            part = jnp.dot(block, wv_in[c], preferred_element_type=F32)
            checks = lax.dot_general(rows_in[:, columns], block, NT, preferred_element_type=F32)
            acc, checked = (part, checks) if c == 0 else (acc + part, checked + checks)
        seen[m] = checked
        values = acc.astype(BF16)
        for head in range(heads):
            weights = jnp.where(query >= keys, weights_in[m, head].astype(F32), 0.0).astype(BF16)
            columns = slice(head * head_dim, (head + 1) * head_dim)
            part = jnp.dot(weights, values[:, columns], preferred_element_type=F32)
            ctx[m, :, columns] = part.astype(BF16)
    stores.append(pltpu.make_async_copy(ctx, ctx_out, out_sems.at[len(stores)]))
    stores.append(pltpu.make_async_copy(seen, seen_out, out_sems.at[len(stores)]))
    for store in stores[-2:]:
        store.start()
    for store in stores:
        store.wait()


def early_step(meta, token, inputs, probs, rows, w_value):
    micro, seq, width = inputs.shape
    inner = w_value.shape[1]
    heads = probs.shape[1]
    in_memory = pl.BlockSpec(memory_space=pltpu.HBM)
    in_smem = pl.BlockSpec(memory_space=pltpu.SMEM)
    token, ctx, seen, *blocks = pl.pallas_call(
        functools.partial(early_kernel, heads, inner // heads),
        in_specs=[in_smem, in_smem] + [in_memory] * 4,
        out_specs=[in_smem] + [in_memory] * 6,
        out_shape=[
            jax.ShapeDtypeStruct((1,), jnp.int32),
            jax.ShapeDtypeStruct((micro, seq, inner), BF16),
            jax.ShapeDtypeStruct((micro, rows.shape[0], seq), F32),
        ]
        + [pltpu.HBM((micro, seq, width // RING), BF16)] * RING,
        scratch_shapes=[
            pltpu.VMEM((micro, seq, width), BF16),
            pltpu.VMEM((micro, RING, seq, width // RING), BF16),
            pltpu.VMEM((CHUNKS, inner, inner), BF16),
            pltpu.VMEM((micro, heads, seq, seq), BF16),
            pltpu.VMEM(rows.shape, BF16),
            pltpu.VMEM((micro, seq, inner), BF16),
            pltpu.VMEM((micro, rows.shape[0], seq), F32),
            pltpu.SemaphoreType.DMA((2 * micro + 1 + CHUNKS,)),
            pltpu.SemaphoreType.DMA((RING * micro + 2,)),
        ],
        cost_estimate=pl.CostEstimate(
            flops=8 * micro * seq * width * inner,
            bytes_accessed=4 * width * inner,
            transcendentals=0,
        ),
        compiler_params=pltpu.CompilerParams(vmem_limit_bytes=VMEM_LIMIT * 1024 * 1024),
    )(meta, token, inputs, probs, rows, w_value)
    return token, ctx, seen, blocks


def product_kernel(of_value, m, last, meta, *refs):
    left, right, refs = refs[:RING], refs[RING : 2 * RING], refs[2 * RING :]
    before = refs[0] if m else None
    refs = refs[-1:] if last is None else refs[-4:]
    inner = right[0].shape[-1]
    rows = inner // RING
    for half in range(2):
        total = before[half] if m else None
        for k in range(RING):
            if of_value:
                part = left[k][m, :, half * inner : (half + 1) * inner], right[k][...]
            else:
                part = left[k][half], right[k][m]
            part = lax.dot_general(*part, TN, preferred_element_type=F32)
            total = part if total is None else total + part
        if last is None:
            refs[0][half] = total
        else:
            *away2, terms, acc = refs
            acc[...] = total * last
            for ahead in range(RING):
                start = lax.rem(meta[0] + ahead, RING) * rows
                term = acc[pl.ds(pl.multiple_of(start, rows), rows), :].astype(BF16)
                terms[half, ahead] = term
                if ahead == 2:
                    away2[half][...] = term


def products(of_value, m, last, place, left, right, before, after=()):
    inner = right[0].shape[-1]
    rows = inner // RING
    in_vmem = pl.BlockSpec(memory_space=pltpu.VMEM)
    operands = list(left) + list(right) + ([before] if m else [])
    if last is None:
        shapes = [jax.ShapeDtypeStruct((2, inner, inner), F32)]
        scratch = []
    else:
        shapes = [jax.ShapeDtypeStruct((rows, inner), BF16)] * 2
        shapes += [jax.ShapeDtypeStruct((2, RING, rows, inner), BF16)]
        scratch = [pltpu.VMEM((inner, inner), F32)]
    return pl.pallas_call(
        functools.partial(product_kernel, of_value, m, last),
        in_specs=[pl.BlockSpec(memory_space=pltpu.SMEM)]
        + [in_vmem] * len(operands)
        + [pl.BlockSpec(memory_space=pl.ANY)] * len(after),
        out_specs=[in_vmem] * len(shapes),
        out_shape=shapes,
        scratch_shapes=scratch,
        cost_estimate=pl.CostEstimate(
            flops=32 * inner * inner * 160, bytes_accessed=16 * inner * inner, transcendentals=0
        ),
        compiler_params=pltpu.CompilerParams(vmem_limit_bytes=24 * 1024 * 1024),
    )(place[None], *operands, *after)


def second_kernel(terms, up2, down2, up, down):
    up[0] = terms[1, 1]
    up[1] = total(terms[0, 1], up2[...]).astype(BF16)
    down[0] = terms[0, 3]
    down[1] = total(terms[1, 3], down2[...]).astype(BF16)


def third_kernel(meta, terms, up, down, *refs):
    away, kept = refs[-2:]
    low = total(terms[0, 0], down[0], up[1])
    high = total(terms[1, 0], up[0], down[1])

    @pl.when(meta[0] == 0)
    def _():
        kept[...] = low
        away[...] = high.astype(BF16)

    @pl.when(meta[0] == 1)
    def _():
        kept[...] = high
        away[...] = low.astype(BF16)


def ring_first(axis, up2, down2, terms):
    _, _, rows, inner = terms.shape
    in_vmem = pl.BlockSpec(memory_space=pltpu.VMEM)
    return pl.pallas_call(
        second_kernel,
        in_specs=[in_vmem] * 3,
        out_specs=[in_vmem] * 2,
        out_shape=[jax.ShapeDtypeStruct((2, rows, inner), BF16)] * 2,
        compiler_params=pltpu.CompilerParams(vmem_limit_bytes=8 * 1024 * 1024),
    )(terms, shifted(up2, axis, 1), shifted(down2, axis, -1))


def ring_last(axis, up, down, terms, after):
    _, _, rows, inner = terms.shape
    in_vmem = pl.BlockSpec(memory_space=pltpu.VMEM)
    in_smem = pl.BlockSpec(memory_space=pltpu.SMEM)
    return pl.pallas_call(
        third_kernel,
        in_specs=[in_smem] + [in_vmem] * 3 + [pl.BlockSpec(memory_space=pl.ANY)] * len(after),
        out_specs=[in_vmem] * 2,
        out_shape=[
            jax.ShapeDtypeStruct((rows, inner), BF16),
            jax.ShapeDtypeStruct((rows, inner), F32),
        ],
        compiler_params=pltpu.CompilerParams(vmem_limit_bytes=8 * 1024 * 1024),
    )(lax.axis_index("yh")[None], terms, shifted(up, axis, 1), shifted(down, axis, -1), *after)


def ring_total(axis, rows):
    rows = rows + shifted(rows, axis, 1)
    return rows + shifted(rows, axis, 2)


def exchanged(blocks, axis):
    return [blocks[0]] + [shifted(blocks[k], axis, d) for k, d in ((1, 1), (2, 2), (3, -1))]


def on_device(stash, attn, w_value, w_out, out_grad, order, check_rows):
    section = lax.axis_index("pipe")
    inputs = stash[0]
    probs = attn[0][:, 0]
    wv = w_value[0]
    wo = w_out[0]
    micro, seq, width = inputs.shape
    inner = wv.shape[1]
    heads = probs.shape[1]
    head_dim = inner // heads
    sections = lax.axis_size("pipe")
    replicas = lax.axis_size("yh") * lax.axis_size("z") * lax.axis_size("x")
    grad_scale = (micro * seq * replicas) ** -0.5
    check_scale = width**-0.5
    highest = lax.Precision.HIGHEST
    n_checks = check_rows.shape[0]
    rows = width // replicas
    z_place, x_place = lax.axis_index("z"), lax.axis_index("x")

    in_hbm = lambda array: pltpu.with_memory_space_constraint(array, pltpu.HBM)
    wo, wv, inputs, probs = in_hbm(wo), in_hbm(wv), in_hbm(inputs), in_hbm(probs)
    check_bf = jnp.pad(check_rows, ((0, 16 - n_checks), (0, 0))).astype(BF16)

    arriving = []
    for m in range(micro):
        own = out_grad[m]
        gathered = [lax.ppermute(own, "pipe", [(s, sections - 1)]) for s in range(sections - 1)]
        arriving.append(tuple(gathered) + (own,))

    token = jnp.zeros((1,), jnp.int32)
    pieces = None
    kept = [None] * micro
    after, y_from, dv_from, early = [], [], [], {}
    for turn in range(sections):
        here = (section == sections - 1 - turn).astype(jnp.int32)
        for m in range(micro):
            meta = jnp.stack([here, order[m], z_place])
            waits = early.get((turn, m), ()) + tuple(after)
            token, sent, kept[m] = section_step(
                meta, token, arriving[m], probs, check_bf, wo, wv, kept[m], waits,
                m if turn == sections - 1 else None, pieces,
            )
            if turn == 0 and m == 0:
                places = jnp.concatenate([x_place[None], order])
                token, context, seen_values, blocks = early_step(
                    places, token, inputs, probs, check_bf, wv
                )
                x_from = exchanged(blocks, "x")
                ctx_from = exchanged([context] * RING, "z")
                early = {
                    (2, 0): (x_from[1], x_from[3]),
                    (2, 1): (x_from[2], ctx_from[1], ctx_from[3]),
                    (3, 1): (ctx_from[2],),
                }
            if turn < sections - 1:
                pair = [(sections - 1 - turn, sections - 2 - turn)]
                arriving[m] = (lax.ppermute(sent[0], "pipe", pair),)
            else:
                pieces = sent
                *y_blocks, dv, _ = kept[m]
                dv_from.append(exchanged([dv] * RING, "x"))
                y_from.append(exchanged(y_blocks, "z"))
                after = dv_from[m][1:]

    checks_v = checks_o = 0.0
    out_sum = value_sum = [None]
    for m in range(micro):
        *_, dv, seen = kept[m]
        checks_v = checks_v + jnp.dot(
            seen_values[m, :n_checks], dv.astype(F32), precision=highest
        )
        checks_o = checks_o + jnp.dot(
            seen[:n_checks], context[m].astype(F32), precision=highest
        )
        last = grad_scale if m == micro - 1 else None
        value_sum = products(True, m, last, z_place, x_from, dv_from[m], value_sum[0])
        waits = dv_from[m][1:] if m else ()
        out_sum = products(False, m, last, x_place, y_from[m], ctx_from, out_sum[0], waits)
    value_next = ring_first("z", *value_sum)
    out_next = ring_first("x", *out_sum)
    came = {}
    came[3] = lax.ppermute(gated(pieces[3], value_next[:1]), "pipe", [(0, 3)])
    value_away, value_kept = ring_last("z", *value_next, value_sum[2], [came[3]])
    came[1] = lax.ppermute(gated(pieces[1], out_next[:1]), "pipe", [(0, 1)])
    out_away, out_kept = ring_last("x", *out_next, out_sum[2], [came[1]])
    checks = jnp.stack([checks_v, checks_o]) * (grad_scale * check_scale)
    checks = ring_total("x", gated(checks, [value_away]))
    came[2] = lax.ppermute(gated(pieces[2], [checks]), "pipe", [(0, 2)])
    checks = ring_total("z", checks)
    owned = pieces[0]
    for s in (1, 2, 3):
        owned = jnp.where(section == s, came[s], owned)
    owned = owned.transpose(0, 2, 1, 3).reshape(micro, seq, 2 * inner)
    grad_v = value_kept + shifted(value_away, "yh", 1).astype(F32)
    grad_o = out_kept + shifted(out_away, "yh", 1).astype(F32)
    check_sum = checks + shifted(checks, "yh", 1)
    return (grad_v[None], grad_o[None], check_sum[None], owned)


def solution(mesh):
    fine = Mesh(mesh.devices.reshape(4, 2, 4, 4), ("pipe",) + REPLICAS)
    return jax.shard_map(
        on_device,
        mesh=fine,
        in_specs=(
            P("pipe", None, REPLICAS, None),
            P("pipe", None, REPLICAS, None, None, None),
            P("pipe", None, None),
            P("pipe", None, None),
            P(None, REPLICAS, "pipe"),
            P(),
            P(),
        ),
        out_specs=(
            P("pipe", REPLICAS, None),
            P("pipe", REPLICAS, None),
            P("pipe", None, None, None),
            P(None, REPLICAS, "pipe"),
        ),
        check_vma=False,
    )
```
